32 devices in a mesh: res: 16 (over z, y, x), half: 2 (over core).
Axes of the slice: x: 2, y: 2, z: 4, core: 2. Of those that a mesh axis runs over, the one named last changes fastest.
Arguments:
- nodes: bfloat16 [1536, 512], P('res'), may hold values from -6 to 6
- edges: bfloat16 [1536, 60, 192], P('res'), may hold values from -6 to 6
- neighbours: int32 [1536, 60], P('res'), may hold values from 0 to 1535, as said below
- counts: int32 [1536], P('res'), may hold values from 30 to 60, as said below
- message_first: bfloat16 [1216, 512], replicated, may hold values from -0.15625 to 0.15625
- message_first_bias: bfloat16 [512], replicated, may hold values from -3 to 3
- message_second: bfloat16 [512, 512], replicated, may hold values from -0.25 to 0.25
- message_second_bias: bfloat16 [512], replicated, may hold values from -3 to 3
- message_third: bfloat16 [512, 512], replicated, may hold values from -0.75 to 0.75
- message_third_bias: bfloat16 [512], replicated, may hold values from -2 to 2
- node_norm_gain: bfloat16 [512], replicated, may hold values from 0.5 to 1.5
- node_norm_shift: bfloat16 [512], replicated, may hold values from -2 to 2
- expand_weight: bfloat16 [512, 2048], replicated, may hold values from -0.25 to 0.25
- expand_bias: bfloat16 [2048], replicated, may hold values from -3 to 3
- reduce_weight: bfloat16 [2048, 512], replicated, may hold values from -0.25 to 0.25
- reduce_bias: bfloat16 [512], replicated, may hold values from -2 to 2
- output_norm_gain: bfloat16 [512], replicated, may hold values from 0.5 to 1.5
- output_norm_shift: bfloat16 [512], replicated, may hold values from -2 to 2
- edge_first: bfloat16 [1216, 192], replicated, may hold values from -0.15625 to 0.15625
- edge_first_bias: bfloat16 [192], replicated, may hold values from -3 to 3
- edge_second: bfloat16 [192, 192], replicated, may hold values from -0.4375 to 0.4375
- edge_second_bias: bfloat16 [192], replicated, may hold values from -3 to 3
- edge_third: bfloat16 [192, 192], replicated, may hold values from -0.875 to 0.875
- edge_third_bias: bfloat16 [192], replicated, may hold values from -2 to 2
- edge_norm_gain: bfloat16 [192], replicated, may hold values from 0.5 to 1.5
- edge_norm_shift: bfloat16 [192], replicated, may hold values from -2 to 2
- cot_nodes: bfloat16 [1536, 512], P('res'), may hold values from -6 to 6
- cot_edges: bfloat16 [1536, 60, 192], P('res'), may hold values from -6 to 6
Outputs:
- nodes_out: bfloat16 [1536, 512], P('res', 'half')
- edges_out: bfloat16 [1536, 60, 192], P('res', 'half')
- fed_grad: float32 [1536, 512], P('res', 'half')
- edges_grad: float32 [1536, 60, 192], P('res', 'half')
- message_first_grad: float32 [1216, 512], P('half')
- message_first_bias_grad: float32 [512], P('half')
- message_second_grad: float32 [512, 512], P('half')
- message_second_bias_grad: float32 [512], P('half')
- message_third_grad: float32 [512, 512], P('half')
- message_third_bias_grad: float32 [512], P('half')
- node_norm_gain_grad: float32 [512], P('half')
- node_norm_shift_grad: float32 [512], P('half')
- expand_weight_grad: float32 [512, 2048], P('half')
- expand_bias_grad: float32 [2048], P('half')
- reduce_weight_grad: float32 [2048, 512], P('half')
- reduce_bias_grad: float32 [512], P('half')
- output_norm_gain_grad: float32 [512], P('half')
- output_norm_shift_grad: float32 [512], P('half')
- edge_first_grad: float32 [1216, 192], P('half')
- edge_first_bias_grad: float32 [192], P('half')
- edge_second_grad: float32 [192, 192], P('half')
- edge_second_bias_grad: float32 [192], P('half')
- edge_third_grad: float32 [192, 192], P('half')
- edge_third_bias_grad: float32 [192], P('half')
- edge_norm_gain_grad: float32 [192], P('half')
- edge_norm_shift_grad: float32 [192], P('half')
The draws below stay inside these ranges and needn't reach their ends.
Inputs may be any that keep to these rules, and one draw needn't show every extreme that they name: `neighbours`: residues form contiguous proteins of 256 to 1024 residues (the last one may be shorter); the first begins at residue 0 and every other begins at a residue whose index is 96 // 2 modulo 96. Every slot names a residue of the same protein at most 64 positions away from residue i; only the first counts[i] slots of residue i are used. Residue i uses slots 0 to counts[i] - 1.
All inputs are finite; a program needn't handle non-finite values.
Results may differ from the reference program's by a relative error of at most 0.025.
Values may be sent and summed in bfloat16 or wider, within the bound.
A program may use at most 320 MiB of HBM per device.

```python
import jax
import jax.numpy as jnp
from jax import lax

D = 512
E = 192
H = 512
F = 2048
KMAX = 60
KMIN = 30
REACH = 64
PMIN = 256
PMAX = 1024
R_DEV = 96
RES = 1536
CAT = 1216


def draw_neighbours(key, part):
    key = jax.random.fold_in(key, 11)
    key_len, key_first, key_near = jax.random.split(key, 3)
    half_unit = R_DEV // 2
    low_mult = (PMIN + R_DEV - 1) // R_DEV
    high_mult = PMAX // R_DEV
    first_mult = (PMIN + half_unit + R_DEV - 1) // R_DEV
    protein_lengths = (jax.random.randint(key_len, (RES // PMIN + 2,), low_mult, high_mult + 1) * R_DEV).astype(jnp.int32)
    first_length = (jax.random.randint(key_first, (), first_mult, high_mult + 1) * R_DEV - half_unit).astype(jnp.int32)
    protein_lengths = protein_lengths.at[0].set(first_length)
    protein_ends = jnp.cumsum(protein_lengths).astype(jnp.int32)
    protein_starts = protein_ends - protein_lengths
    positions = jnp.arange(RES, dtype=jnp.int32)
    owner = jnp.sum((protein_ends[None, :] <= positions[:, None]).astype(jnp.int32), 1).astype(jnp.int32)
    lowest = protein_starts[owner]
    highest = jnp.minimum(protein_ends[owner], RES) - 1
    offsets = jax.random.randint(key_near, (RES, KMAX), -REACH, REACH + 1).astype(jnp.int32)
    chosen = jnp.clip(positions[:, None] + offsets, lowest[:, None], highest[:, None])
    slot_index = lax.broadcasted_iota(jnp.int32, (RES, KMAX), 1)
    place = positions % R_DEV
    lower_edge = (place == 0) & (positions > 0)
    upper_edge = (place == R_DEV - 1) & (positions < RES - 1)
    chosen = jnp.where(lower_edge[:, None] & (slot_index == 0), positions[:, None] - 1, chosen)
    chosen = jnp.where(upper_edge[:, None] & (slot_index == 1), positions[:, None] + 1, chosen)
    chosen = chosen.at[0, 0].set(0).at[RES - 1, 0].set(RES - 1)
    return chosen.astype(jnp.int32)


def draw_counts(key, part):
    key = jax.random.fold_in(key, 23)
    drawn = jax.random.randint(key, (RES,), KMIN, KMAX + 1)
    drawn = drawn.at[0].set(KMAX).at[RES - 1].set(KMIN)
    return drawn.astype(jnp.int32)


def steps_of(stream_key, extent, cuts, least, top_value):
    def one(axis_at, blocks):
        heights = jax.random.uniform(jax.random.fold_in(jax.random.fold_in(stream_key, 6), axis_at), (blocks,), jnp.float32, least / len(cuts), top_value / len(cuts))
        return jnp.repeat(jnp.exp(heights), extent[axis_at] // blocks).reshape((-1,) + (1,) * (len(extent) - axis_at - 1))

    loudness = one(*cuts[0])
    for cut in cuts[1:]:
        loudness = loudness * one(*cut)
    return loudness


def scatter_about(own_key, dims, spread, limit, cuts=(), kind=jnp.bfloat16):
    loudness = steps_of(own_key, dims, cuts, -0.22, 0.18) if cuts else 1.0
    values = jax.random.normal(own_key, dims, jnp.float32) * spread * loudness
    return jnp.minimum(jnp.maximum(values, -limit), limit).astype(kind)


def setup_inputs(seed: int = 0) -> dict:
    key_list = jax.random.split(jax.random.key(seed), 29)
    return {
        "nodes": scatter_about(key_list[0], (RES, D), 1.0, 6.0, ((0, 16),)),
        "edges": scatter_about(key_list[1], (RES, KMAX, E), 1.0, 6.0, ((0, 16),)),
        "neighbours": draw_neighbours(jax.random.fold_in(key_list[28], 71), 0),
        "counts": draw_counts(jax.random.fold_in(key_list[28], 71), 0),
        "message_first": scatter_about(key_list[4], (CAT, H), CAT ** -0.5, 0.15625),
        "message_first_bias": scatter_about(key_list[5], (H,), 0.5, 3.0),
        "message_second": scatter_about(key_list[6], (H, H), H ** -0.5, 0.25),
        "message_second_bias": scatter_about(key_list[7], (H,), 0.5, 3.0),
        "message_third": scatter_about(key_list[8], (H, D), (H // 8) ** -0.5, 0.75),
        "message_third_bias": scatter_about(key_list[9], (D,), 0.3, 2.0),
        "node_norm_gain": jnp.clip(1.0 + 0.1 * jax.random.normal(key_list[10], (D,), jnp.float32), 0.5, 1.5).astype(jnp.bfloat16),
        "node_norm_shift": scatter_about(key_list[11], (D,), 0.3, 2.0),
        "expand_weight": scatter_about(key_list[12], (D, F), D ** -0.5, 0.25),
        "expand_bias": scatter_about(key_list[13], (F,), 0.5, 3.0),
        "reduce_weight": scatter_about(key_list[14], (F, D), (F // 4) ** -0.5, 0.25),
        "reduce_bias": scatter_about(key_list[15], (D,), 0.3, 2.0),
        "output_norm_gain": jnp.clip(1.0 + 0.1 * jax.random.normal(key_list[16], (D,), jnp.float32), 0.5, 1.5).astype(jnp.bfloat16),
        "output_norm_shift": scatter_about(key_list[17], (D,), 0.3, 2.0),
        "edge_first": scatter_about(key_list[18], (CAT, E), CAT ** -0.5, 0.15625),
        "edge_first_bias": scatter_about(key_list[19], (E,), 0.5, 3.0),
        "edge_second": scatter_about(key_list[20], (E, E), E ** -0.5, 0.4375),
        "edge_second_bias": scatter_about(key_list[21], (E,), 0.5, 3.0),
        "edge_third": scatter_about(key_list[22], (E, E), (E // 4) ** -0.5, 0.875),
        "edge_third_bias": scatter_about(key_list[23], (E,), 0.3, 2.0),
        "edge_norm_gain": jnp.clip(1.0 + 0.1 * jax.random.normal(key_list[24], (E,), jnp.float32), 0.5, 1.5).astype(jnp.bfloat16),
        "edge_norm_shift": scatter_about(key_list[25], (E,), 0.3, 2.0),
        "cot_nodes": scatter_about(key_list[26], (RES, D), 1.0, 6.0, ((0, 16),)),
        "cot_edges": scatter_about(key_list[27], (RES, KMAX, E), 1.0, 6.0, ((0, 16),)),
    }


EPSILON = 1e-05
PRECISE = lax.Precision.HIGHEST

@jax.custom_vjp
def low(v):
    return lax.optimization_barrier(v.astype(jnp.bfloat16)).astype(jnp.float32)

@jax.custom_vjp
def low_back(v):
    return v

def low_keep(v):
    return (low(v), None)

def low_pass(kept, grad):
    return (grad,)

def back_keep(v):
    return (v, None)

def back_low(kept, grad):
    return (low(grad),)
low.defvjp(low_keep, low_pass)
low_back.defvjp(back_keep, back_low)

def activation(values):
    return jax.nn.gelu(values, approximate=True)

def layer_norm(values, norm_gain, norm_shift):
    centered = values - lax.optimization_barrier(jnp.mean(values, -1, keepdims=True))
    variance = lax.optimization_barrier(jnp.mean(centered * centered, -1, keepdims=True))
    return centered * lax.rsqrt(variance + EPSILON) * norm_gain + norm_shift

def block_rows():
    rows_each = R_DEV
    while rows_each * 2 <= 512 and RES % (rows_each * 2) == 0:
        rows_each = rows_each * 2
    return rows_each

def three_layers(joined, weights):
    w_first, b_first, w_second, b_second, w_third, b_third = weights
    pre_one = low_back(jnp.einsum('rkc,ch->rkh', joined, w_first, precision=PRECISE) + b_first)
    act_one = low(activation(pre_one))
    pre_two = low_back(jnp.einsum('rkc,ch->rkh', act_one, w_second, precision=PRECISE) + b_second)
    act_two = low(activation(pre_two))
    return low_back(jnp.einsum('rkc,ch->rkh', act_two, w_third, precision=PRECISE) + b_third)

def joined_inputs(low_nodes, edges, neighbours, start, rows_each):
    own_rows = lax.dynamic_slice_in_dim(low_nodes, start, rows_each, 0)
    picks = lax.dynamic_slice_in_dim(neighbours, start, rows_each, 0)
    edge_block = lax.dynamic_slice_in_dim(edges, start, rows_each, 0)
    far_rows = low_nodes[picks]
    near_rows = jnp.broadcast_to(own_rows[:, None, :], far_rows.shape)
    return (jnp.concatenate([near_rows, far_rows, edge_block], -1), edge_block)

def node_update(nodes_in, edges, neighbours, live_mask, counts_f, weights):
    rows_each = block_rows()
    low_nodes = low(nodes_in)

    def one_block(index):
        start = (index * rows_each).astype(jnp.int32)
        joined, edge_block = joined_inputs(low_nodes, edges, neighbours, start, rows_each)
        message = three_layers(joined, weights[:6])
        mask_block = lax.dynamic_slice_in_dim(live_mask, start, rows_each, 0)
        count_block = lax.dynamic_slice_in_dim(counts_f, start, rows_each, 0)
        return lax.optimization_barrier(jnp.sum(message * mask_block[:, :, None], 1)) / count_block[:, None]
    pooled = lax.map(jax.checkpoint(one_block), jnp.arange(RES // rows_each, dtype=jnp.int32)).reshape(RES, D)
    summed = nodes_in + pooled
    normed = layer_norm(summed, weights[6], weights[7])
    pre_expand = low_back(jnp.dot(low(normed), weights[8], precision=PRECISE) + weights[9])
    act_expand = low(activation(pre_expand))
    reduced = low_back(jnp.dot(act_expand, weights[10], precision=PRECISE) + weights[11])
    return layer_norm(normed + reduced, weights[12], weights[13])

def edge_update(nodes_out, edges, neighbours, live_mask, weights):
    rows_each = block_rows()
    low_nodes = low(nodes_out)

    def one_block(index):
        start = (index * rows_each).astype(jnp.int32)
        joined, edge_block = joined_inputs(low_nodes, edges, neighbours, start, rows_each)
        update = three_layers(joined, weights[:6])
        mask_block = lax.dynamic_slice_in_dim(live_mask, start, rows_each, 0)
        return layer_norm(edge_block + update, weights[6], weights[7]) * mask_block[:, :, None]
    return lax.map(jax.checkpoint(one_block), jnp.arange(RES // rows_each, dtype=jnp.int32)).reshape(RES, KMAX, E)

def reference(nodes, edges, neighbours, counts, message_first, message_first_bias, message_second, message_second_bias, message_third, message_third_bias, node_norm_gain, node_norm_shift, expand_weight, expand_bias, reduce_weight, reduce_bias, output_norm_gain, output_norm_shift, edge_first, edge_first_bias, edge_second, edge_second_bias, edge_third, edge_third_bias, edge_norm_gain, edge_norm_shift, cot_nodes, cot_edges):
    node_params = tuple((member.astype(jnp.float32) for member in (message_first, message_first_bias, message_second, message_second_bias, message_third, message_third_bias, node_norm_gain, node_norm_shift, expand_weight, expand_bias, reduce_weight, reduce_bias, output_norm_gain, output_norm_shift)))
    edge_params = tuple((member.astype(jnp.float32) for member in (edge_first, edge_first_bias, edge_second, edge_second_bias, edge_third, edge_third_bias, edge_norm_gain, edge_norm_shift)))
    live_mask = (lax.broadcasted_iota(jnp.int32, (RES, KMAX), 1) < counts[:, None]).astype(jnp.float32)
    counts_f = counts.astype(jnp.float32)
    edges_f = edges.astype(jnp.float32)
    first = node_update(nodes.astype(jnp.float32), edges_f, neighbours, live_mask, counts_f, node_params)
    fed = low(first)

    def forward(fed_in, edges_in, node_p, edge_p):
        nodes_new = node_update(fed_in, edges_in, neighbours, live_mask, counts_f, node_p)
        edges_new = edge_update(nodes_new, edges_in, neighbours, live_mask, edge_p)
        return (nodes_new, edges_new)
    outputs, backward = jax.vjp(forward, fed, edges_f, node_params, edge_params)
    fed_grad, edges_grad, node_g, edge_g = backward((cot_nodes.astype(jnp.float32), cot_edges.astype(jnp.float32)))
    return (outputs[0].astype(jnp.bfloat16), outputs[1].astype(jnp.bfloat16), fed_grad, edges_grad, node_g[0], node_g[1], node_g[2], node_g[3], node_g[4], node_g[5], node_g[6], node_g[7], node_g[8], node_g[9], node_g[10], node_g[11], node_g[12], node_g[13], edge_g[0], edge_g[1], edge_g[2], edge_g[3], edge_g[4], edge_g[5], edge_g[6], edge_g[7])
```

```python
import functools

import jax
import jax.numpy as jnp
from jax import lax
from jax.experimental import pallas as pl
from jax.experimental.pallas import tpu as pltpu
from jax.sharding import PartitionSpec as P

EPSILON = 1e-05
REACH = 64
CORES = 2
NEAR = 0.7978845608
CUBE = 0.044715
BLOCK = 8
LANES = 256
VMEM = 60 * 2**20
MESH = pl.DeviceIdType.MESH
F32 = jnp.float32
BF16 = jnp.bfloat16


def dot(left, right):
    return jnp.dot(left, right, preferred_element_type=F32)


def dot_t(left, right):
    return lax.dot_general(left, right, (((1,), (1,)), ((), ())), preferred_element_type=F32)


def t_dot(left, right):
    return lax.dot_general(left, right, (((0,), (0,)), ((), ())), preferred_element_type=F32)


def two_parts(values):
    high = values.astype(BF16)
    return high, (values - high.astype(F32)).astype(BF16)


def dot_wide(values, right, transposed=False):
    rows = values.shape[0]
    both = (dot_t if transposed else dot)(jnp.concatenate(two_parts(values), 0), right)
    return both[:rows] + both[rows:]


def gelu(values):
    square = values * values
    bend = jnp.tanh(values * (NEAR + (NEAR * CUBE) * square))
    return values * (0.5 + 0.5 * bend)


def gelu_and_slope(values):
    square = values * values
    bend = jnp.tanh(values * (NEAR + (NEAR * CUBE) * square))
    part = 0.5 + 0.5 * bend
    act = values * part
    slope = part + act * (1.0 - part) * (2.0 * NEAR + (6.0 * NEAR * CUBE) * square)
    return act, slope


def norm_parts(values):
    centered = values - jnp.mean(values, -1, keepdims=True)
    scale = lax.rsqrt(jnp.mean(centered * centered, -1, keepdims=True) + EPSILON)
    return centered * scale, scale


def norm_back(grad, unit, scale, gain):
    scaled = gain * grad
    flat = jnp.mean(scaled, -1, keepdims=True)
    slant = jnp.mean(scaled * unit, -1, keepdims=True)
    return (scaled - flat - unit * slant) * scale


def col_sum(values):
    return jnp.sum(values, 0, keepdims=True)


def line_neighbours():
    res, half, count = lax.axis_index("res"), lax.axis_index("half"), lax.axis_size("res")
    return (
        (res > 0, (res - 1, half)),
        (res + half > 0, (res - 1 + half, 1 - half)),
        (res + half < count, (res + half, 1 - half)),
        (res < count - 1, (res + 1, half)),
    )


def line_count():
    res, half, count = lax.axis_index("res"), lax.axis_index("half"), lax.axis_size("res")
    return 4 - jnp.where(res > 0, 0, 2 - half) - jnp.where(res < count - 1, 0, 1 + half)


def greet_line():
    barrier = pltpu.get_barrier_semaphore()
    for exists, place in line_neighbours():

        @pl.when(exists)
        def _():
            pl.semaphore_signal(barrier, inc=1, device_id=place, device_id_type=MESH)


def halo_layout(rows):
    edge = REACH - rows
    return ((0, edge), (edge, rows), (REACH + rows, rows), (REACH + 2 * rows, edge))


def halo_kernel(own_ref, out_ref, window, send, recv):
    rows = own_ref.shape[0]
    layout = halo_layout(rows)
    neighbours = line_neighbours()
    greet_line()
    for (exists, _), (offset, size) in zip(neighbours, layout):

        @pl.when(jnp.logical_not(exists))
        def _():
            window[pl.ds(offset, size), :] = jnp.zeros((size, own_ref.shape[1]), own_ref.dtype)

    pl.semaphore_wait(pltpu.get_barrier_semaphore(), line_count())
    copies = []
    for at, (exists, place) in enumerate(neighbours):
        offset, size = layout[3 - at]
        first = rows - size if at == 3 else 0
        copy = pltpu.make_async_remote_copy(
            src_ref=own_ref.at[pl.ds(first, size)],
            dst_ref=window.at[pl.ds(offset, size)],
            send_sem=send.at[at],
            recv_sem=recv.at[3 - at],
            device_id=place,
            device_id_type=MESH,
        )
        copies.append((exists, copy))

        @pl.when(exists)
        def _():
            copy.start()

    window[pl.ds(REACH, rows), :] = own_ref[...]
    for at, (exists, _) in enumerate(neighbours):
        offset, size = layout[at]

        @pl.when(exists)
        def _():
            copies[at][1].wait_send()
            pltpu.make_async_remote_copy(
                src_ref=own_ref.at[pl.ds(0, size)],
                dst_ref=window.at[pl.ds(offset, size)],
                send_sem=send.at[at],
                recv_sem=recv.at[at],
                device_id=neighbours[at][1],
                device_id_type=MESH,
            ).wait_recv()

    out_ref[...] = window[...]


def fetch_window(own, collective):
    rows, width = own.shape
    return pl.pallas_call(
        halo_kernel,
        out_shape=jax.ShapeDtypeStruct((rows + 2 * REACH, width), own.dtype),
        in_specs=[pl.BlockSpec(memory_space=pltpu.VMEM)],
        out_specs=pl.BlockSpec(memory_space=pltpu.VMEM),
        scratch_shapes=[
            pltpu.VMEM((rows + 2 * REACH, width), own.dtype),
            pltpu.SemaphoreType.DMA((4,)),
            pltpu.SemaphoreType.DMA((4,)),
        ],
        compiler_params=pltpu.CompilerParams(collective_id=collective, has_side_effects=True),
        name="fetch_window",
    )(own)


def start_returns(table, landing, send, recv, rows):
    layout = halo_layout(rows)
    copies = []
    for at, (exists, place) in enumerate(line_neighbours()):
        offset, size = layout[at]
        back_offset, _ = layout[3 - at]
        copy = pltpu.make_async_remote_copy(
            src_ref=table.at[pl.ds(offset, size)],
            dst_ref=landing.at[pl.ds(back_offset, size)],
            send_sem=send.at[at],
            recv_sem=recv.at[3 - at],
            device_id=place,
            device_id_type=MESH,
        )
        copies.append(copy)

        @pl.when(exists)
        def _():
            copy.start()

    return copies


def finish_returns(table, landing, total, send, recv, rows, copies):
    layout = halo_layout(rows)
    total[...] = table[pl.ds(REACH, rows), :]
    for at, (exists, place) in enumerate(line_neighbours()):
        offset, size = layout[at]
        first = rows - size if at == 3 else 0

        @pl.when(exists)
        def _():
            copies[at].wait_send()
            pltpu.make_async_remote_copy(
                src_ref=table.at[pl.ds(offset, size)],
                dst_ref=landing.at[pl.ds(offset, size)],
                send_sem=send.at[at],
                recv_sem=recv.at[at],
                device_id=place,
                device_id_type=MESH,
            ).wait_recv()
            total[pl.ds(first, size), :] += landing[pl.ds(offset, size), :]


def return_kernel(table_ref, out_ref, landing, total, send, recv):
    rows = out_ref.shape[0]
    greet_line()
    pl.semaphore_wait(pltpu.get_barrier_semaphore(), line_count())
    copies = start_returns(table_ref, landing, send, recv, rows)
    finish_returns(table_ref, landing, total, send, recv, rows, copies)
    out_ref[...] = total[...]


def return_rows(table, collective):
    window, width = table.shape
    rows = window - 2 * REACH
    return pl.pallas_call(
        return_kernel,
        out_shape=jax.ShapeDtypeStruct((rows, width), F32),
        in_specs=[pl.BlockSpec(memory_space=pltpu.VMEM)],
        out_specs=pl.BlockSpec(memory_space=pltpu.VMEM),
        scratch_shapes=[
            pltpu.VMEM((window, width), F32),
            pltpu.VMEM((rows, width), F32),
            pltpu.SemaphoreType.DMA((4,)),
            pltpu.SemaphoreType.DMA((4,)),
        ],
        compiler_params=pltpu.CompilerParams(collective_id=collective, has_side_effects=True),
        name="return_rows",
    )(table)


def fill_table(window, far, own, table, rows):
    places = window.shape[0]
    table[pl.ds(0, places), :] = dot(window[...], far[...]).astype(BF16)
    table[pl.ds(places, rows), :] = dot(window[pl.ds(REACH, rows), :], own[...]).astype(BF16)
    rest = LANES - places - rows
    if rest:
        table[pl.ds(places + rows, rest), :] = jnp.zeros((rest, table.shape[1]), BF16)


def feed_forward(pooled, counts, own, w, keep):
    mean = pooled / counts
    summed = own + dot_wide(mean, w["third"][...]) + w["third_bias"][...]
    unit, _ = norm_parts(summed)
    normed = unit * w["gain_one"][...] + w["shift_one"][...]
    low = normed.astype(BF16)
    pre = dot(low, w["expand"][...]) + w["expand_bias"][...]
    act = gelu(pre).astype(BF16)
    second = normed + dot(act, w["reduce"][...]) + w["reduce_bias"][...]
    unit_two, _ = norm_parts(second)
    if keep is not None:
        keep["summed"][...] = summed
        keep["pre_expand"][...] = pre
        keep["second"][...] = second
        keep["normed"][...] = low
    return unit_two * w["gain_two"][...] + w["shift_two"][...]


NODE_WEIGHTS = (
    "far",
    "own",
    "edge",
    "second",
    "second_bias",
    "third",
    "third_bias",
    "gain_one",
    "shift_one",
    "expand",
    "expand_bias",
    "reduce",
    "reduce_bias",
    "gain_two",
    "shift_two",
)


def pool_rows(live_row, act_two, step):
    slots = act_two.shape[0] // BLOCK
    shape = (BLOCK, act_two.shape[0])
    mine = lax.broadcasted_iota(jnp.int32, shape, 1) // slots == lax.broadcasted_iota(jnp.int32, shape, 0)
    return dot(jnp.where(mine, live_row, 0.0).astype(BF16), act_two)


def first_kernel(rows, window, picks, edges, live_row, counts, *refs):
    w = dict(zip(NODE_WEIGHTS, refs))
    out, onehot, table, pooled = refs[len(NODE_WEIGHTS) :]
    step = pl.program_id(0)
    places = window.shape[0]

    @pl.when(step == 0)
    def _():
        fill_table(window, w["far"], w["own"], table, rows)

    size = edges.shape[0]
    lane = lax.broadcasted_iota(jnp.int32, (size, LANES), 1)
    residue = lax.broadcasted_iota(jnp.int32, (size, LANES), 0) // (size // BLOCK) + step * BLOCK
    hit = (lane == picks[...]) | (lane == residue + places)
    hot = jnp.where(hit, 1.0, 0.0).astype(BF16)
    onehot[...] = hot
    pre_one = dot(
        jnp.concatenate([hot, edges[...]], 1), jnp.concatenate([table[...], w["edge"][...]], 0)
    )
    act_one = gelu(pre_one).astype(BF16)
    pre_two = dot(act_one, w["second"][...]) + w["second_bias"][...]
    act_two = gelu(pre_two).astype(BF16)
    pooled[pl.ds(step * BLOCK, BLOCK), :] = pool_rows(live_row[...], act_two, step)

    @pl.when(step == pl.num_programs(0) - 1)
    def _():
        own = window[pl.ds(REACH, rows), :].astype(F32)
        out[...] = feed_forward(pooled[...], counts[...], own, w, None).astype(BF16)


def second_kernel(rows, window, onehot, edges, live, live_row, counts, *refs):
    w = dict(zip(NODE_WEIGHTS, refs))
    out, act_kept, slope_one, slope_two, pooled, summed, pre_expand, second, normed, table = refs[
        len(NODE_WEIGHTS) :
    ]
    step = pl.program_id(0)

    @pl.when(step == 0)
    def _():
        fill_table(window, w["far"], w["own"], table, rows)

    pre_one = dot(
        jnp.concatenate([onehot[...], edges[...]], 1),
        jnp.concatenate([table[...], w["edge"][...]], 0),
    )
    act_one, slope = gelu_and_slope(pre_one)
    act_one = act_one.astype(BF16)
    act_kept[...] = act_one
    slope_one[...] = slope.astype(BF16)
    pre_two = dot(act_one, w["second"][...]) + w["second_bias"][...]
    act_two, slope = gelu_and_slope(pre_two)
    slope_two[...] = (slope * live[...]).astype(BF16)
    pooled[pl.ds(step * BLOCK, BLOCK), :] = pool_rows(live_row[...], act_two.astype(BF16), step)

    @pl.when(step == pl.num_programs(0) - 1)
    def _():
        own = window[pl.ds(REACH, rows), :].astype(F32)
        keep = {"summed": summed, "pre_expand": pre_expand, "second": second, "normed": normed}
        out[...] = feed_forward(pooled[...], counts[...], own, w, keep).astype(BF16)


def whole(array):
    return pl.BlockSpec(array.shape, lambda i: (0,) * len(array.shape))


def by_rows(array, size):
    return pl.BlockSpec((size,) + array.shape[1:], lambda i: (i,) + (0,) * (len(array.shape) - 1))


def by_lanes(array, size):
    return pl.BlockSpec((1, size), lambda i: (0, i))


def shape(dims, kind):
    return jax.ShapeDtypeStruct(dims, kind)


def node_pass(first, window, hot, edges, live, live_row, counts, weights):
    rows = window.shape[0] - 2 * REACH
    width = window.shape[1]
    total = edges.shape[0]
    size = total // (rows // BLOCK)
    hidden = weights["second"].shape[0]
    inner = weights["expand"].shape[1]
    args = [window, hot, edges] + ([] if first else [live]) + [live_row, counts]
    specs = [whole(window), by_rows(hot, size), by_rows(edges, size)]
    specs += ([] if first else [by_rows(live, size)]) + [by_lanes(live_row, size), whole(counts)]
    for name in NODE_WEIGHTS:
        args.append(weights[name])
        specs.append(whole(weights[name]))
    out = shape((rows, width), BF16)
    table = pltpu.VMEM((LANES, hidden), BF16)
    if first:
        onehot = shape((total, LANES), BF16)
        outs, out_specs = (out, onehot), (whole(out), by_rows(onehot, size))
        scratch = [table, pltpu.VMEM((rows, hidden), F32)]
        kernel = first_kernel
    else:
        slots = shape((total, hidden), BF16)
        kept = (
            shape((rows, hidden), F32),
            shape((rows, width), F32),
            shape((rows, inner), F32),
            shape((rows, width), F32),
            shape((rows, width), BF16),
        )
        outs = (out, slots, slots, slots) + kept
        out_specs = (whole(out),) + (by_rows(slots, size),) * 3 + tuple(whole(k) for k in kept)
        scratch = [table]
        kernel = second_kernel
    return pl.pallas_call(
        functools.partial(kernel, rows),
        grid=(rows // BLOCK,),
        out_shape=outs,
        in_specs=specs,
        out_specs=out_specs,
        scratch_shapes=scratch,
        compiler_params=pltpu.CompilerParams(vmem_limit_bytes=VMEM),
        name="node_pass_first" if first else "node_pass_second",
    )(*args)


EDGE_WEIGHTS = ("far", "own", "edge", "edge_x", "second", "second_x", "third", "third_x", "gain", "shift")


def edge_kernel(rows, features, window, onehot, edges, cot, live, *refs):
    w = dict(zip(EDGE_WEIGHTS, refs))
    out, grad, spread, g_edge, g_second, g_third, g_norm, g_own, g_far, d_own, table = refs[
        len(EDGE_WEIGHTS) :
    ]
    step = pl.program_id(0)

    @pl.when(step == 0)
    def _():
        fill_table(window, w["far"], w["own"], table, rows)
        for total in (spread, g_edge, g_second, g_third, g_norm):
            total[...] = jnp.zeros(total.shape, F32)

    lane = lax.broadcasted_iota(jnp.int32, (1, LANES), 1)
    one = jnp.where(lane == features, 1.0, 0.0)
    inside = jnp.where(lane < features, 1.0, 0.0)
    hot, feats = onehot[...], edges[...]
    t_one = dot(jnp.concatenate([hot, feats], 1), jnp.concatenate([table[...], w["edge_x"][...]], 0))
    o_one, slope_one = gelu_and_slope(t_one)
    o_one = (o_one + one).astype(BF16)
    o_two, slope_two = gelu_and_slope(dot(o_one, w["second_x"][...]))
    o_two = (o_two + one).astype(BF16)
    summed = feats.astype(F32) + dot(o_two, w["third_x"][...])
    mean = jnp.sum(summed, -1, keepdims=True) * (1.0 / features)
    centered = (summed - mean) * inside
    scale = lax.rsqrt(jnp.sum(centered * centered, -1, keepdims=True) * (1.0 / features) + EPSILON)
    unit = centered * scale
    gain = w["gain"][...]
    out[...] = ((unit * gain + w["shift"][...]) * live[...]).astype(BF16)
    d_out = cot[...].astype(F32)
    tilted = d_out * unit
    scaled = d_out * gain
    flat = jnp.sum(scaled, -1, keepdims=True) * (1.0 / features)
    slant = jnp.sum(tilted * gain, -1, keepdims=True) * (1.0 / features)
    d_sum = ((scaled - flat - unit * slant) * scale) * inside
    g_norm[...] += jnp.concatenate([col_sum(tilted), col_sum(d_out)], 0)
    d_three = d_sum.astype(BF16)
    g_third[...] += t_dot(o_two, d_three)
    d_two = (dot_t(d_three, w["third"][...]) * slope_two).astype(BF16)
    g_second[...] += t_dot(o_one, d_two)
    d_one = (dot_t(d_two, w["second"][...]) * slope_one).astype(BF16)
    g_edge[...] += t_dot(feats, d_one)
    spread[...] += t_dot(hot, d_one)
    grad[...] = d_sum + dot_t(d_one, w["edge"][...])

    @pl.when(step == pl.num_programs(0) - 1)
    def _():
        places = window.shape[0]
        own_spread = spread[pl.ds(places, rows), :]
        g_own[...] = t_dot(window[pl.ds(REACH, rows), :], own_spread.astype(BF16))
        g_far[...] = t_dot(window[...], spread[pl.ds(0, places), :].astype(BF16))
        d_own[...] = dot_wide(own_spread, w["own"][...], True)


def edge_pass(features, window, hot, edges, cot, live, weights):
    places, width = window.shape
    rows = places - 2 * REACH
    total = edges.shape[0]
    size = total // (rows // BLOCK)
    args = [window, hot, edges, cot, live] + [weights[name] for name in EDGE_WEIGHTS]
    specs = [whole(window)] + [by_rows(a, size) for a in args[1:5]] + [whole(a) for a in args[5:]]
    out = shape((total, LANES), BF16)
    grad = shape((total, LANES), F32)
    square = shape((LANES, LANES), F32)
    tall = shape((width, LANES), F32)
    kept = (square,) * 4 + (shape((2, LANES), F32), tall, tall, shape((rows, width), F32))
    return pl.pallas_call(
        functools.partial(edge_kernel, rows, features),
        grid=(rows // BLOCK,),
        out_shape=(out, grad) + kept,
        in_specs=specs,
        out_specs=(by_rows(out, size), by_rows(grad, size)) + tuple(whole(k) for k in kept),
        scratch_shapes=[pltpu.VMEM((LANES, LANES), BF16)],
        compiler_params=pltpu.CompilerParams(vmem_limit_bytes=VMEM),
        name="edge_pass",
    )(*args)


def node_grad_kernel(
    cot, d_own, d_far, edge_far, summed, second, pre_expand, pooled, counts, third, expand, reduce_w,
    gain_one, gain_two, ds_out, du_out, slot_out, g_third, small,
):
    grad = cot[...].astype(F32) + d_own[...] + dot_wide(d_far[...], edge_far[...], True)
    unit, scale = norm_parts(second[...])
    dw = norm_back(grad, unit, scale, gain_two[...])
    gain_grad_two, shift_grad_two = col_sum(grad * unit), col_sum(grad)
    ds = dw.astype(BF16)
    ds_out[...] = ds
    _, slope = gelu_and_slope(pre_expand[...])
    dq = (dot_t(ds, reduce_w[...]) * slope).astype(BF16)
    dv = dw + dot_t(dq, expand[...])
    unit, scale = norm_parts(summed[...])
    du = norm_back(dv, unit, scale, gain_one[...])
    du_out[...] = du
    dm = (du / counts[...]).astype(BF16)
    slot_out[...] = dot_t(dm, third[...])
    g_third[...] = t_dot(jnp.concatenate(two_parts(pooled[...]), 0), jnp.concatenate([dm, dm], 0)).astype(
        BF16
    )
    width = cot.shape[1]
    small[...] = jnp.zeros(small.shape, F32)
    small[2:3, :] = col_sum(counts[...] * dm.astype(F32))
    small[3:4, :] = col_sum(dv * unit)
    small[4:5, :] = col_sum(dv)
    dq_sum = col_sum(dq.astype(F32))
    for part in range(dq_sum.shape[1] // width):
        small[5 + part : 6 + part, :] = dq_sum[:, part * width : (part + 1) * width]
    small[9:10, :] = col_sum(ds.astype(F32))
    small[10:11, :] = gain_grad_two
    small[11:12, :] = shift_grad_two


def node_grad(cot, d_own, d_far, edge_far, summed, second, pre_expand, pooled, counts, weights):
    rows, width = cot.shape
    hidden = weights["third"].shape[0]
    args = [cot, d_own, d_far, edge_far, summed, second, pre_expand, pooled, counts]
    args += [weights[n] for n in ("third", "expand", "reduce", "gain_one", "gain_two")]
    outs = (
        shape((rows, width), BF16),
        shape((rows, width), F32),
        shape((rows, hidden), F32),
        shape((hidden, width), BF16),
        shape((16, width), F32),
    )
    return pl.pallas_call(
        node_grad_kernel,
        out_shape=outs,
        in_specs=[pl.BlockSpec(memory_space=pltpu.VMEM)] * len(args),
        out_specs=tuple(pl.BlockSpec(memory_space=pltpu.VMEM) for _ in outs),
        compiler_params=pltpu.CompilerParams(vmem_limit_bytes=VMEM),
        name="node_grad",
    )(*args)


def pack_rows(pack, first, second, third, e_first, e_second, e_third):
    def cut(pieces, start, stop):
        at, got = 0, []
        for piece in pieces:
            low, high = max(start, at), min(stop, at + piece.shape[0])
            if low < high:
                got.append(piece[low - at : high - at])
            at += piece.shape[0]
        return jnp.concatenate(got, 0) if len(got) > 1 else got[0]

    for half in range(CORES):
        at = 0
        for pieces in (first, (second,), (third,)):
            size = sum(p.shape[0] for p in pieces) // CORES
            pack[half, pl.ds(at, size), :] = cut(pieces, half * size, (half + 1) * size).astype(BF16)
            at += size
        size = sum(p.shape[0] for p in e_first) // (2 * CORES)
        for side in range(2):
            start = (2 * half + side) * size
            pack[half, pl.ds(at, size), pl.ds(side * LANES, LANES)] = cut(
                e_first, start, start + size
            ).astype(BF16)
        at += size
        size = e_second.shape[0] // CORES
        for side, piece in enumerate((e_second, e_third)):
            pack[half, pl.ds(at, size), pl.ds(side * LANES, LANES)] = piece[
                half * size : (half + 1) * size
            ].astype(BF16)
        at += size
    return at


def message_grad_kernel(
    rows, features, window, onehot, edges, act, slope_one, slope_two, edge_grad, slot_grad, du,
    far, own, edge_w, second_w, g_third, small, e_edge, e_second, e_third, e_norm, e_own, e_far,
    grad, pack, spread, d_own, g_second, g_edge, g_bias,
):
    step = pl.program_id(0)

    @pl.when(step == 0)
    def _():
        for total in (spread, g_second, g_edge, g_bias):
            total[...] = jnp.zeros(total.shape, F32)

    slots = onehot.shape[0] // BLOCK
    hidden = act.shape[1]
    coming = slot_grad[pl.ds(step * BLOCK, BLOCK), :]
    coming = jnp.broadcast_to(coming[:, None, :], (BLOCK, slots, hidden)).reshape(BLOCK * slots, hidden)
    dp_two_f = coming * slope_two[...].astype(F32)
    g_bias[...] += col_sum(dp_two_f)
    dp_two = dp_two_f.astype(BF16)
    g_second[...] += t_dot(act[...], dp_two)
    dp_one = (dot_t(dp_two, second_w[...]) * slope_one[...].astype(F32)).astype(BF16)
    spread[...] += t_dot(onehot[...], dp_one)
    g_edge[...] += t_dot(edges[...], dp_one)
    grad[...] = edge_grad[...] + dot_t(dp_one, edge_w[...])

    @pl.when(step == pl.num_programs(0) - 1)
    def _():
        places = window.shape[0]
        own_spread = spread[pl.ds(places, rows), :]
        g_own = t_dot(window[pl.ds(REACH, rows), :], own_spread.astype(BF16))
        g_far = t_dot(window[...], spread[pl.ds(0, places), :].astype(BF16))
        d_own[...] = du[...] + dot_wide(own_spread, own[...], True)
        at = pack_rows(
            pack,
            (g_own, g_far, g_edge[pl.ds(0, features), :]),
            g_second[...],
            g_third[...],
            (e_own[...], e_far[...], e_edge[pl.ds(0, features), :]),
            e_second[pl.ds(0, features), :],
            e_third[pl.ds(0, features), :],
        )
        ones = [r[features : features + 1, :] for r in (e_edge, e_second, e_third)]
        tail = jnp.concatenate(
            [
                g_edge[features : features + 1, :],
                g_bias[...],
                small[2:12, :],
                jnp.concatenate([ones[0], ones[1]], 1),
                jnp.concatenate([ones[2], e_norm[0:1, :]], 1),
                jnp.concatenate([e_norm[1:2, :], jnp.zeros((1, LANES), F32)], 1),
                jnp.zeros((1, 2 * LANES), F32),
            ],
            0,
        ).astype(BF16)
        for half in range(CORES):
            pack[half, pl.ds(at, 16), :] = tail
            rest = pack.shape[1] - at - 16
            if rest:
                pack[half, pl.ds(at + 16, rest), :] = jnp.zeros((rest, pack.shape[2]), BF16)


def pack_size(count, features, width, hidden):
    used = (2 * width + features) // 2 + hidden // 2 + width // 2
    used += (2 * width + features) // 4 + features // 2 + 16
    part = -(-used // (2 * count * 16)) * 16
    return used, part


def message_grad(count, features, window, hot, edges, act, slope_one, slope_two, edge_grad, slot_grad,
                 du, weights, g_third, small, edge_grads):
    places, width = window.shape
    rows = places - 2 * REACH
    total, hidden = act.shape
    size = total // (rows // BLOCK)
    args = [window, hot, edges, act, slope_one, slope_two, edge_grad, slot_grad, du]
    args += [weights[n] for n in ("far", "own", "edge_plain", "second")] + [g_third, small] + edge_grads
    specs = [whole(window)] + [by_rows(a, size) for a in args[1:7]] + [whole(a) for a in args[7:]]
    _, part = pack_size(count, features, width, hidden)
    grad = shape((total, LANES), F32)
    kept = (
        shape((CORES, 2 * count * part, width), BF16),
        shape((LANES, hidden), F32),
        shape((rows, width), F32),
    )
    return pl.pallas_call(
        functools.partial(message_grad_kernel, rows, features),
        grid=(rows // BLOCK,),
        out_shape=(grad,) + kept,
        in_specs=specs,
        out_specs=(by_rows(grad, size),) + tuple(whole(k) for k in kept),
        scratch_shapes=[
            pltpu.VMEM((hidden, hidden), F32),
            pltpu.VMEM((LANES, hidden), F32),
            pltpu.VMEM((1, hidden), F32),
        ],
        compiler_params=pltpu.CompilerParams(vmem_limit_bytes=VMEM),
        name="message_grad",
    )(*args)


def wide_grad_kernel(normed, ds, expand, expand_bias, reduce_w, g_expand, g_reduce):
    chunk, at = pl.program_id(0), pl.program_id(1)
    half = lax.axis_index("half")
    width = normed.shape[1]
    part = expand.shape[1] // pl.num_programs(1)
    count = pl.num_programs(1) // CORES
    block = lax.rem(at + half * count, CORES * count)
    here = pl.ds(pl.multiple_of(block * part, part), part)

    @pl.when((chunk == 0) & (at == 0))
    def _():
        g_expand[...] = jnp.zeros(g_expand.shape, F32)
        g_reduce[...] = jnp.zeros(g_reduce.shape, F32)

    pre = dot(normed[...], expand[:, here]) + expand_bias[:, here]
    act, slope = gelu_and_slope(pre)
    dq = (dot_t(ds[...], reduce_w[here, :]) * slope).astype(BF16)
    mine = pl.ds(pl.multiple_of(half * (width // CORES), width // CORES), width // CORES)
    g_expand[:, here] += t_dot(normed[:, mine], dq)

    @pl.when(at < count)
    def _():
        rows = pl.ds(pl.multiple_of(at * part, part), part)
        g_reduce[rows, :] += t_dot(act.astype(BF16), ds[...])


def wide_grad(normed, ds, weights, chunk):
    total, width = normed.shape
    expand, bias, reduce_w = weights["expand"], weights["expand_bias"], weights["reduce"]
    inner = expand.shape[1]
    blocks = inner // 256
    row_spec = pl.BlockSpec((chunk, width), lambda i, j: (i, 0))
    fixed = lambda a: pl.BlockSpec(a.shape, lambda i, j: (0, 0))
    outs = (shape((width // CORES, inner), F32), shape((inner // CORES, width), F32))
    return pl.pallas_call(
        wide_grad_kernel,
        grid=(total // chunk, blocks),
        out_shape=outs,
        in_specs=[row_spec, row_spec, fixed(expand), fixed(bias), fixed(reduce_w)],
        out_specs=tuple(fixed(o) for o in outs),
        compiler_params=pltpu.CompilerParams(vmem_limit_bytes=VMEM),
        name="wide_grad",
    )(normed, ds, expand, bias, reduce_w)


def chip_dims(count):
    side = 1
    while 2 * (2 * side) ** 3 <= count and count % (4 * side * side) == 0:
        side *= 2
    return {"z": count // (side * side), "y": side, "x": side}


ORDERS = (("x", "y", "z"), ("y", "x", "z"))


def sum_kernel(
    dims, part, pack, out_half, grad_half, table, d_own, far,
    total_out, edges_out, grads_out, nodes_out,
    acc, got, landed, away, gathered, rows_in, row_total, node_buf, node_half, edges_in, grads_in,
    pair_send, pair_recv, step_send, step_recv, line_send, line_recv,
):
    res, half = lax.axis_index("res"), lax.axis_index("half")
    place = {
        "x": lax.rem(res, dims["x"]),
        "y": lax.rem(res // dims["x"], dims["y"]),
        "z": res // (dims["x"] * dims["y"]),
    }
    stride = {"x": 1, "y": dims["x"], "z": dims["x"] * dims["y"]}
    count = dims["x"] * dims["y"] * dims["z"]
    rows = d_own.shape[0]
    partner = (res, 1 - half)

    def peer(axis, ahead):
        to = lax.rem(place[axis] + ahead, dims[axis])
        return to, (res + (to - place[axis]) * stride[axis], half)

    barrier = pltpu.get_barrier_semaphore()
    greet_line()
    pl.semaphore_signal(barrier, inc=1, device_id=partner, device_id_type=MESH)
    others = 1
    for axis in dims:
        for ahead in range(1, dims[axis]):
            pl.semaphore_signal(barrier, inc=1, device_id=peer(axis, ahead)[1], device_id_type=MESH)
            others += 1
    pl.semaphore_wait(barrier, others + line_count())

    def pair_copy(at, source, target):
        copy = pltpu.make_async_remote_copy(
            src_ref=source,
            dst_ref=target,
            send_sem=pair_send.at[at],
            recv_sem=pair_recv.at[at],
            device_id=partner,
            device_id_type=MESH,
        )
        copy.start()
        return copy

    span = count * part
    parts = [
        pair_copy(p, pack.at[1 - half, pl.ds(p * span, span)], got.at[pl.ds(p * span, span)])
        for p in range(2)
    ]
    returns = start_returns(table, rows_in, line_send, line_recv, rows)
    pairs = [pair_copy(2, out_half.at[1 - half], edges_in), pair_copy(3, grad_half.at[1 - half], grads_in)]

    sem = 0
    regions = []
    for p in range(2):
        parts[p].wait()
        here = pl.ds(p * span, span)
        acc[here, :] = (pack[half, here, :].astype(F32) + got[here, :].astype(F32)).astype(BF16)
        regions.append((p * span, span))
    bases = [p * span for p in range(2)]
    for level in range(3):
        started = []
        for p in range(2):
            axis = ORDERS[p][level]
            start, size = regions[p]
            share = size // dims[axis]
            copies = []
            for ahead in range(1, dims[axis]):
                to, device = peer(axis, ahead)
                copy = pltpu.make_async_remote_copy(
                    src_ref=acc.at[pl.ds(pl.multiple_of(start + to * share, 16), share)],
                    dst_ref=landed.at[pl.ds(bases[p], share)],
                    send_sem=step_send.at[sem],
                    recv_sem=step_recv.at[sem],
                    device_id=device,
                    device_id_type=MESH,
                )
                copy.start()
                copies.append((copy, bases[p], share))
                bases[p] += share
                sem += 1
            started.append(copies)
        for p in range(2):
            axis = ORDERS[p][level]
            start, size = regions[p]
            share = size // dims[axis]
            mine = pl.multiple_of(start + place[axis] * share, 16)
            total = acc[pl.ds(mine, share), :].astype(F32)
            for copy, base, _ in started[p]:
                copy.wait()
                total = total + landed[pl.ds(base, share), :].astype(F32)
            acc[pl.ds(mine, share), :] = total.astype(BF16)
            regions[p] = (mine, share)
        if level == 0:
            finish_returns(table, rows_in, row_total, line_send, line_recv, rows, returns)
            grad = d_own[...] + dot_wide(row_total[...], far[...], True)
            wide = grad.shape[1] // CORES
            node_buf[0] = grad[:, :wide]
            node_buf[1] = grad[:, wide:]
            pairs.append(pair_copy(4, node_buf.at[1 - half], node_half))

    for p in range(2):
        mine, share = regions[p]
        gathered[pl.ds(mine, share), :] = acc[pl.ds(mine, share), :]
    for level in (2, 1, 0):
        started = []
        for p in range(2):
            axis = ORDERS[p][level]
            mine, share = regions[p]
            for ahead in range(1, dims[axis]):
                _, device = peer(axis, ahead)
                copy = pltpu.make_async_remote_copy(
                    src_ref=gathered.at[pl.ds(mine, share)],
                    dst_ref=gathered.at[pl.ds(mine, share)],
                    send_sem=step_send.at[sem],
                    recv_sem=step_recv.at[sem],
                    device_id=device,
                    device_id_type=MESH,
                )
                copy.start()
                started.append(copy)
                sem += 1
            regions[p] = (pl.multiple_of(mine - place[axis] * share, 16), share * dims[axis])
        for copy in started:
            copy.wait()
    for copy in pairs:
        copy.wait()
    total_out[...] = gathered[...]
    edges_out[half] = out_half[half]
    edges_out[1 - half] = edges_in[...]
    grads_out[half] = grad_half[half]
    grads_out[1 - half] = grads_in[...]
    nodes_out[half] = node_buf[half]
    nodes_out[1 - half] = node_half[...]


def sum_over_chips(count, pack, out_half, grad_half, table, d_own, far):
    dims = chip_dims(count)
    total, width = pack.shape[1:]
    part = total // (2 * count)
    rows = d_own.shape[0]
    steps = 2 * 2 * sum(size - 1 for size in dims.values())
    vmem = pl.BlockSpec(memory_space=pltpu.VMEM)
    outs = (
        shape((total, width), BF16),
        shape(out_half.shape, BF16),
        shape(grad_half.shape, F32),
        shape((CORES, rows, width // CORES), F32),
    )
    return pl.pallas_call(
        functools.partial(sum_kernel, dims, part),
        out_shape=outs,
        in_specs=[vmem] * 6,
        out_specs=(vmem,) * 4,
        scratch_shapes=[
            pltpu.VMEM((total, width), BF16),
            pltpu.VMEM((total, width), BF16),
            pltpu.VMEM((total, width), BF16),
            pltpu.VMEM((16, width), BF16),
            pltpu.VMEM((total, width), BF16),
            pltpu.VMEM(table.shape, F32),
            pltpu.VMEM((rows, table.shape[1]), F32),
            pltpu.VMEM((CORES, rows, width // CORES), F32),
            pltpu.VMEM((rows, width // CORES), F32),
            pltpu.VMEM(out_half.shape[1:], BF16),
            pltpu.VMEM(grad_half.shape[1:], F32),
            pltpu.SemaphoreType.DMA((5,)),
            pltpu.SemaphoreType.DMA((5,)),
            pltpu.SemaphoreType.DMA((steps,)),
            pltpu.SemaphoreType.DMA((steps,)),
            pltpu.SemaphoreType.DMA((4,)),
            pltpu.SemaphoreType.DMA((4,)),
        ],
        compiler_params=pltpu.CompilerParams(
            collective_id=7, has_side_effects=True, vmem_limit_bytes=VMEM
        ),
        name="sum_over_chips",
    )(pack, out_half, grad_half, table, d_own, far)


def as_row(vector, width=None):
    vector = vector.astype(F32)
    if width is not None:
        vector = jnp.pad(vector, (0, width - vector.shape[0]))
    return vector[None, :]


def spread_slots(values, fill=0):
    rows, slots = values.shape[:2]
    each = slots // CORES
    room = -(-each // 16) * 16
    values = values.reshape((rows, CORES, each) + values.shape[2:])
    pads = [(0, 0), (0, 0), (0, room - each)] + [(0, 0)] * (values.ndim - 3)
    values = jnp.pad(values, pads, constant_values=fill)
    return values.reshape((rows * CORES * room,) + values.shape[3:])


def body(
    nodes, edges, neighbours, counts,
    message_first, message_first_bias, message_second, message_second_bias, message_third, message_third_bias,
    node_norm_gain, node_norm_shift, expand_weight, expand_bias, reduce_weight, reduce_bias,
    output_norm_gain, output_norm_shift,
    edge_first, edge_first_bias, edge_second, edge_second_bias, edge_third, edge_third_bias,
    edge_norm_gain, edge_norm_shift, cot_nodes, cot_edges,
):
    res, half, count = lax.axis_index("res"), lax.axis_index("half"), lax.axis_size("res")
    rows_dev, width = nodes.shape
    slots, features = edges.shape[1:]
    hidden = message_second.shape[0]
    rows = rows_dev // CORES
    room = -(-(slots // CORES) // 16) * 16

    def mine(values):
        return lax.dynamic_slice_in_dim(values, half * rows, rows, 0)

    own = mine(nodes)
    own_counts = mine(counts)
    base = res * rows_dev + half * rows - REACH
    picks = spread_slots(mine(neighbours) - base, -1)[:, None]
    used = lax.broadcasted_iota(jnp.int32, (rows, slots), 1) < own_counts[:, None]
    live_flat = spread_slots(used.astype(F32))
    live, live_row = live_flat[:, None], live_flat[None, :]
    counts_f = own_counts.astype(F32)[:, None]
    lane = lax.broadcasted_iota(jnp.int32, (1, 1, LANES), 2)
    feats = jnp.pad(mine(edges), ((0, 0), (0, 0), (0, LANES - features)))
    feats = spread_slots(jnp.where(lane == features, jnp.ones((), BF16), feats))
    cots = mine(cot_edges) * used.astype(BF16)[:, :, None]
    cots = spread_slots(jnp.pad(cots, ((0, 0), (0, 0), (0, LANES - features))))

    node_w = {
        "own": message_first[:width],
        "far": message_first[width : 2 * width],
        "edge": jnp.concatenate(
            [
                message_first[2 * width :],
                message_first_bias[None],
                jnp.zeros((LANES - features - 1, hidden), BF16),
            ],
            0,
        ),
        "edge_plain": jnp.pad(message_first[2 * width :], ((0, LANES - features), (0, 0))),
        "second": message_second,
        "second_bias": as_row(message_second_bias),
        "third": message_third,
        "third_bias": as_row(message_third_bias),
        "gain_one": as_row(node_norm_gain),
        "shift_one": as_row(node_norm_shift),
        "expand": expand_weight,
        "expand_bias": as_row(expand_bias),
        "reduce": reduce_weight,
        "reduce_bias": as_row(reduce_bias),
        "gain_two": as_row(output_norm_gain),
        "shift_two": as_row(output_norm_shift),
    }

    def square(weight, bias=None):
        weight = jnp.pad(weight, ((0, 0), (0, LANES - weight.shape[1])))
        parts = [weight]
        if bias is not None:
            parts.append(bias[None, :])
        have = sum(p.shape[0] for p in parts)
        return jnp.concatenate(parts + [jnp.zeros((LANES - have, LANES), BF16)], 0)

    def padded(vector):
        return jnp.pad(vector, (0, LANES - features))

    tall = jnp.pad(edge_first[: 2 * width], ((0, 0), (0, LANES - features)))
    take_one = jnp.where(jnp.arange(LANES) == features, -jnp.ones((), BF16), padded(edge_third_bias))
    edge_w = {
        "own": tall[:width],
        "far": tall[width:],
        "edge": square(edge_first[2 * width :]),
        "edge_x": square(edge_first[2 * width :], padded(edge_first_bias)),
        "second": square(edge_second),
        "second_x": square(edge_second, padded(edge_second_bias)),
        "third": square(edge_third),
        "third_x": square(edge_third, take_one),
        "gain": as_row(edge_norm_gain, LANES),
        "shift": as_row(edge_norm_shift, LANES),
    }

    window = fetch_window(own, 1)
    fed, hot = node_pass(True, window, picks, feats, live, live_row, counts_f, node_w)
    fed_window = fetch_window(fed, 2)
    state, act, slope_one, slope_two, pooled, summed, pre_expand, second, normed = node_pass(
        False, fed_window, hot, feats, live, live_row, counts_f, node_w
    )
    state_window = fetch_window(state, 3)
    normed_all = lax.all_gather(normed, ("res", "half"), tiled=True)
    out, grad, spread, e_edge, e_second, e_third, e_norm, e_own, e_far, d_own = edge_pass(
        features, state_window, hot, feats, cots, live, edge_w
    )
    d_far = return_rows(spread[: rows + 2 * REACH], 4)
    ds, du, slot_grad, g_third, small = node_grad(
        mine(cot_nodes), d_own, d_far, edge_w["far"], summed, second, pre_expand, pooled, counts_f, node_w
    )
    ds_all = lax.all_gather(ds, ("res", "half"), tiled=True)
    grad, pack, spread, d_own = message_grad(
        count, features, fed_window, hot, feats, act, slope_one, slope_two, grad, slot_grad, du, node_w,
        g_third, small, [e_edge, e_second, e_third, e_norm, e_own, e_far],
    )

    def by_half(values):
        values = values.reshape(rows, CORES, room, LANES)
        return jnp.transpose(values, (1, 0, 2, 3))

    sums, out_pair, grad_pair, node_pair = sum_over_chips(
        count, pack, by_half(out), by_half(grad), spread[: rows + 2 * REACH], d_own, node_w["far"]
    )
    g_expand, g_reduce = wide_grad(normed_all, ds_all, node_w, rows_dev * min(count, 16))

    each = slots // CORES
    at = 0
    taken = []
    for size in ((2 * width + features) // 2, hidden // 2, hidden // 2):
        taken.append(sums[at : at + size].astype(F32))
        at += size
    size = (2 * width + features) // 4
    first = sums[at : at + size]
    e_first_grad = jnp.concatenate([first[:, :features], first[:, LANES : LANES + features]], 0).astype(F32)
    at += size
    both = sums[at : at + features // 2].astype(F32)
    at += features // 2
    tail = sums[at : at + 16].astype(F32)

    def share(row, size):
        return lax.dynamic_slice_in_dim(row, half * (size // CORES), size // CORES, 0)

    inner = expand_weight.shape[1]
    wide_bias = tail[5 : 5 + inner // width].reshape(-1)
    state_out = lax.dynamic_slice(
        state_window, (REACH - half * rows, half * (width // CORES)), (rows_dev, width // CORES)
    )
    return (
        state_out,
        out_pair[:, :, :each, :features].reshape(rows_dev, each, features),
        node_pair.reshape(rows_dev, width // CORES),
        grad_pair[:, :, :each, :features].reshape(rows_dev, each, features),
        taken[0],
        share(tail[0], hidden),
        taken[1],
        share(tail[1], hidden),
        taken[2],
        share(tail[2], width),
        share(tail[3], width),
        share(tail[4], width),
        g_expand,
        share(wide_bias, inner),
        g_reduce,
        share(tail[9], width),
        share(tail[10], width),
        share(tail[11], width),
        e_first_grad,
        share(tail[12, :features], features),
        both[:, :features],
        share(tail[12, LANES : LANES + features], features),
        both[:, LANES : LANES + features],
        share(tail[13, :features], features),
        share(tail[13, LANES : LANES + features], features),
        share(tail[14, :features], features),
    )


def solution(mesh):
    rows, slots = P("res", None), P("res", None, None)
    copied = P()
    down, vec = P("half", None), P("half")
    return jax.shard_map(
        body,
        mesh=mesh,
        in_specs=(rows, slots, rows, P("res")) + (copied,) * 22 + (rows, slots),
        out_specs=(
            P("res", "half"),
            P("res", "half", None),
            P("res", "half"),
            P("res", "half", None),
            down, vec, down, vec, down, vec, vec, vec, down, vec, down, vec, vec, vec,
            down, vec, down, vec, down, vec, vec, vec,
        ),
        check_vma=False,
    )
```

```python
import functools
import types

import jax
import jax.numpy as jnp
from jax import lax
from jax.experimental import pallas as pl
from jax.experimental.pallas import tpu as pltpu
from jax.sharding import PartitionSpec as P

EPSILON = 1e-05
REACH = 64
CORES = 2
NEAR = 0.7978845608
CUBE = 0.044715
STEP = 20
CHAIN = 5
LANES = 256
LANE = 128
WIDE = 256
VMEM = 62 * 2**20
MESH = pl.DeviceIdType.MESH
F32 = jnp.float32
BF16 = jnp.bfloat16


def dot(left, right):
    return jnp.dot(left, right, preferred_element_type=F32)


def dot_t(left, right):
    return lax.dot_general(left, right, (((1,), (1,)), ((), ())), preferred_element_type=F32)


def t_dot(left, right):
    return lax.dot_general(left, right, (((0,), (0,)), ((), ())), preferred_element_type=F32)


def two_parts(values):
    high = values.astype(BF16)
    return high, (values - high.astype(F32)).astype(BF16)


def dot_wide(values, right, transposed=False):
    rows = values.shape[0]
    both = (dot_t if transposed else dot)(jnp.concatenate(two_parts(values), 0), right)
    return both[:rows] + both[rows:]


def gelu(values):
    square = values * values
    bend = jnp.tanh(values * (NEAR + (NEAR * CUBE) * square))
    return values * (0.5 + 0.5 * bend)


def gelu_and_slope(values):
    square = values * values
    bend = jnp.tanh(values * (NEAR + (NEAR * CUBE) * square))
    part = 0.5 + 0.5 * bend
    act = values * part
    slope = part + act * (1.0 - part) * (2.0 * NEAR + (6.0 * NEAR * CUBE) * square)
    return act, slope


def norm_parts(values):
    centered = values - jnp.mean(values, -1, keepdims=True)
    scale = lax.rsqrt(jnp.mean(centered * centered, -1, keepdims=True) + EPSILON)
    return centered * scale, scale


def norm_back(grad, unit, scale, gain):
    scaled = gain * grad
    flat = jnp.mean(scaled, -1, keepdims=True)
    slant = jnp.mean(scaled * unit, -1, keepdims=True)
    return (scaled - flat - unit * slant) * scale


def col_sum(values):
    return jnp.sum(values, 0, keepdims=True)


def iota(dims, axis):
    return lax.broadcasted_iota(jnp.int32, dims, axis)


def chip_dims(count):
    side = 1
    while 2 * (2 * side) ** 3 <= count and count % (4 * side * side) == 0:
        side *= 2
    return side, count // (side * side)


def up(size, unit):
    return -(-size // unit) * unit


def chunk_rows(count, width, hidden, features):
    tall = (2 * width + features) // CORES
    wide = width // LANE
    early = (hidden // CORES) * wide + features * (up(tall, LANE) // LANE) + 3 * (features // CORES)
    second = (hidden // CORES) * wide
    first = tall * wide + 16 * wide
    return tuple(up(rows, 16 * count) for rows in (early, second, first))


def cut(pieces, start, stop):
    at, got = 0, []
    for piece in pieces:
        low, high = max(start, at), min(stop, at + piece.shape[0])
        if low < high:
            got.append(piece[low - at : high - at])
        at += piece.shape[0]
    return jnp.concatenate(got, 0) if len(got) > 1 else got[0]


def put_wide(pack, half, at, piece):
    rows = piece.shape[0]
    for block in range(piece.shape[1] // LANE):
        pack[half, pl.ds(at, rows), :] = piece[:, block * LANE : (block + 1) * LANE].astype(BF16)
        at += rows
    return at


def put_rest(pack, at):
    rest = pack.shape[1] - at
    if rest:
        for half in range(CORES):
            pack[half, pl.ds(at, rest), :] = jnp.zeros((rest, LANE), BF16)


def take_wide(packed, at, rows, blocks):
    pieces = [packed[pl.ds(at + b * rows, rows), :] for b in range(blocks)]
    return jnp.concatenate(pieces, 1).astype(F32), at + blocks * rows


class Copies:
    def __init__(self, send, recv):
        self.send, self.recv, self.used = send, recv, 0

    def group(self, entries):
        made = []
        for source, target, device in entries:
            at = self.used
            self.used += 1
            made.append(functools.partial(self._make, source, target, device, at))
        return Group(made)

    def _make(self, source, target, device, at):
        return pltpu.make_async_remote_copy(
            src_ref=source,
            dst_ref=target,
            send_sem=self.send.at[at],
            recv_sem=self.recv.at[at],
            device_id=device,
            device_id_type=MESH,
        )


class Group:
    def __init__(self, made):
        self.made = made

    def start(self):
        for make in self.made:
            make().start()

    def wait(self):
        for make in self.made:
            make().wait()


class Place:
    def __init__(self):
        res, half, count = lax.axis_index("res"), lax.axis_index("half"), lax.axis_size("res")
        side, deep = chip_dims(count)
        x, y, z = lax.rem(res, side), lax.rem(res // side, side), res // (side * side)
        first = half == 0
        self.res, self.half, self.count = res, half, count
        self.dims = (side, side, deep)
        self.at = (jnp.where(first, x, y), jnp.where(first, y, x), z)
        self.strides = (jnp.where(first, 1, side), jnp.where(first, side, 1), side * side)
        self.partner = (res, 1 - half)

    def peers(self, level):
        size, here = self.dims[level], self.at[level]
        found = []
        for ahead in range(1, size):
            to = lax.rem(here + ahead, size)
            found.append((to, (self.res + (to - here) * self.strides[level], self.half)))
        return found

    def line(self):
        res, half, count = self.res, self.half, self.count
        return (
            (res > 0, (res - 1, half)),
            (res + half > 0, (res - 1 + half, 1 - half)),
            (res + half < count, (res + half, 1 - half)),
            (res < count - 1, (res + 1, half)),
        )

    def line_count(self):
        res, half, count = self.res, self.half, self.count
        return 4 - jnp.where(res > 0, 0, 2 - half) - jnp.where(res < count - 1, 0, 1 + half)


def greet(place):
    barrier = pltpu.get_barrier_semaphore()

    def signal(device):
        pl.semaphore_signal(barrier, inc=1, device_id=device, device_id_type=MESH)

    for exists, device in place.line():
        pl.when(exists)(functools.partial(signal, device))
    signal(place.partner)
    others = 1
    for level in range(3):
        for _, device in place.peers(level):
            signal(device)
            others += 1
    pl.semaphore_wait(barrier, others + place.line_count())


def halo_layout(rows):
    edge = REACH - rows
    return ((0, edge), (edge, rows), (REACH + rows, rows), (REACH + 2 * rows, edge))


class Halo:
    def __init__(self, place, window, rows, send, recv, first):
        self.place, self.window, self.rows = place, window, rows
        self.send, self.recv, self.first = send, recv, first

    def clear(self):
        for (exists, _), (offset, size) in zip(self.place.line(), halo_layout(self.rows)):

            @pl.when(jnp.logical_not(exists))
            def _():
                self.window[pl.ds(offset, size), :] = jnp.zeros((size, self.window.shape[1]), self.window.dtype)

    def _copy(self, at, device):
        offset, size = halo_layout(self.rows)[3 - at]
        first = REACH + (self.rows - size if at == 3 else 0)
        return pltpu.make_async_remote_copy(
            src_ref=self.window.at[pl.ds(first, size)],
            dst_ref=self.window.at[pl.ds(offset, size)],
            send_sem=self.send.at[self.first + at],
            recv_sem=self.recv.at[self.first + 3 - at],
            device_id=device,
            device_id_type=MESH,
        )

    def start(self):
        for at, (exists, device) in enumerate(self.place.line()):

            @pl.when(exists)
            def _():
                self._copy(at, device).start()

    def wait(self):
        for at, (exists, device) in enumerate(self.place.line()):
            offset, size = halo_layout(self.rows)[at]

            @pl.when(exists)
            def _():
                self._copy(at, device).wait_send()
                pltpu.make_async_remote_copy(
                    src_ref=self.window.at[pl.ds(offset, size)],
                    dst_ref=self.window.at[pl.ds(offset, size)],
                    send_sem=self.send.at[self.first + at],
                    recv_sem=self.recv.at[self.first + at],
                    device_id=device,
                    device_id_type=MESH,
                ).wait_recv()


class Returns:
    def __init__(self, place, table, landing, rows, send, recv, first):
        self.place, self.table, self.landing, self.rows = place, table, landing, rows
        self.send, self.recv, self.first = send, recv, first

    def _copy(self, at, device):
        layout = halo_layout(self.rows)
        offset, size = layout[at]
        return pltpu.make_async_remote_copy(
            src_ref=self.table.at[pl.ds(offset, size)],
            dst_ref=self.landing.at[pl.ds(layout[3 - at][0], size)],
            send_sem=self.send.at[self.first + at],
            recv_sem=self.recv.at[self.first + 3 - at],
            device_id=device,
            device_id_type=MESH,
        )

    def start(self):
        for at, (exists, device) in enumerate(self.place.line()):

            @pl.when(exists)
            def _():
                self._copy(at, device).start()

    def finish(self, total):
        total[...] = self.table[pl.ds(REACH, self.rows), :]
        for at, (exists, device) in enumerate(self.place.line()):
            offset, size = halo_layout(self.rows)[at]
            first = self.rows - size if at == 3 else 0

            @pl.when(exists)
            def _():
                self._copy(at, device).wait_send()
                pltpu.make_async_remote_copy(
                    src_ref=self.table.at[pl.ds(offset, size)],
                    dst_ref=self.landing.at[pl.ds(offset, size)],
                    send_sem=self.send.at[self.first + at],
                    recv_sem=self.recv.at[self.first + at],
                    device_id=device,
                    device_id_type=MESH,
                ).wait_recv()
                total[pl.ds(first, size), :] += self.landing[pl.ds(offset, size), :]


def gather_groups(place, copies, ref, unit, source=None, base=0):
    mine = (place.at[0] * place.dims[1] + place.at[1]) * place.dims[2] + place.at[2]
    groups, size = [], unit
    start = mine * unit
    for level in (2, 1, 0):
        here = ref.at[pl.ds(pl.multiple_of(base + start, 16), size)]
        from_ref = here if source is None or level < 2 else source
        groups.append(copies.group([(from_ref, here, device) for _, device in place.peers(level)]))
        start = start - place.at[level] * size
        size = size * place.dims[level]
    return groups


class ChipSum:
    def __init__(self, place, copies, pack, got, landed, gathered):
        self.place, self.pack, self.got, self.landed, self.gathered = place, pack, got, landed, gathered
        half, size = place.half, pack.shape[1]
        self.pair = copies.group([(pack.at[1 - half], got, place.partner)])
        self.steps, self.shares = [], []
        start, base = 0, 0
        for level in range(3):
            share = size // place.dims[level]
            entries, lands = [], []
            for to, device in place.peers(level):
                source = pack.at[half, pl.ds(pl.multiple_of(start + to * share, 16), share)]
                entries.append((source, landed.at[pl.ds(base, share)], device))
                lands.append(base)
                base += share
            start = pl.multiple_of(start + place.at[level] * share, 16)
            size = share
            self.steps.append(copies.group(entries))
            self.shares.append((start, share, lands))
        self.back = gather_groups(place, copies, gathered, size)

    def send_pair(self):
        self.pair.start()

    def add_pair(self):
        self.pair.wait()
        half = self.place.half
        self.pack[half] = (self.pack[half].astype(F32) + self.got[...].astype(F32)).astype(BF16)

    def start(self, level):
        self.steps[level].start()

    def finish(self, level):
        self.steps[level].wait()
        start, share, lands = self.shares[level]
        half = self.place.half
        total = self.pack[half, pl.ds(start, share), :].astype(F32)
        for base in lands:
            total = total + self.landed[pl.ds(base, share), :].astype(F32)
        if level < 2:
            self.pack[half, pl.ds(start, share), :] = total.astype(BF16)
        else:
            self.gathered[pl.ds(start, share), :] = total.astype(BF16)

    def start_back(self, step):
        self.back[step].start()

    def finish_back(self, step):
        self.back[step].wait()


def flat(values):
    return values.reshape(values.shape[0] * values.shape[1], values.shape[2])


def feed_forward(r, pooled, own):
    width = own.shape[1]
    v = r.vec
    mean = pooled / r.counts[:, 0:1]
    summed = own + dot_wide(mean, r.third[...]) + v[2:3, :width]
    unit, _ = norm_parts(summed)
    normed = unit * v[3:4, :width] + v[4:5, :width]
    low = normed.astype(BF16)
    pre = dot(low, r.expand[...]) + v[8:9, :]
    second = normed + dot(gelu(pre).astype(BF16), r.reduce[...]) + v[5:6, :width]
    unit_two, _ = norm_parts(second)
    r.summed[...] = summed
    r.pre_expand[...] = pre
    r.second[...] = second
    r.normed[...] = low
    return unit_two * v[6:7, :width] + v[7:8, :width]


def fill_table(window, far, own, bias, table, rows, multiply):
    places = window.shape[0]
    table[pl.ds(0, places), :] = multiply(window[...], far).astype(BF16)
    table[pl.ds(places, rows), :] = (multiply(window[pl.ds(REACH, rows), :], own) + bias).astype(BF16)


def chain_parts(step):
    return [step * STEP + part * CHAIN for part in range(STEP // CHAIN)]


def chain_rows(r, slot):
    rows = r.counts.shape[0]
    return pl.ds(pl.multiple_of(slot * rows, CHAIN * rows), CHAIN * rows)


def step_rows(r, step):
    rows = r.counts.shape[0]
    return pl.ds(pl.multiple_of(step * (STEP * rows), STEP * rows), STEP * rows)


def build_block(r, step, half, places):
    rows = r.counts.shape[0]
    here = pl.ds(step * STEP, STEP)
    named = r.picks[here]
    dims = (STEP, rows, named.shape[2])
    spread = jnp.broadcast_to(named, dims)
    mine = iota(dims, 2) == iota(dims, 1) + half * rows
    pick = jnp.sum(jnp.where(mine, spread, 0.0), -1, keepdims=True)
    dims = (STEP, rows, LANES)
    lane = iota(dims, 2)
    hit = (lane.astype(F32) == pick) | (lane == iota(dims, 1) + places)
    r.onehot[here] = jnp.where(hit, 1.0, 0.0).astype(BF16)


def joined_rows(r, slot, slots):
    here = pl.ds(slot, slots)
    return jnp.concatenate([flat(r.onehot[here]), flat(r.edges_raw[here])], 1)


def live_rows(r, slot, width):
    count = r.counts[...]
    dims = (CHAIN,) + count.shape
    live = jnp.where(iota(dims, 0) + slot < count[None], 1.0, 0.0)
    return flat(jnp.concatenate([live] * (width // LANE), -1))


def live_column(r, slot):
    count = r.counts[...]
    dims = (CHAIN,) + count.shape
    return flat(jnp.where(iota(dims, 0) + slot < count[None], 1.0, 0.0))[:, 0:1]


def node_block(r, step, keep):
    rows = r.counts.shape[0]
    hidden = r.second_w.shape[0]
    slots = chain_parts(step)
    dims = (rows, CHAIN * rows)
    count = jnp.broadcast_to(r.counts[:, 0:1], dims)
    pre = [dot(joined_rows(r, slot, CHAIN), r.table[...]) for slot in slots]
    acts = []
    for slot, values in zip(slots, pre):
        if keep:
            here = chain_rows(r, slot)
            act, slope = gelu_and_slope(values)
            act = act.astype(BF16)
            r.act[here, :] = act
            r.slope_one[here, :] = slope.astype(BF16)
        else:
            act = gelu(values).astype(BF16)
        acts.append(act)
    pre = [dot(act, r.second_w[...]) + r.vec[1:2, :hidden] for act in acts]
    total = r.pooled[...]
    for slot, values in zip(slots, pre):
        if keep:
            act, slope = gelu_and_slope(values)
            r.slope_two[chain_rows(r, slot), :] = (slope * live_rows(r, slot, hidden)).astype(BF16)
        else:
            act = gelu(values)
        used = jnp.where(r.lane_slot[0:1, :] + slot.astype(F32) < count, r.diagonal[...], 0.0)
        total = total + dot(used.astype(BF16), act.astype(BF16))
    r.pooled[...] = total


def edge_block(r, step, features):
    v = r.vec
    bias_two, bias_three = v[10:11, :features], v[11:12, :features]
    gain, shift = v[12:13, :features], v[13:14, :features]
    rows = r.counts.shape[0]
    split = lambda values: values.reshape(CHAIN, rows, features)
    for slot in chain_parts(step):
        here = pl.ds(slot, CHAIN)
        joined = joined_rows(r, slot, CHAIN)
        live = live_column(r, slot)
        o_one, slope_one = gelu_and_slope(dot(joined, r.e_table[...]))
        o_one = o_one.astype(BF16)
        o_two, slope_two = gelu_and_slope(dot(o_one, r.e_second_w[...]) + bias_two)
        o_two = o_two.astype(BF16)
        summed = joined[:, LANES:].astype(F32) + (dot(o_two, r.e_third_w[...]) + bias_three)
        unit, scale = norm_parts(summed)
        r.edge_out[here] = split((unit * gain + shift) * live).astype(BF16)
        d_out = flat(r.cots_raw[here]).astype(F32) * live
        r.ge_norm[0:1, :] += col_sum(d_out * unit)
        r.ge_norm[1:2, :] += col_sum(d_out)
        d_sum = norm_back(d_out, unit, scale, gain)
        r.ge_norm[2:3, :] += col_sum(d_sum)
        d_three = d_sum.astype(BF16)
        r.ge_third[...] += t_dot(o_two, d_three)
        d_two = dot_t(d_three, r.e_third_w[...]) * slope_two
        r.ge_norm[3:4, :] += col_sum(d_two)
        d_two = d_two.astype(BF16)
        r.ge_second[...] += t_dot(o_one, d_two)
        d_one = (dot_t(d_two, r.e_second_w[...]) * slope_one).astype(BF16)
        r.ge_first[...] += t_dot(joined, d_one)
        r.edge_grad[here] = split(d_sum + dot(d_one, r.e_first_t[:, pl.ds(2 * r.nodes_width, features)]))


def node_grad(r, cot, far_total):
    v = r.vec
    width = cot.shape[1]
    grad = cot.astype(F32) + r.e_own_back[...] + dot_wide(far_total, r.e_first_t[:, pl.ds(width, width)])
    unit, scale = norm_parts(r.second[...])
    dw = norm_back(grad, unit, scale, v[6:7, :width])
    gain_two, shift_two = col_sum(grad * unit), col_sum(grad)
    ds = dw.astype(BF16)
    r.ds[...] = ds
    _, slope = gelu_and_slope(r.pre_expand[...])
    dq = (dot_t(ds, r.reduce[...]) * slope).astype(BF16)
    dv = dw + dot_t(dq, r.expand[...])
    unit, scale = norm_parts(r.summed[...])
    du = norm_back(dv, unit, scale, v[3:4, :width])
    r.du[...] = du
    counts = r.counts[:, 0:1]
    dm = (du / counts).astype(BF16)
    r.slot_grad[...] = dot_t(dm, r.third[...])
    r.dm[...] = dm
    small = r.small
    small[...] = jnp.zeros(small.shape, F32)
    small[2:3, :] = col_sum(counts * dm.astype(F32))
    small[3:4, :] = col_sum(dv * unit)
    small[4:5, :] = col_sum(dv)
    dq_sum = col_sum(dq.astype(F32))
    for part in range(dq_sum.shape[1] // width):
        small[5 + part : 6 + part, :] = dq_sum[:, part * width : (part + 1) * width]
    small[9:10, :] = col_sum(ds.astype(F32))
    small[10:11, :] = gain_two
    small[11:12, :] = shift_two


def put_features(pack, half, at, e_second, e_third):
    part = e_second.shape[0] // CORES
    two = [ref[pl.ds(half * part, part), :] for ref in (e_second, e_third)]
    for piece in two:
        at = put_wide(pack, half, at, piece[:, :LANE])
    return put_wide(pack, half, at, jnp.concatenate([piece[:, LANE:] for piece in two], 1))


def pack_early(r, pack):
    hidden, width = r.third.shape
    features = r.ge_second.shape[0]
    dm = r.dm[...]
    g_third = t_dot(jnp.concatenate(two_parts(r.pooled[...]), 0), jnp.concatenate([dm, dm], 0))
    g_edge = jnp.transpose(r.ge_first[pl.ds(LANES, features), :])
    e_first = jnp.concatenate([r.ge_own[...], r.ge_far[...], g_edge], 1)
    tall = e_first.shape[1] // CORES
    fill = jnp.zeros((features, up(tall, LANE) - tall), F32)
    for half in range(CORES):
        part = hidden // CORES
        at = put_wide(pack, half, 0, g_third[half * part : (half + 1) * part])
        piece = jnp.concatenate([e_first[:, half * tall : (half + 1) * tall], fill], 1)
        at = put_wide(pack, half, at, piece)
        at = put_features(pack, half, at, r.ge_second, r.ge_third)
    put_rest(pack, at)


def pack_second(r, pack):
    part = r.g_second.shape[0] // CORES
    for half in range(CORES):
        at = put_wide(pack, half, 0, r.g_second[pl.ds(half * part, part), :])
    put_rest(pack, at)


def small_rows(r, places):
    rows = r.counts.shape[0]
    features = r.ge_norm.shape[1]
    fill = jnp.zeros((1, LANES - features), F32)
    own = pl.ds(places, rows)
    edge = [col_sum(r.ge_first[own, :])] + [r.ge_norm[at : at + 1, :] for at in (3, 2, 0, 1)]
    edge = [jnp.concatenate([row, fill], 1) for row in edge] + [jnp.zeros((1, LANES), F32)]
    lines = [col_sum(r.g_first[own, :]), r.g_bias[...], r.small[2:12, :]]
    lines += [jnp.concatenate(edge[at : at + 2], 1) for at in (0, 2, 4)]
    return jnp.concatenate(lines + [jnp.zeros((1, r.small.shape[1]), F32)], 0)


def pack_first(r, pack, g_own, g_far, features, places):
    pieces = [g_own, g_far, r.g_first[pl.ds(LANES, features), :]]
    tall = sum(piece.shape[0] for piece in pieces) // CORES
    small = small_rows(r, places)
    for half in range(CORES):
        at = put_wide(pack, half, 0, cut(pieces, half * tall, (half + 1) * tall))
        at = put_wide(pack, half, at, small)
    put_rest(pack, at)


def second_block(r, step):
    hidden = r.act.shape[1]
    here = step_rows(r, step)
    coming = jnp.broadcast_to(r.slot_grad[...][None], (STEP,) + r.slot_grad.shape)
    d_two_f = flat(coming) * r.slope_two[here, :].astype(F32)
    r.g_bias[...] += col_sum(d_two_f)
    d_two = d_two_f.astype(BF16)
    r.g_second[...] += t_dot(r.act[here, :], d_two)
    r.slope_one[here, :] = (dot_t(d_two, r.second_w[...]) * r.slope_one[here, :].astype(F32)).astype(BF16)


def first_block(r, step, features):
    rows = r.counts.shape[0]
    d_one = r.slope_one[step_rows(r, step), :]
    r.g_first[...] += t_dot(joined_rows(r, step * STEP, STEP), d_one)
    more = dot_t(d_one, r.table[pl.ds(LANES, features), :])
    r.edge_grad[pl.ds(step * STEP, STEP)] += more.reshape(STEP, rows, features)


def wide_block(r, step, half, fresh):
    width, inner = r.expand.shape
    blocks = inner // WIDE
    mine = blocks // CORES
    block = lax.rem(step + half * mine, blocks)
    here = pl.ds(pl.multiple_of(block * WIDE, WIDE), WIDE)
    cols = pl.ds(pl.multiple_of(half * (width // CORES), width // CORES), width // CORES)
    bias = r.vec[8:9, here]
    total_rows = r.normed_all.shape[0]
    parts = 4
    size = total_rows // parts
    g_expand = jnp.zeros((width // CORES, WIDE), F32)
    g_reduce = jnp.zeros((WIDE, width), F32)
    for part in range(parts):
        rows = pl.ds(part * size, size)
        normed, ds = r.normed_all[rows, :], r.ds_all[rows, :]
        act, slope = gelu_and_slope(dot(normed, r.expand[:, here]) + bias)
        dq = (dot_t(ds, r.reduce[here, :]) * slope).astype(BF16)
        g_expand = g_expand + t_dot(r.normed_all[rows, cols], dq)
        r.wide_act[rows, :] = act.astype(BF16)
    if fresh:
        r.g_expand[:, here] = g_expand
    else:
        r.g_expand[:, here] += g_expand

    @pl.when(step < mine)
    def _():
        out = pl.ds(pl.multiple_of(step * WIDE, WIDE), WIDE)
        found = t_dot(r.wide_act[...], r.ds_all[...])
        if fresh:
            r.g_reduce[out, :] = found
        else:
            r.g_reduce[out, :] += found


INPUTS = (
    "vec", "nodes", "edges", "neighbours", "first_in", "second_in", "third_in", "expand_in", "reduce_in",
    "e_first_in", "e_second_in", "e_third_in", "cot_nodes", "cot_edges",
)
OUTPUTS = (
    "state_out", "edges_out", "fed_out", "grads_out", "sum_early", "sum_second", "sum_first",
    "expand_out", "reduce_out", "normed_slots", "ds_slots",
)


def kernel(names, features, *refs):
    r = types.SimpleNamespace(**dict(zip(names, refs)))
    place = Place()
    res, half, count = place.res, place.half, place.count
    rows_dev, width = r.nodes.shape
    rows = rows_dev // CORES
    places = rows + 2 * REACH
    slots = r.edges.shape[0]
    each = slots // CORES
    steps = slots // STEP
    r.nodes_width = width
    own = pl.ds(REACH, rows)
    mine = pl.ds(pl.multiple_of(half * rows, 16), rows)

    loads = {}

    def load(name, source, target):
        copy = pltpu.make_async_copy(source, target, r.load_sem.at[len(loads)])
        loads[name] = copy
        copy.start()

    load("nodes", r.nodes.at[mine], r.windows.at[0, own])
    load("neighbours", r.neighbours, r.neighbours_raw)
    load("first", r.first_in, r.first)
    load("edges", r.edges.at[:, mine, :], r.edges_raw)
    load("second", r.second_in, r.second_w)
    load("e_first", r.e_first_in, r.e_first_t)
    load("e_second", r.e_second_in, r.e_second_w)
    load("e_third", r.e_third_in, r.e_third_w)
    load("third", r.third_in, r.third)
    load("expand", r.expand_in, r.expand)
    load("reduce", r.reduce_in, r.reduce)
    load("cot_edges", r.cot_edges.at[:, mine, :], r.cots_raw)
    load("cot_nodes", r.cot_nodes.at[mine], r.cot_rows)

    halos = [
        Halo(place, r.windows.at[k], rows, r.line_send, r.line_recv, 4 * k) for k in range(3)
    ]
    edge_returns = Returns(place, r.ge_first, r.edge_landing, rows, r.line_send, r.line_recv, 12)
    node_returns = Returns(place, r.g_first, r.node_landing, rows, r.line_send, r.line_recv, 16)
    copies = Copies(r.step_send, r.step_recv)
    sums = [
        ChipSum(place, copies, pack, got, landed, gathered)
        for pack, got, landed, gathered in (
            (r.pack_early, r.got_early, r.landed_early, r.all_early),
            (r.pack_second, r.got_second, r.landed_second, r.all_second),
            (r.pack_first, r.got_first, r.landed_first, r.all_first),
        )
    ]
    early, second, first = sums
    span = count * rows

    def row_gather(source, slot_ref):
        base = half * span
        groups = gather_groups(place, copies, slot_ref, rows, source, base)
        here = slot_ref.at[pl.ds(pl.multiple_of(base, 16), span)]
        groups.append(copies.group([(here, here, place.partner)]))
        return groups

    normed_gather = row_gather(r.normed, r.normed_slots)
    ds_gather = row_gather(r.ds, r.ds_slots)
    my_unit = (place.at[0] * place.dims[1] + place.at[1]) * place.dims[2] + place.at[2]
    my_slot = pl.ds(pl.multiple_of(half * span + my_unit * rows, 16), rows)
    normed_keep = pltpu.make_async_copy(r.normed, r.normed_slots.at[my_slot], r.keep_sem.at[0])
    ds_keep = pltpu.make_async_copy(r.ds, r.ds_slots.at[my_slot], r.keep_sem.at[1])
    there = pl.ds(pl.multiple_of(half * rows, 16), rows)
    my_slots = pl.ds(half * each, each)
    its_slots = pl.ds((1 - half) * each, each)
    edges_target = r.edges_out.at[:, there, :]
    edges_pair = copies.group([(r.edge_out.at[its_slots], edges_target, place.partner)])
    edges_keep = pltpu.make_async_copy(r.edge_out.at[my_slots], edges_target, r.keep_sem.at[2])
    grads_target = r.grads_out.at[:, there, :]
    grads_pair = copies.group([(r.edge_grad.at[its_slots], grads_target, place.partner)])
    grads_keep = pltpu.make_async_copy(r.edge_grad.at[my_slots], grads_target, r.keep_sem.at[3])
    fed_pair = copies.group([(r.fed_grad.at[1 - half], r.fed_out.at[there], place.partner)])
    fed_keep = pltpu.make_async_copy(r.fed_grad.at[half], r.fed_out.at[there], r.keep_sem.at[4])

    greet(place)
    loads["nodes"].wait()
    halos[0].start()
    for halo in halos:
        halo.clear()
    dims = (rows, LANE)
    counted = jnp.broadcast_to(r.vec[14:15, :LANE], dims)
    counted = jnp.sum(jnp.where(iota(dims, 1) == iota(dims, 0) + half * rows, counted, 0.0), -1, keepdims=True)
    r.counts[...] = jnp.broadcast_to(counted, dims)
    dims = (rows, CHAIN * rows)
    lane = iota(dims, 1)
    r.diagonal[...] = jnp.where(lax.rem(lane, rows) == iota(dims, 0), 1.0, 0.0)
    r.lane_slot[...] = (iota(r.lane_slot.shape, 1) // rows).astype(F32)
    loads["neighbours"].wait()
    base = res * rows_dev + half * rows - REACH
    named = (r.neighbours_raw[...] - base).astype(F32)
    r.picks[...] = named.reshape(slots, 1, rows_dev)

    def build(step, carry):
        build_block(r, step, half, places)
        return carry

    lax.fori_loop(0, steps, build, 0)
    for table in (r.table, r.e_table):
        rest = LANES - places - rows
        if rest:
            table[pl.ds(places + rows, rest), :] = jnp.zeros((rest, table.shape[1]), BF16)
    hidden = r.table.shape[1]
    for name in ("first", "e_first", "e_second", "e_third"):
        loads[name].wait()
    r.table[pl.ds(LANES, features), :] = r.first[pl.ds(2 * width, features), :]
    edge_part = r.e_first_t[:, pl.ds(2 * width, features)]
    r.e_table[pl.ds(LANES, features), :] = jnp.transpose(edge_part.astype(F32)).astype(BF16)
    loads["edges"].wait()
    bias = r.vec[0:1, :hidden]
    far_w, own_w = r.first[pl.ds(width, width), :], r.first[pl.ds(0, width), :]
    halos[0].wait()
    fill_table(r.windows.at[0], far_w, own_w, bias, r.table, rows, dot)
    r.pooled[...] = jnp.zeros(r.pooled.shape, F32)
    loads["second"].wait()

    def first_pass(step, carry):
        node_block(r, step, False)
        return carry

    lax.fori_loop(0, steps, first_pass, 0)
    loads["third"].wait()
    loads["expand"].wait()
    loads["reduce"].wait()
    r.windows[1, own, :] = feed_forward(r, r.pooled[...], r.windows[0, own, :].astype(F32)).astype(BF16)

    halos[1].start()
    loads["cot_edges"].wait()
    loads["cot_nodes"].wait()
    halos[1].wait()
    fill_table(r.windows.at[1], far_w, own_w, bias, r.table, rows, dot)
    r.pooled[...] = jnp.zeros(r.pooled.shape, F32)

    def second_pass(step, carry):
        node_block(r, step, True)
        return carry

    lax.fori_loop(0, steps, second_pass, 0)
    r.windows[2, own, :] = feed_forward(r, r.pooled[...], r.windows[1, own, :].astype(F32)).astype(BF16)

    halos[2].start()
    normed_keep.start()
    normed_gather[0].start()
    for ref in (r.ge_norm, r.ge_first, r.ge_second, r.ge_third, r.g_second, r.g_first, r.g_bias):
        ref[...] = jnp.zeros(ref.shape, F32)
    halos[2].wait()
    e_own, e_far = r.e_first_t[:, pl.ds(0, width)], r.e_first_t[:, pl.ds(width, width)]
    fill_table(r.windows.at[2], e_far, e_own, r.vec[9:10, :features], r.e_table, rows, dot_t)
    state_keep = pltpu.make_async_copy(
        r.windows.at[
            2,
            pl.ds(pl.multiple_of(REACH - half * rows, 16), rows_dev),
            pl.ds(pl.multiple_of(half * (width // CORES), width // CORES), width // CORES),
        ],
        r.state_out,
        r.keep_sem.at[5],
    )
    state_keep.start()

    def edge_pass(step, carry):
        edge_block(r, step, features)

        @pl.when(step == 1)
        def _():
            normed_keep.wait()
            normed_gather[0].wait()
            normed_gather[1].start()

        return carry

    lax.fori_loop(0, steps, edge_pass, 0)
    edge_returns.start()
    edges_keep.start()
    edges_pair.start()
    normed_gather[1].wait()
    normed_gather[2].start()
    own_spread = r.ge_first[pl.ds(places, rows), :]
    r.ge_own[...] = t_dot(own_spread.astype(BF16), r.windows[2, own, :])
    r.ge_far[...] = t_dot(r.ge_first[pl.ds(0, places), :].astype(BF16), r.windows[2])
    r.e_own_back[...] = dot_wide(own_spread, e_own)
    edge_returns.finish(r.edge_total)

    node_grad(r, r.cot_rows[...], r.edge_total[...])
    ds_keep.start()
    ds_gather[0].start()
    pack_early(r, r.pack_early)
    early.send_pair()
    normed_gather[2].wait()
    normed_gather[3].start()

    def second_layer(step, carry):
        second_block(r, step)

        @pl.when(step == 0)
        def _():
            early.add_pair()
            early.start(0)

        @pl.when(step == 1)
        def _():
            ds_keep.wait()
            ds_gather[0].wait()
            ds_gather[1].start()

        return carry

    lax.fori_loop(0, steps, second_layer, 0)
    pack_second(r, r.pack_second)
    second.send_pair()
    early.finish(0)
    early.start(1)
    ds_gather[1].wait()
    ds_gather[2].start()

    def first_layer(step, carry):
        first_block(r, step, features)

        @pl.when(step == 0)
        def _():
            second.add_pair()
            second.start(0)

        @pl.when(step == 1)
        def _():
            early.finish(1)
            early.start(2)

        return carry

    lax.fori_loop(0, steps, first_layer, 0)
    node_returns.start()
    grads_keep.start()
    own_spread = r.g_first[pl.ds(places, rows), :]
    g_own = t_dot(r.windows[1, own, :], own_spread.astype(BF16))
    g_far = t_dot(r.windows[1], r.g_first[pl.ds(0, places), :].astype(BF16))
    pack_first(r, r.pack_first, g_own, g_far, features, places)
    first.send_pair()
    grads_pair.start()
    second.finish(0)
    second.start(1)
    ds_gather[2].wait()
    ds_gather[3].start()
    own_back = r.du[...] + dot_wide(own_spread, own_w, True)
    first.add_pair()
    first.start(0)
    node_returns.finish(r.node_total)
    fed = own_back + dot_wide(r.node_total[...], far_w, True)
    for part in range(CORES):
        r.fed_grad[part] = fed[:, part * (width // CORES) : (part + 1) * (width // CORES)]
    fed_keep.start()
    fed_pair.start()
    early.finish(2)
    early.start_back(0)
    second.finish(1)
    second.start(2)
    normed_gather[3].wait()
    ds_gather[3].wait()

    events = {
        0: (lambda: early.finish_back(0), lambda: early.start_back(1)),
        1: (lambda: second.finish(2), lambda: second.start_back(0), lambda: first.finish(0), lambda: first.start(1)),
        2: (lambda: early.finish_back(1), lambda: early.start_back(2)),
        3: (lambda: second.finish_back(0), lambda: second.start_back(1), lambda: first.finish(1), lambda: first.start(2)),
        4: (lambda: early.finish_back(2),),
        5: (lambda: second.finish_back(1), lambda: second.start_back(2), lambda: first.finish(2), lambda: first.start_back(0)),
        7: (lambda: second.finish_back(2), lambda: first.finish_back(0), lambda: first.start_back(1)),
    }
    blocks = r.expand.shape[1] // WIDE
    chunk = r.normed_all.shape[0]
    for at in range(2 * span // chunk):
        rows_here = pl.ds(at * chunk, chunk)
        fetches = [
            pltpu.make_async_copy(r.normed_slots.at[rows_here], r.normed_all, r.keep_sem.at[6]),
            pltpu.make_async_copy(r.ds_slots.at[rows_here], r.ds_all, r.keep_sem.at[7]),
        ]
        for fetch in fetches:
            fetch.start()
        for fetch in fetches:
            fetch.wait()

        def wide(step, carry):
            wide_block(r, step, half, at == 0)
            if at == 0:
                for when, actions in events.items():

                    @pl.when(step == when)
                    def _():
                        for act in actions:
                            act()

            return carry

        lax.fori_loop(0, blocks, wide, 0)

    outs = [
        (r.g_expand, r.expand_out),
        (r.g_reduce, r.reduce_out),
        (r.all_early, r.sum_early),
        (r.all_second, r.sum_second),
        (r.all_first, r.sum_first),
    ]
    stores = [
        pltpu.make_async_copy(source, target, r.keep_sem.at[8 + at]) for at, (source, target) in enumerate(outs)
    ]
    for store in stores[:4]:
        store.start()
    first.finish_back(1)
    first.start_back(2)
    for group in (edges_pair, grads_pair, fed_pair):
        group.wait()
    for copy in (edges_keep, grads_keep, fed_keep, state_keep):
        copy.wait()
    first.finish_back(2)
    stores[4].start()
    for store in stores:
        store.wait()


def shape(dims, kind):
    return jax.ShapeDtypeStruct(dims, kind)


def run(arrays):
    by_name = dict(zip(INPUTS, arrays))
    count = lax.axis_size("res")
    rows_dev, width = by_name["nodes"].shape
    slots, _, features = by_name["edges"].shape
    hidden = by_name["second_in"].shape[0]
    inner = by_name["expand_in"].shape[1]
    rows = rows_dev // CORES
    places = rows + 2 * REACH
    total = rows * slots
    each = slots // CORES
    tall = by_name["first_in"].shape[0]
    early, second, first = chunk_rows(count, width, hidden, features)
    side, deep = chip_dims(count)
    everyone = CORES * count * rows
    chunk = min(everyone, 16 * rows_dev)
    outs = (
        shape((rows_dev, width // CORES), BF16),
        shape((each, rows_dev, features), BF16),
        shape((rows_dev, width // CORES), F32),
        shape((each, rows_dev, features), F32),
        shape((early, LANE), BF16),
        shape((second, LANE), BF16),
        shape((first, LANE), BF16),
        shape((width // CORES, inner), F32),
        shape((inner // CORES, width), F32),
        shape((everyone, width), BF16),
        shape((everyone, width), BF16),
    )
    peers = 2 * (side - 1) + deep - 1
    remote = 3 * (2 * peers + 1) + 2 * (peers + 1) + 3
    scratch = {
        "windows": ((3, places, width), BF16),
        "neighbours_raw": ((slots, rows_dev), jnp.int32),
        "picks": ((slots, 1, rows_dev), F32),
        "counts": ((rows, LANE), F32),
        "diagonal": ((rows, CHAIN * rows), F32),
        "lane_slot": ((8, CHAIN * rows), F32),
        "first": ((tall, hidden), BF16),
        "second_w": ((hidden, hidden), BF16),
        "third": ((hidden, width), BF16),
        "expand": ((width, inner), BF16),
        "reduce": ((inner, width), BF16),
        "e_first_t": ((features, tall), BF16),
        "e_second_w": ((features, features), BF16),
        "e_third_w": ((features, features), BF16),
        "edges_raw": ((slots, rows, features), BF16),
        "cots_raw": ((slots, rows, features), BF16),
        "cot_rows": ((rows, width), BF16),
        "onehot": ((slots, rows, LANES), BF16),
        "table": ((LANES + features, hidden), BF16),
        "e_table": ((LANES + features, features), BF16),
        "act": ((total, hidden), BF16),
        "slope_one": ((total, hidden), BF16),
        "slope_two": ((total, hidden), BF16),
        "pooled": ((rows, hidden), F32),
        "summed": ((rows, width), F32),
        "second": ((rows, width), F32),
        "pre_expand": ((rows, inner), F32),
        "normed": ((rows, width), BF16),
        "edge_out": ((slots, rows, features), BF16),
        "edge_grad": ((slots, rows, features), F32),
        "ge_norm": ((8, features), F32),
        "ge_first": ((LANES + features, features), F32),
        "ge_second": ((features, features), F32),
        "ge_third": ((features, features), F32),
        "ge_own": ((features, width), F32),
        "ge_far": ((features, width), F32),
        "e_own_back": ((rows, width), F32),
        "edge_landing": ((places, features), F32),
        "edge_total": ((rows, features), F32),
        "ds": ((rows, width), BF16),
        "du": ((rows, width), F32),
        "dm": ((rows, width), BF16),
        "slot_grad": ((rows, hidden), F32),
        "small": ((16, width), F32),
        "g_second": ((hidden, hidden), F32),
        "g_first": ((LANES + features, hidden), F32),
        "g_bias": ((1, hidden), F32),
        "node_landing": ((places, hidden), F32),
        "node_total": ((rows, hidden), F32),
        "fed_grad": ((CORES, rows, width // CORES), F32),
        "normed_all": ((chunk, width), BF16),
        "ds_all": ((chunk, width), BF16),
        "wide_act": ((chunk, WIDE), BF16),
        "g_expand": ((width // CORES, inner), F32),
        "g_reduce": ((inner // CORES, width), F32),
    }
    for name, size in (("early", early), ("second", second), ("first", first)):
        scratch["pack_" + name] = ((CORES, size, LANE), BF16)
        for kind in ("got_", "landed_", "all_"):
            scratch[kind + name] = ((size, LANE), BF16)
    sems = {"load_sem": 13, "keep_sem": 13, "line_send": 20, "line_recv": 20, "step_send": remote, "step_recv": remote}
    names = INPUTS + OUTPUTS + tuple(scratch) + tuple(sems)
    anywhere = pl.BlockSpec(memory_space=pl.ANY)
    return pl.pallas_call(
        functools.partial(kernel, names, features),
        out_shape=outs,
        in_specs=[pl.BlockSpec(memory_space=pltpu.VMEM)] + [anywhere] * (len(INPUTS) - 1),
        out_specs=(anywhere,) * len(outs),
        scratch_shapes=[pltpu.VMEM(dims, kind) for dims, kind in scratch.values()]
        + [pltpu.SemaphoreType.DMA((size,)) for size in sems.values()],
        compiler_params=pltpu.CompilerParams(
            collective_id=1, has_side_effects=True, vmem_limit_bytes=VMEM
        ),
        name="graph_layer",
    )(*arrays)


def unpack_kernel(width, hidden, features, inner, early, second, first, *outs):
    (first_g, b_one, second_g, b_two, third_g, b_three, gain_one, shift_one, b_expand, b_reduce, gain_two,
     shift_two, e_first, eb_one, e_second, eb_two, e_third, eb_three, e_gain, e_shift) = outs
    half = lax.axis_index("half")
    wide = width // LANE
    tall = (2 * width + features) // CORES
    third_g[...], at = take_wide(early, 0, hidden // CORES, wide)
    e_whole, at = take_wide(early, at, features, up(tall, LANE) // LANE)
    e_first[...] = e_whole[:, :tall]
    rest = features - LANE
    part = features // CORES
    left_two, at = take_wide(early, at, part, 1)
    left_three, at = take_wide(early, at, part, 1)
    right, at = take_wide(early, at, part, 1)
    e_second[...] = jnp.concatenate([left_two, right[:, :rest]], 1)
    e_third[...] = jnp.concatenate([left_three, right[:, rest:]], 1)
    second_g[...], _ = take_wide(second, 0, hidden // CORES, wide)
    first_g[...], at = take_wide(first, 0, tall, wide)
    small, _ = take_wide(first, at, 16, wide)

    def share(target, row):
        size = target.shape[-1]
        target[...] = jnp.where(half == 0, row[:, :size], row[:, size : 2 * size])

    for target, row in ((b_one, 0), (b_two, 1), (b_three, 2), (gain_one, 3), (shift_one, 4), (b_reduce, 9), (gain_two, 10), (shift_two, 11)):
        share(target, small[row : row + 1])
    share(b_expand, jnp.concatenate([small[5 + p : 6 + p] for p in range(inner // width)], 1))
    share(eb_one, small[12:13, :LANES])
    share(eb_two, small[12:13, LANES:])
    share(eb_three, small[13:14, :LANES])
    share(e_gain, small[13:14, LANES:])
    share(e_shift, small[14:15, :LANES])


def unpack(sums, width, hidden, features, inner):
    tall = (2 * width + features) // CORES
    flat = lambda size: shape((1, size // CORES), F32)
    outs = (
        shape((tall, hidden), F32), flat(hidden),
        shape((hidden // CORES, hidden), F32), flat(hidden),
        shape((hidden // CORES, width), F32), flat(width),
        flat(width), flat(width), flat(inner), flat(width), flat(width), flat(width),
        shape((features, tall), F32), flat(features),
        shape((features // CORES, features), F32), flat(features),
        shape((features // CORES, features), F32), flat(features),
        flat(features), flat(features),
    )
    vmem = pl.BlockSpec(memory_space=pltpu.VMEM)
    return pl.pallas_call(
        functools.partial(unpack_kernel, width, hidden, features, inner),
        out_shape=outs,
        in_specs=[vmem] * 3,
        out_specs=(vmem,) * len(outs),
        compiler_params=pltpu.CompilerParams(vmem_limit_bytes=VMEM),
        name="unpack",
    )(*sums)


def body(
    nodes, edges, neighbours, counts,
    message_first, message_first_bias, message_second, message_second_bias, message_third, message_third_bias,
    node_norm_gain, node_norm_shift, expand_weight, expand_bias, reduce_weight, reduce_bias,
    output_norm_gain, output_norm_shift,
    edge_first, edge_first_bias, edge_second, edge_second_bias, edge_third, edge_third_bias,
    edge_norm_gain, edge_norm_shift, cot_nodes, cot_edges,
):
    width, features = nodes.shape[1], edges.shape[2]
    hidden, inner = message_second.shape[0], expand_weight.shape[1]

    rows = (
        message_first_bias, message_second_bias, message_third_bias, node_norm_gain, node_norm_shift, reduce_bias,
        output_norm_gain, output_norm_shift, expand_bias, edge_first_bias, edge_second_bias, edge_third_bias,
        edge_norm_gain, edge_norm_shift, counts,
    )
    at = iota((16, inner), 0)
    vec = jnp.zeros((16, inner), F32)
    for row, vector in enumerate(rows):
        line = jnp.pad(vector.astype(F32), (0, inner - vector.shape[0]))
        vec = jnp.where(at == row, line[None, :], vec)
    by_slots = lambda values: jnp.transpose(values, (1, 0, 2))
    (state, out, fed_grad, edge_grad, early, second, first, g_expand, g_reduce, _, _) = run(
        (vec, nodes, by_slots(edges), neighbours.T, message_first, message_second, message_third, expand_weight,
         reduce_weight, edge_first.T, edge_second, edge_third, cot_nodes, by_slots(cot_edges))
    )
    got = unpack((early, second, first), width, hidden, features, inner)
    got = [g[0] if g.shape[0] == 1 else g for g in got]
    got[12] = got[12].T
    return (state, by_slots(out), fed_grad, by_slots(edge_grad)) + tuple(got[:8]) + (g_expand, got[8], g_reduce) + tuple(got[9:])


def solution(mesh):
    rows, slots = P("res", None), P("res", None, None)
    copied = P()
    down, vec = P("half", None), P("half")
    return jax.shard_map(
        body,
        mesh=mesh,
        in_specs=(rows, slots, rows, P("res")) + (copied,) * 22 + (rows, slots),
        out_specs=(
            P("res", "half"),
            P("res", "half", None),
            P("res", "half"),
            P("res", "half", None),
            down, vec, down, vec, down, vec, vec, vec, down, vec, down, vec, vec, vec,
            down, vec, down, vec, down, vec, vec, vec,
        ),
        check_vma=False,
    )
```

```python
import functools
import types
from typing import Any, NamedTuple

import jax
import jax.numpy as jnp
from jax import lax
from jax.experimental import pallas as pl
from jax.experimental.pallas import tpu as pltpu
from jax.sharding import PartitionSpec as P

EPSILON = 1e-05
REACH = 64
CORES = 2
NEAR = 0.7978845608
CUBE = 0.044715
STEP = 30
CHAIN = 5
BACK_CHAIN = 15
EDGE_CHAIN = 15
EARLY_WIDE = 6
PARTS = 2
LANES = 256
LANE = 128
WIDE = 256
VMEM = 62 * 2**20
MESH = pl.DeviceIdType.MESH
F32 = jnp.float32
BF16 = jnp.bfloat16


def dot(left, right):
    return jnp.dot(left, right, preferred_element_type=F32)


def dot_t(left, right):
    return lax.dot_general(left, right, (((1,), (1,)), ((), ())), preferred_element_type=F32)


def t_dot(left, right):
    return lax.dot_general(left, right, (((0,), (0,)), ((), ())), preferred_element_type=F32)


def two_parts(values):
    high = values.astype(BF16)
    return high, (values - high.astype(F32)).astype(BF16)


def dot_wide(values, right, transposed=False):
    rows = values.shape[0]
    both = (dot_t if transposed else dot)(jnp.concatenate(two_parts(values), 0), right)
    return both[:rows] + both[rows:]


def gelu(values):
    square = values * values
    bend = jnp.tanh(values * (NEAR + (NEAR * CUBE) * square))
    return values * (0.5 + 0.5 * bend)


def gelu_slope(values):
    square = values * values
    part = 0.5 + 0.5 * jnp.tanh(values * (NEAR + (NEAR * CUBE) * square))
    return part + values * part * (1.0 - part) * (2.0 * NEAR + (6.0 * NEAR * CUBE) * square)


def gelu_and_slope(values):
    values = values.astype(BF16)
    square = values * values
    part = BF16(0.5) + BF16(0.5) * jnp.tanh(values * (BF16(NEAR) + BF16(NEAR * CUBE) * square))
    act = values * part
    slope = part + act * (1 - part) * (BF16(2.0 * NEAR) + BF16(6.0 * NEAR * CUBE) * square)
    return act, slope


def norm_parts(values):
    centered = values - jnp.mean(values, -1, keepdims=True)
    scale = lax.rsqrt(jnp.mean(centered * centered, -1, keepdims=True) + EPSILON)
    return centered * scale, scale


def norm_back(grad, unit, scale, gain):
    scaled = gain * grad
    flat = jnp.mean(scaled, -1, keepdims=True)
    slant = jnp.mean(scaled * unit, -1, keepdims=True)
    return (scaled - flat - unit * slant) * scale


def col_sum(values):
    return jnp.sum(values, 0, keepdims=True)


def iota(dims, axis):
    return lax.broadcasted_iota(jnp.int32, dims, axis)


def chip_dims(count):
    side = 1
    while 2 * (2 * side) ** 3 <= count and count % (4 * side * side) == 0:
        side *= 2
    return side, count // (side * side)


def up(size, unit):
    return -(-size // unit) * unit


class Chunks(NamedTuple):
    edge: Any
    third: Any
    first_a: Any
    first_b: Any
    second: Any


ORDERS = Chunks((0, 2, 1), (0, 1, 2), (2, 0, 1), (0, 1, 2), (0, 2, 1))


def chunk_rows(count, width, hidden, features):
    tall = (2 * width + features) // CORES
    wide = width // LANE
    edge = features * (up(tall, LANE) // LANE) + 3 * (features // CORES)
    square = (hidden // CORES) * wide
    first = tall * (wide // 2)
    sizes = (edge, square, first, first + 16 * wide, square)
    return Chunks(*(up(rows, 16 * count) for rows in sizes))


def cut(pieces, start, stop):
    at, got = 0, []
    for piece in pieces:
        low, high = max(start, at), min(stop, at + piece.shape[0])
        if low < high:
            got.append(piece[low - at : high - at])
        at += piece.shape[0]
    return jnp.concatenate(got, 0) if len(got) > 1 else got[0]


def put_wide(pack, half, at, piece):
    rows = piece.shape[0]
    for block in range(piece.shape[1] // LANE):
        pack[half, pl.ds(at, rows), :] = piece[:, block * LANE : (block + 1) * LANE].astype(BF16)
        at += rows
    return at


def put_rest(pack, at):
    rest = pack.shape[1] - at
    if rest:
        for half in range(CORES):
            pack[half, pl.ds(at, rest), :] = jnp.zeros((rest, LANE), BF16)


def take_wide(packed, at, rows, blocks):
    pieces = [packed[pl.ds(at + b * rows, rows), :] for b in range(blocks)]
    return jnp.concatenate(pieces, 1).astype(F32), at + blocks * rows


class Copies:
    def __init__(self, send, recv):
        self.send, self.recv, self.used = send, recv, 0

    def group(self, entries):
        made = []
        for source, target, device in entries:
            at = self.used
            self.used += 1
            made.append(functools.partial(self._make, source, target, device, at))
        return Group(made)

    def _make(self, source, target, device, at):
        return pltpu.make_async_remote_copy(
            src_ref=source,
            dst_ref=target,
            send_sem=self.send.at[at],
            recv_sem=self.recv.at[at],
            device_id=device,
            device_id_type=MESH,
        )


class Group:
    def __init__(self, made):
        self.made = made

    def start(self):
        for make in self.made:
            make().start()

    def wait(self):
        for make in self.made:
            make().wait()


class Place:
    def __init__(self):
        res, half, count = lax.axis_index("res"), lax.axis_index("half"), lax.axis_size("res")
        side, deep = chip_dims(count)
        x, y, z = lax.rem(res, side), lax.rem(res // side, side), res // (side * side)
        first = half == 0
        self.res, self.half, self.count = res, half, count
        self.dims = (side, side, deep)
        self.at = (jnp.where(first, x, y), jnp.where(first, y, x), z)
        self.strides = (jnp.where(first, 1, side), jnp.where(first, side, 1), side * side)
        self.partner = (res, 1 - half)

    def peers(self, level):
        size, here = self.dims[level], self.at[level]
        found = []
        for ahead in range(1, size):
            to = lax.rem(here + ahead, size)
            found.append((to, (self.res + (to - here) * self.strides[level], self.half)))
        return found

    def line(self):
        res, half, count = self.res, self.half, self.count
        return (
            (res > 0, (res - 1, half)),
            (res + half > 0, (res - 1 + half, 1 - half)),
            (res + half < count, (res + half, 1 - half)),
            (res < count - 1, (res + 1, half)),
        )

    def line_count(self):
        res, half, count = self.res, self.half, self.count
        return 4 - jnp.where(res > 0, 0, 2 - half) - jnp.where(res < count - 1, 0, 1 + half)


def greet(place):
    barrier = pltpu.get_barrier_semaphore()

    def signal(device):
        pl.semaphore_signal(barrier, inc=1, device_id=device, device_id_type=MESH)

    for exists, device in place.line():
        pl.when(exists)(functools.partial(signal, device))
    signal(place.partner)
    others = 1
    for level in range(3):
        for _, device in place.peers(level):
            signal(device)
            others += 1
    pl.semaphore_wait(barrier, others + place.line_count())


def halo_layout(rows):
    edge = REACH - rows
    return ((0, edge), (edge, rows), (REACH + rows, rows), (REACH + 2 * rows, edge))


class Halo:
    def __init__(self, place, window, rows, send, recv, first):
        self.place, self.window, self.rows = place, window, rows
        self.send, self.recv, self.first = send, recv, first

    def clear(self):
        for (exists, _), (offset, size) in zip(self.place.line(), halo_layout(self.rows)):

            @pl.when(jnp.logical_not(exists))
            def _():
                self.window[pl.ds(offset, size), :] = jnp.zeros((size, self.window.shape[1]), self.window.dtype)

    def _copy(self, at, device):
        offset, size = halo_layout(self.rows)[3 - at]
        first = REACH + (self.rows - size if at == 3 else 0)
        return pltpu.make_async_remote_copy(
            src_ref=self.window.at[pl.ds(first, size)],
            dst_ref=self.window.at[pl.ds(offset, size)],
            send_sem=self.send.at[self.first + at],
            recv_sem=self.recv.at[self.first + 3 - at],
            device_id=device,
            device_id_type=MESH,
        )

    def start(self):
        for at, (exists, device) in enumerate(self.place.line()):

            @pl.when(exists)
            def _():
                self._copy(at, device).start()

    def wait(self):
        for at, (exists, device) in enumerate(self.place.line()):
            offset, size = halo_layout(self.rows)[at]

            @pl.when(exists)
            def _():
                self._copy(at, device).wait_send()
                pltpu.make_async_remote_copy(
                    src_ref=self.window.at[pl.ds(offset, size)],
                    dst_ref=self.window.at[pl.ds(offset, size)],
                    send_sem=self.send.at[self.first + at],
                    recv_sem=self.recv.at[self.first + at],
                    device_id=device,
                    device_id_type=MESH,
                ).wait_recv()


class Returns:
    def __init__(self, place, table, landing, rows, send, recv, first):
        self.place, self.table, self.landing, self.rows = place, table, landing, rows
        self.send, self.recv, self.first = send, recv, first

    def _copy(self, at, device):
        layout = halo_layout(self.rows)
        offset, size = layout[at]
        return pltpu.make_async_remote_copy(
            src_ref=self.table.at[pl.ds(offset, size)],
            dst_ref=self.landing.at[pl.ds(layout[3 - at][0], size)],
            send_sem=self.send.at[self.first + at],
            recv_sem=self.recv.at[self.first + 3 - at],
            device_id=device,
            device_id_type=MESH,
        )

    def start(self):
        for at, (exists, device) in enumerate(self.place.line()):

            @pl.when(exists)
            def _():
                self._copy(at, device).start()

    def finish(self, total):
        total[...] = self.table[pl.ds(REACH, self.rows), :]
        for at, (exists, device) in enumerate(self.place.line()):
            offset, size = halo_layout(self.rows)[at]
            first = self.rows - size if at == 3 else 0

            @pl.when(exists)
            def _():
                self._copy(at, device).wait_send()
                pltpu.make_async_remote_copy(
                    src_ref=self.table.at[pl.ds(offset, size)],
                    dst_ref=self.landing.at[pl.ds(offset, size)],
                    send_sem=self.send.at[self.first + at],
                    recv_sem=self.recv.at[self.first + at],
                    device_id=device,
                    device_id_type=MESH,
                ).wait_recv()
                total[pl.ds(first, size), :] += self.landing[pl.ds(offset, size), :]


def gather_groups(place, copies, ref, unit, source=None, base=0):
    mine = (place.at[0] * place.dims[1] + place.at[1]) * place.dims[2] + place.at[2]
    groups, size = [], unit
    start = mine * unit
    for level in (2, 1, 0):
        here = ref.at[pl.ds(pl.multiple_of(base + start, 16), size)]
        from_ref = here if source is None or level < 2 else source
        groups.append(copies.group([(from_ref, here, device) for _, device in place.peers(level)]))
        start = start - place.at[level] * size
        size = size * place.dims[level]
    return groups


class ChipSum:
    def __init__(self, place, copies, order, pack, got, landed, gathered):
        self.place, self.pack, self.got, self.landed, self.gathered = place, pack, got, landed, gathered
        half, size = place.half, pack.shape[1]
        self.pair = copies.group([(pack.at[1 - half], got, place.partner)])
        self.steps, self.shares, self.back = [], [], []
        start, base = 0, 0
        for level in order:
            share = size // place.dims[level]
            entries, lands = [], []
            for to, device in place.peers(level):
                source = pack.at[half, pl.ds(pl.multiple_of(start + to * share, 16), share)]
                entries.append((source, landed.at[pl.ds(base, share)], device))
                lands.append(base)
                base += share
            start = pl.multiple_of(start + place.at[level] * share, 16)
            size = share
            self.steps.append(copies.group(entries))
            self.shares.append((start, share, lands))
            here = gathered.at[pl.ds(start, share)]
            back = [(here, here, device) for _, device in place.peers(level)]
            self.back.insert(0, copies.group(back))

    def send_pair(self):
        self.pair.start()

    def add_pair(self):
        self.pair.wait()
        half = self.place.half
        self.pack[half] = (self.pack[half].astype(F32) + self.got[...].astype(F32)).astype(BF16)

    def start(self, level):
        self.steps[level].start()

    def finish(self, level):
        self.steps[level].wait()
        start, share, lands = self.shares[level]
        half = self.place.half
        total = self.pack[half, pl.ds(start, share), :].astype(F32)
        for base in lands:
            total = total + self.landed[pl.ds(base, share), :].astype(F32)
        if level < len(self.steps) - 1:
            self.pack[half, pl.ds(start, share), :] = total.astype(BF16)
        else:
            self.gathered[pl.ds(start, share), :] = total.astype(BF16)

    def start_back(self, step):
        self.back[step].start()

    def finish_back(self, step):
        self.back[step].wait()


def flat(values):
    return values.reshape(values.shape[0] * values.shape[1], values.shape[2])


def feed_forward(r, pooled, own):
    width = own.shape[1]
    mean = pooled / r.counts[:, 0:1]
    summed = own + dot_wide(mean, r.third[...]) + r.b_three
    unit, _ = norm_parts(summed)
    normed = unit * r.gain_one + r.shift_one
    low = normed.astype(BF16)
    pre = dot(low, r.expand[...]) + r.b_expand
    second = normed + dot(gelu(pre).astype(BF16), r.reduce[...]) + r.b_reduce
    unit_two, _ = norm_parts(second)
    r.summed[...] = summed
    r.pre_expand[...] = pre
    r.second[...] = second
    r.normed[...] = low
    return unit_two * r.gain_two + r.shift_two


def fill_table(window, far, own, bias, table, rows, multiply):
    places = window.shape[0]
    table[pl.ds(0, places), :] = multiply(window[...], far).astype(BF16)
    table[pl.ds(places, rows), :] = (multiply(window[pl.ds(REACH, rows), :], own) + bias).astype(BF16)


def chain_parts(step):
    return [step * STEP + part * CHAIN for part in range(STEP // CHAIN)]


def chain_rows(r, slot):
    rows = r.counts.shape[0]
    return pl.ds(pl.multiple_of(slot * rows, CHAIN * rows), CHAIN * rows)


def step_rows(r, step):
    rows = r.counts.shape[0]
    return pl.ds(pl.multiple_of(step * (STEP * rows), STEP * rows), STEP * rows)


def build_block(r, step, half, places):
    rows = r.counts.shape[0]
    here = pl.ds(step * STEP, STEP)
    named = r.picks[here]
    dims = (STEP, rows, named.shape[2])
    spread = jnp.broadcast_to(named, dims)
    mine = iota(dims, 2) == iota(dims, 1) + half * rows
    pick = jnp.sum(jnp.where(mine, spread, 0.0), -1, keepdims=True)
    dims = (STEP, rows, LANES)
    lane = iota(dims, 2)
    hit = (lane.astype(F32) == pick) | (lane == iota(dims, 1) + places)
    r.onehot[here] = jnp.where(hit, 1.0, 0.0).astype(BF16)


def joined_rows(r, slot, slots):
    here = pl.ds(slot, slots)
    return jnp.concatenate([flat(r.onehot[here]), flat(r.edges_raw[here])], 1)


def live_rows(r, slot, width):
    count = r.counts[...]
    dims = (CHAIN,) + count.shape
    live = jnp.where(iota(dims, 0) + slot < count[None], 1.0, 0.0)
    return flat(jnp.concatenate([live] * (width // LANE), -1))


def live_column(r, slot, slots):
    count = r.counts[...]
    dims = (slots,) + count.shape
    return flat(jnp.where(iota(dims, 0) + slot < count[None], 1.0, 0.0))[:, 0:1]


def node_block(r, step, keep):
    rows = r.counts.shape[0]
    hidden = r.second_w.shape[0]
    slots = chain_parts(step)
    dims = (rows, CHAIN * rows)
    count = jnp.broadcast_to(r.counts[:, 0:1], dims)
    pre = [dot(joined_rows(r, slot, CHAIN), r.table[...]) for slot in slots]
    acts = []
    for slot, values in zip(slots, pre):
        if keep:
            here = chain_rows(r, slot)
            act, slope = gelu_and_slope(values)
            r.act[here, :] = act
            r.slope_one[here, :] = slope
        else:
            act = gelu(values).astype(BF16)
        acts.append(act)
    pre = [dot(act, r.second_w[...]) + r.b_two for act in acts]
    total = r.pooled[...]
    for slot, values in zip(slots, pre):
        if keep:
            act, slope = gelu_and_slope(values)
            r.slope_two[chain_rows(r, slot), :] = slope * live_rows(r, slot, hidden).astype(BF16)
        else:
            act = gelu(values)
        used = jnp.where(r.lane_slot[0:1, :] + slot.astype(F32) < count, r.diagonal[...], 0.0)
        total = total + dot(used.astype(BF16), act.astype(BF16))
    r.pooled[...] = total


def edge_block(r, step, features):
    rows = r.counts.shape[0]
    split = lambda values: values.reshape(values.shape[0] // rows, rows, features)
    slots = [step * STEP + part * EDGE_CHAIN for part in range(STEP // EDGE_CHAIN)]
    each = lambda body, *lists: [body(*items) for items in zip(*lists)]
    joined = [joined_rows(r, slot, EDGE_CHAIN) for slot in slots]
    live = [live_column(r, slot, EDGE_CHAIN) for slot in slots]
    pre = each(lambda z: dot(z, r.e_table[...]), joined)
    o_one, slope_one = zip(*each(gelu_and_slope, pre))
    pre = each(lambda a: dot(a, r.e_second_w[...]) + r.eb_two, o_one)
    o_two, slope_two = zip(*each(gelu_and_slope, pre))
    summed = each(lambda z, a: z[:, LANES:].astype(F32) + (dot(a, r.e_third_w[...]) + r.eb_three), joined, o_two)
    unit, scale = zip(*each(norm_parts, summed))
    d_three, d_sums = [], []
    for slot, u, k, used in zip(slots, unit, scale, live):
        here = pl.ds(slot, EDGE_CHAIN)
        r.edge_out[here] = split((u * r.e_gain + r.e_shift) * used).astype(BF16)
        d_out = flat(r.cots_raw[here]).astype(F32) * used
        r.ge_norm[0:1, :] += col_sum(d_out * u)
        r.ge_norm[1:2, :] += col_sum(d_out)
        d_sum = norm_back(d_out, u, k, r.e_gain)
        r.ge_norm[2:3, :] += col_sum(d_sum)
        d_sums.append(d_sum)
        d_three.append(d_sum.astype(BF16))
    d_two = each(lambda d, k: dot_t(d, r.e_third_w[...]) * k, d_three, slope_two)
    r.ge_norm[3:4, :] += sum(col_sum(d) for d in d_two)
    d_two = each(lambda d: d.astype(BF16), d_two)
    d_one = each(lambda d, k: (dot_t(d, r.e_second_w[...]) * k).astype(BF16), d_two, slope_one)
    for slot, d_sum, d in zip(slots, d_sums, d_one):
        more = dot(d, r.e_first_t[:, pl.ds(2 * r.nodes_width, features)])
        r.edge_grad[pl.ds(slot, EDGE_CHAIN)] = split(d_sum + more)
    together = lambda values: jnp.concatenate(values, 0)
    r.ge_third[...] += t_dot(together(o_two), together(d_three))
    r.ge_second[...] += t_dot(together(o_one), together(d_two))
    r.ge_first[...] += t_dot(together(joined), together(d_one))


def node_grad(r, cot, far_total, when_ds):
    width = cot.shape[1]
    grad = cot.astype(F32) + r.e_own_back[...] + dot_wide(far_total, r.e_first_t[:, pl.ds(width, width)])
    unit, scale = norm_parts(r.second[...])
    dw = norm_back(grad, unit, scale, r.gain_two)
    gain_two, shift_two = col_sum(grad * unit), col_sum(grad)
    ds = dw.astype(BF16)
    r.ds[...] = ds
    when_ds()
    slope = gelu_slope(r.pre_expand[...])
    dq = (dot_t(ds, r.reduce[...]) * slope).astype(BF16)
    dv = dw + dot_t(dq, r.expand[...])
    unit, scale = norm_parts(r.summed[...])
    du = norm_back(dv, unit, scale, r.gain_one)
    r.du[...] = du
    counts = r.counts[:, 0:1]
    dm = (du / counts).astype(BF16)
    r.slot_grad[...] = dot_t(dm, r.third[...])
    r.dm[...] = dm
    small = r.small
    small[...] = jnp.zeros(small.shape, F32)
    small[2:3, :] = col_sum(counts * dm.astype(F32))
    small[3:4, :] = col_sum(dv * unit)
    small[4:5, :] = col_sum(dv)
    dq_sum = col_sum(dq.astype(F32))
    for part in range(dq_sum.shape[1] // width):
        small[5 + part : 6 + part, :] = dq_sum[:, part * width : (part + 1) * width]
    small[9:10, :] = col_sum(ds.astype(F32))
    small[10:11, :] = gain_two
    small[11:12, :] = shift_two


def put_features(pack, half, at, e_second, e_third):
    part = e_second.shape[0] // CORES
    two = [ref[pl.ds(half * part, part), :] for ref in (e_second, e_third)]
    for piece in two:
        at = put_wide(pack, half, at, piece[:, :LANE])
    return put_wide(pack, half, at, jnp.concatenate([piece[:, LANE:] for piece in two], 1))


def pack_edge(r, pack):
    features = r.ge_second.shape[0]
    g_edge = jnp.transpose(r.ge_first[pl.ds(LANES, features), :])
    e_first = jnp.concatenate([r.ge_own[...], r.ge_far[...], g_edge], 1)
    tall = e_first.shape[1] // CORES
    fill = jnp.zeros((features, up(tall, LANE) - tall), F32)
    for half in range(CORES):
        piece = jnp.concatenate([e_first[:, half * tall : (half + 1) * tall], fill], 1)
        at = put_wide(pack, half, 0, piece)
        at = put_features(pack, half, at, r.ge_second, r.ge_third)
    put_rest(pack, at)


def pack_third(r, pack):
    dm = r.dm[...]
    found = t_dot(jnp.concatenate(two_parts(r.pooled[...]), 0), jnp.concatenate([dm, dm], 0))
    part = found.shape[0] // CORES
    for half in range(CORES):
        at = put_wide(pack, half, 0, found[half * part : (half + 1) * part])
    put_rest(pack, at)


def pack_second(r, pack):
    part = r.g_second.shape[0] // CORES
    for half in range(CORES):
        at = put_wide(pack, half, 0, r.g_second[pl.ds(half * part, part), :])
    put_rest(pack, at)


def small_rows(r, places):
    rows = r.counts.shape[0]
    features = r.ge_norm.shape[1]
    fill = jnp.zeros((1, LANES - features), F32)
    own = pl.ds(places, rows)
    edge = [col_sum(r.ge_first[own, :])] + [r.ge_norm[at : at + 1, :] for at in (3, 2, 0, 1)]
    edge = [jnp.concatenate([row, fill], 1) for row in edge] + [jnp.zeros((1, LANES), F32)]
    lines = [col_sum(r.g_first[own, :]), r.g_bias[...], r.small[2:12, :]]
    lines += [jnp.concatenate(edge[at : at + 2], 1) for at in (0, 2, 4)]
    return jnp.concatenate(lines + [jnp.zeros((1, r.small.shape[1]), F32)], 0)


def pack_first(r, packs, g_own, g_far, features, small):
    pieces = [g_own, g_far, r.g_first[pl.ds(LANES, features), :]]
    tall = sum(piece.shape[0] for piece in pieces) // CORES
    hidden = g_own.shape[1]
    for side, pack in enumerate(packs):
        cols = slice(side * (hidden // 2), (side + 1) * (hidden // 2))
        for half in range(CORES):
            at = put_wide(pack, half, 0, cut([piece[:, cols] for piece in pieces], half * tall, (half + 1) * tall))
            if side == 1:
                at = put_wide(pack, half, at, small)
        put_rest(pack, at)


def first_grad_block(r, step, features):
    rows = r.counts.shape[0]
    hidden = r.act.shape[1]
    coming = jnp.broadcast_to(r.slot_grad[...][None], (BACK_CHAIN,) + r.slot_grad.shape)
    slots = [step * STEP + part * BACK_CHAIN for part in range(STEP // BACK_CHAIN)]
    places = [pl.ds(pl.multiple_of(slot * rows, BACK_CHAIN * rows), BACK_CHAIN * rows) for slot in slots]
    twos, ones = [], []
    for here in places:
        d_two = flat(coming) * r.slope_two[here, :].astype(F32)
        r.g_bias[...] += col_sum(d_two)
        twos.append(d_two.astype(BF16))
        r.slope_two[here, :] = twos[-1]
    backs = [dot_t(d_two, r.second_w[...]) for d_two in twos]
    for here, back in zip(places, backs):
        ones.append((back * r.slope_one[here, :].astype(F32)).astype(BF16))
        r.slope_one[here, :] = ones[-1]
    r.g_first[...] += t_dot(joined_rows(r, step * STEP, STEP), jnp.concatenate(ones, 0))


def second_grad_block(r, step, features):
    rows = r.counts.shape[0]
    here = step_rows(r, step)
    r.g_second[...] += t_dot(r.act[here, :], r.slope_two[here, :])
    more = dot_t(r.slope_one[here, :], r.table[pl.ds(LANES, features), :])
    r.edge_grad[pl.ds(step * STEP, STEP)] += more.reshape(STEP, rows, features)


class WideBlock:
    def __init__(self, r, step, half):
        width, inner = r.expand.shape
        blocks = inner // WIDE
        self.r, self.step, self.mine = r, step, blocks // CORES
        self.block = lax.rem(step + half * self.mine, blocks)
        self.here = pl.ds(pl.multiple_of(self.block * WIDE, WIDE), WIDE)
        part = width // CORES
        self.cols = pl.ds(pl.multiple_of(half * part, part), part)
        self.total = r.normed_all.shape[0]
        size = self.total // PARTS
        self.rows = [pl.ds(at * size, size) for at in range(PARTS)]

    def forward(self):
        r = self.r
        bias = r.bias_wide[pl.ds(self.block, 1), :]
        pre = [dot(r.normed_all[rows, :], r.expand[:, self.here]) + bias for rows in self.rows]
        both = [gelu_and_slope(values) for values in pre]
        return [act for act, _ in both], [slope for _, slope in both]

    def place(self, slot, rows=None):
        size = self.total if rows is None else rows.size
        first = (slot // 2) * self.total + (0 if rows is None else rows.start)
        return self.r.kept.at[
            pl.ds(pl.multiple_of(first, 16), size), pl.ds(pl.multiple_of(lax.rem(slot, 2) * WIDE, WIDE), WIDE)
        ]

    def keep(self):
        acts, slopes = self.forward()
        for rows, slope in zip(self.rows, slopes):
            self.place(self.step, rows)[...] = slope

        @pl.when(self.step < self.mine)
        def _():
            for rows, act in zip(self.rows, acts):
                self.place(EARLY_WIDE + self.step, rows)[...] = act

    def backward(self, slopes, act, fresh):
        r = self.r
        back = [dot_t(r.ds_all[rows, :], r.reduce[self.here, :]) for rows in self.rows]
        dqs = [(grad * slope.astype(F32)).astype(BF16) for grad, slope in zip(back, slopes)]
        found = t_dot(r.normed_all[:, self.cols], jnp.concatenate(dqs, 0))
        r.g_expand[:, self.here] = found if fresh else r.g_expand[:, self.here] + found

        @pl.when(self.step < self.mine)
        def _():
            out = pl.ds(pl.multiple_of(self.step * WIDE, WIDE), WIDE)
            found = t_dot(act(), r.ds_all[...])
            r.g_reduce[out, :] = found if fresh else r.g_reduce[out, :] + found

    def from_kept(self):
        slopes = [self.place(self.step, rows)[...] for rows in self.rows]
        self.backward(slopes, lambda: self.place(EARLY_WIDE + self.step)[...], True)

    def whole(self, fresh):
        acts, slopes = self.forward()
        self.backward(slopes, lambda: jnp.concatenate(acts, 0), fresh)


class Vectors(NamedTuple):
    b_one: Any
    b_two: Any
    b_three: Any
    gain_one: Any
    shift_one: Any
    b_reduce: Any
    gain_two: Any
    shift_two: Any
    b_expand: Any
    eb_one: Any
    eb_two: Any
    eb_three: Any
    e_gain: Any
    e_shift: Any
    counts_in: Any


class Arrays(NamedTuple):
    nodes: Any
    edges: Any
    neighbours: Any
    first_in: Any
    second_in: Any
    third_in: Any
    expand_in: Any
    reduce_in: Any
    e_first_in: Any
    e_second_in: Any
    e_third_in: Any
    cot_nodes: Any
    cot_edges: Any


class Results(NamedTuple):
    state_out: Any
    edges_out: Any
    fed_out: Any
    grads_out: Any
    expand_out: Any
    reduce_out: Any
    normed_slots: Any
    ds_slots: Any


def kernel(names, features, *refs):
    kinds, refs = (Vectors, Arrays, Results), list(refs)
    r = types.SimpleNamespace()
    for kind in kinds:
        for name in kind._fields:
            setattr(r, name, refs.pop(0))
    r.sums_out = Chunks(*(refs.pop(0) for _ in Chunks._fields))
    for name in names:
        setattr(r, name, refs.pop(0))
    r.pack, r.got, r.landed, r.gathered = (Chunks(*(refs.pop(0) for _ in Chunks._fields)) for _ in range(4))
    place = Place()
    res, half, count = place.res, place.half, place.count
    rows_dev, width = r.nodes.shape
    rows = rows_dev // CORES
    places = rows + 2 * REACH
    slots = r.edges.shape[0]
    each = slots // CORES
    steps = slots // STEP
    r.nodes_width = width
    total = r.edges_raw.shape[0] * rows
    r.act, r.slope_one, r.slope_two = (r.kept.at[pl.ds(at * total, total)] for at in range(3))
    for name in Vectors._fields:
        vector = getattr(r, name)
        setattr(r, name, vector[...].astype(F32).reshape(1, vector.shape[0]))
    own = pl.ds(REACH, rows)
    mine = pl.ds(pl.multiple_of(half * rows, 16), rows)

    pairs = dict(
        nodes=(r.nodes.at[mine], r.windows.at[0, own]),
        neighbours=(r.neighbours, r.neighbours_raw),
        first=(r.first_in, r.first),
        edges=(r.edges.at[:, mine, :], r.edges_raw),
        second=(r.second_in, r.second_w),
        e_first=(r.e_first_in, r.e_first_t),
        e_second=(r.e_second_in, r.e_second_w),
        e_third=(r.e_third_in, r.e_third_w),
        third=(r.third_in, r.third),
        expand=(r.expand_in, r.expand),
        reduce=(r.reduce_in, r.reduce),
        cot_edges=(r.cot_edges.at[:, mine, :], r.cots_raw),
        cot_nodes=(r.cot_nodes.at[mine], r.cot_rows),
    )
    loads = types.SimpleNamespace()
    for at, (name, pair) in enumerate(pairs.items()):
        copy = pltpu.make_async_copy(*pair, r.load_sem.at[at])
        setattr(loads, name, copy)
        copy.start()

    halos = [
        Halo(place, r.windows.at[k], rows, r.line_send, r.line_recv, 4 * k) for k in range(3)
    ]
    edge_returns = Returns(place, r.ge_first, r.edge_landing, rows, r.line_send, r.line_recv, 12)
    node_returns = Returns(place, r.g_first, r.node_landing, rows, r.line_send, r.line_recv, 16)
    copies = Copies(r.step_send, r.step_recv)
    edge, third, first_a, first_b, second = sums = Chunks(
        *(ChipSum(place, copies, *parts) for parts in zip(ORDERS, r.pack, r.got, r.landed, r.gathered))
    )
    span = count * rows

    def row_gather(source, slot_ref):
        base = half * span
        groups = gather_groups(place, copies, slot_ref, rows, source, base)
        here = slot_ref.at[pl.ds(pl.multiple_of(base, 16), span)]
        groups.append(copies.group([(here, here, place.partner)]))
        return groups

    normed_gather = row_gather(r.normed, r.normed_slots)
    ds_gather = row_gather(r.ds, r.ds_slots)
    my_unit = (place.at[0] * place.dims[1] + place.at[1]) * place.dims[2] + place.at[2]
    my_slot = pl.ds(pl.multiple_of(half * span + my_unit * rows, 16), rows)
    normed_keep = pltpu.make_async_copy(r.normed, r.normed_slots.at[my_slot], r.keep_sem.at[0])
    ds_keep = pltpu.make_async_copy(r.ds, r.ds_slots.at[my_slot], r.keep_sem.at[1])
    there = pl.ds(pl.multiple_of(half * rows, 16), rows)
    my_slots = pl.ds(half * each, each)
    its_slots = pl.ds((1 - half) * each, each)
    edges_target = r.edges_out.at[:, there, :]
    edges_pair = copies.group([(r.edge_out.at[its_slots], edges_target, place.partner)])
    edges_keep = pltpu.make_async_copy(r.edge_out.at[my_slots], edges_target, r.keep_sem.at[2])
    grads_target = r.grads_out.at[:, there, :]
    grads_pair = copies.group([(r.edge_grad.at[its_slots], grads_target, place.partner)])
    grads_keep = pltpu.make_async_copy(r.edge_grad.at[my_slots], grads_target, r.keep_sem.at[3])
    fed_pair = copies.group([(r.fed_grad.at[1 - half], r.fed_out.at[there], place.partner)])
    fed_keep = pltpu.make_async_copy(r.fed_grad.at[half], r.fed_out.at[there], r.keep_sem.at[4])

    greet(place)
    loads.nodes.wait()
    halos[0].start()
    for halo in halos:
        halo.clear()
    dims = (rows, LANE)
    counted = jnp.broadcast_to(r.counts_in, (rows, rows_dev))
    here = iota(counted.shape, 1) == iota(counted.shape, 0) + half * rows
    r.counts[...] = jnp.broadcast_to(jnp.sum(jnp.where(here, counted, 0.0), -1, keepdims=True), dims)
    for block in range(r.expand.shape[1] // WIDE):
        r.bias_wide[block : block + 1, :] = r.b_expand[:, block * WIDE : (block + 1) * WIDE]
    dims = (rows, CHAIN * rows)
    lane = iota(dims, 1)
    r.diagonal[...] = jnp.where(lax.rem(lane, rows) == iota(dims, 0), 1.0, 0.0)
    r.lane_slot[...] = (iota(r.lane_slot.shape, 1) // rows).astype(F32)
    loads.neighbours.wait()
    base = res * rows_dev + half * rows - REACH
    named = (r.neighbours_raw[...] - base).astype(F32)
    r.picks[...] = named.reshape(slots, 1, rows_dev)

    def build(step, carry):
        build_block(r, step, half, places)
        return carry

    lax.fori_loop(0, steps, build, 0)
    for table in (r.table, r.e_table):
        rest = LANES - places - rows
        if rest:
            table[pl.ds(places + rows, rest), :] = jnp.zeros((rest, table.shape[1]), BF16)
    for load in (loads.first, loads.e_first, loads.e_second, loads.e_third):
        load.wait()
    r.table[pl.ds(LANES, features), :] = r.first[pl.ds(2 * width, features), :]
    edge_part = r.e_first_t[:, pl.ds(2 * width, features)]
    r.e_table[pl.ds(LANES, features), :] = jnp.transpose(edge_part.astype(F32)).astype(BF16)
    loads.edges.wait()
    bias = r.b_one
    far_w, own_w = r.first[pl.ds(width, width), :], r.first[pl.ds(0, width), :]
    halos[0].wait()
    fill_table(r.windows.at[0], far_w, own_w, bias, r.table, rows, dot)
    r.pooled[...] = jnp.zeros(r.pooled.shape, F32)
    loads.second.wait()

    def first_pass(step, carry):
        node_block(r, step, False)
        return carry

    lax.fori_loop(0, steps, first_pass, 0)
    loads.third.wait()
    loads.expand.wait()
    loads.reduce.wait()
    r.windows[1, own, :] = feed_forward(r, r.pooled[...], r.windows[0, own, :].astype(F32)).astype(BF16)

    halos[1].start()
    loads.cot_edges.wait()
    loads.cot_nodes.wait()
    halos[1].wait()
    fill_table(r.windows.at[1], far_w, own_w, bias, r.table, rows, dot)
    r.pooled[...] = jnp.zeros(r.pooled.shape, F32)

    def second_pass(step, carry):
        node_block(r, step, True)
        return carry

    lax.fori_loop(0, steps, second_pass, 0)
    r.windows[2, own, :] = feed_forward(r, r.pooled[...], r.windows[1, own, :].astype(F32)).astype(BF16)

    halos[2].start()
    normed_keep.start()
    normed_gather[0].start()
    for ref in (r.ge_norm, r.ge_first, r.ge_second, r.ge_third, r.g_second, r.g_first, r.g_bias):
        ref[...] = jnp.zeros(ref.shape, F32)
    halos[2].wait()
    e_own, e_far = r.e_first_t[:, pl.ds(0, width)], r.e_first_t[:, pl.ds(width, width)]
    fill_table(r.windows.at[2], e_far, e_own, r.eb_one, r.e_table, rows, dot_t)
    state_keep = pltpu.make_async_copy(
        r.windows.at[
            2,
            pl.ds(pl.multiple_of(REACH - half * rows, 16), rows_dev),
            pl.ds(pl.multiple_of(half * (width // CORES), width // CORES), width // CORES),
        ],
        r.state_out,
        r.keep_sem.at[5],
    )
    state_keep.start()

    def loop(count, body, events=None):
        def one(step, carry):
            body(step)
            for when, actions in (events or {}).items():

                @pl.when(step == when)
                def _():
                    for act in actions:
                        act()

            return carry

        lax.fori_loop(0, count, one, 0)

    loop(
        steps,
        lambda step: edge_block(r, step, features),
        {0: (normed_keep.wait, normed_gather[0].wait, normed_gather[1].start)},
    )
    edge_returns.start()
    edges_keep.start()
    normed_gather[1].wait()
    normed_gather[2].start()
    own_spread = r.ge_first[pl.ds(places, rows), :]
    r.ge_own[...] = t_dot(own_spread.astype(BF16), r.windows[2, own, :])
    r.ge_far[...] = t_dot(r.ge_first[pl.ds(0, places), :].astype(BF16), r.windows[2])
    pack_edge(r, r.pack.edge)
    edge.send_pair()
    edges_pair.start()
    r.e_own_back[...] = dot_wide(own_spread, e_own)

    outs = [(r.g_expand, r.expand_out), (r.g_reduce, r.reduce_out)] + list(zip(r.gathered, r.sums_out))
    stores = [pltpu.make_async_copy(*pair, r.keep_sem.at[8 + at]) for at, pair in enumerate(outs)]
    expand_store, reduce_store = stores[:2]
    sum_stores = dict(zip(sums, stores[2:]))

    def move(chunk, at):
        if at == 0:
            chunk.add_pair()
            chunk.start(0)
        elif at < 3:
            chunk.finish(at - 1)
            chunk.start(at)
        elif at == 3:
            chunk.finish(2)
            chunk.start_back(0)
        elif at < 6:
            chunk.finish_back(at - 4)
            chunk.start_back(at - 3)
        else:
            chunk.finish_back(2)
            sum_stores[chunk].start()

    def ahead(groups, at):
        groups[at].wait()
        if at + 1 < len(groups):
            groups[at + 1].start()

    def moves(*pairs):
        for chunk, at in pairs:
            (move if isinstance(chunk, ChipSum) else ahead)(chunk, at)

    def events(*pairs):
        return (functools.partial(moves, *pairs),)

    moves((edge, 0))
    edge_returns.finish(r.edge_total)

    def send_ds():
        ds_keep.start()
        ds_gather[0].start()

    node_grad(r, r.cot_rows[...], r.edge_total[...], send_ds)
    pack_third(r, r.pack.third)
    third.send_pair()
    loop(steps, lambda step: first_grad_block(r, step, features), {0: events((third, 0))})
    node_returns.start()
    moves((normed_gather, 2))
    own_spread = r.g_first[pl.ds(places, rows), :]
    g_own = t_dot(r.windows[1, own, :], own_spread.astype(BF16))
    g_far = t_dot(r.windows[1], r.g_first[pl.ds(0, places), :].astype(BF16))
    pack_first(r, (r.pack.first_a, r.pack.first_b), g_own, g_far, features, small_rows(r, places))
    first_a.send_pair()
    first_b.send_pair()
    moves((edge, 1))
    ds_keep.wait()
    moves((ds_gather, 0))
    own_back = r.du[...] + dot_wide(own_spread, own_w, True)
    loop(steps, lambda step: second_grad_block(r, step, features), {0: events((third, 1))})
    moves((normed_gather, 3), (first_a, 0))
    pack_second(r, r.pack.second)
    second.send_pair()
    grads_keep.start()
    moves((first_b, 0))
    grads_pair.start()
    node_returns.finish(r.node_total)
    fed = own_back + dot_wide(r.node_total[...], far_w, True)
    for part in range(CORES):
        r.fed_grad[part] = fed[:, part * (width // CORES) : (part + 1) * (width // CORES)]
    fed_keep.start()
    fed_pair.start()

    blocks = r.expand.shape[1] // WIDE
    chunk = r.normed_all.shape[0]
    chunks = 2 * span // chunk
    waiting = events((second, 0), (ds_gather, 1), (edge, 2), (third, 2)), events((first_b, 1))
    until_ds = (
        (second, 1), (first_a, 1), (third, 3), (ds_gather, 2), (edge, 3), (first_b, 2), (second, 2), (first_a, 2),
        (third, 4), (edge, 4), (ds_gather, 3),
    )
    beside = {
        0: events((second, 3)),
        1: events((first_a, 3), (first_b, 3)),
        2: events((third, 5)),
        3: events((second, 4)) + (reduce_store.start,),
        4: events((first_a, 4), (edge, 5)),
        5: events((first_b, 4)),
        6: events((third, 6), (first_a, 5)),
        7: events((second, 5), (edge, 6), (first_b, 5)),
    }

    def fetch(slots, target, sem, at=0):
        return pltpu.make_async_copy(slots.at[pl.ds(at * chunk, chunk)], target, r.keep_sem.at[sem])

    if chunks == 1:
        normed_fetch = fetch(r.normed_slots, r.normed_all, 6)
        normed_fetch.start()
        normed_fetch.wait()
        loop(EARLY_WIDE, lambda step: WideBlock(r, step, half).keep(), {1: waiting[0], 4: waiting[1]})
        moves(*until_ds)
        ds_fetch = fetch(r.ds_slots, r.ds_all, 7)
        ds_fetch.start()
        ds_fetch.wait()
        loop(EARLY_WIDE, lambda step: WideBlock(r, step, half).from_kept(), beside)
        last = {at - EARLY_WIDE: actions for at, actions in beside.items() if at >= EARLY_WIDE}
        loop(blocks - EARLY_WIDE, lambda step: WideBlock(r, step + EARLY_WIDE, half).whole(True), last)
    else:
        for actions in waiting:
            for act in actions:
                act()
        moves(*until_ds)
        for at in range(chunks):
            fetches = [fetch(r.normed_slots, r.normed_all, 6, at), fetch(r.ds_slots, r.ds_all, 7, at)]
            for copy in fetches:
                copy.start()
            for copy in fetches:
                copy.wait()
            loop(blocks, lambda step: WideBlock(r, step, half).whole(at == 0))
        for actions in beside.values():
            for act in actions:
                act()
    expand_store.start()
    for group in (edges_pair, grads_pair, fed_pair):
        group.wait()
    for copy in (edges_keep, grads_keep, fed_keep, state_keep):
        copy.wait()
    moves((second, 6), (first_b, 6), (first_a, 6))
    for store in stores:
        store.wait()


def shape(dims, kind):
    return jax.ShapeDtypeStruct(dims, kind)


def run(vectors, arrays):
    count = lax.axis_size("res")
    rows_dev, width = arrays.nodes.shape
    slots, _, features = arrays.edges.shape
    hidden = arrays.second_in.shape[0]
    inner = arrays.expand_in.shape[1]
    rows = rows_dev // CORES
    places = rows + 2 * REACH
    total = rows * slots
    each = slots // CORES
    tall = arrays.first_in.shape[0]
    chunks = chunk_rows(count, width, hidden, features)
    side, deep = chip_dims(count)
    everyone = CORES * count * rows
    chunk = everyone if everyone <= 16 * rows_dev else 8 * rows_dev
    outs = (
        shape((rows_dev, width // CORES), BF16),
        shape((each, rows_dev, features), BF16),
        shape((rows_dev, width // CORES), F32),
        shape((each, rows_dev, features), F32),
        shape((width // CORES, inner), F32),
        shape((inner // CORES, width), F32),
        shape((everyone, width), BF16),
        shape((everyone, width), BF16),
    ) + tuple(shape((size, LANE), BF16) for size in chunks)
    peers = 2 * (side - 1) + deep - 1
    remote = len(chunks) * (2 * peers + 1) + 2 * (peers + 1) + 3
    scratch = dict(
        windows=((3, places, width), BF16),
        neighbours_raw=((slots, rows_dev), jnp.int32),
        picks=((slots, 1, rows_dev), F32),
        counts=((rows, LANE), F32),
        bias_wide=((inner // WIDE, WIDE), F32),
        diagonal=((rows, CHAIN * rows), F32),
        lane_slot=((8, CHAIN * rows), F32),
        first=((tall, hidden), BF16),
        second_w=((hidden, hidden), BF16),
        third=((hidden, width), BF16),
        expand=((width, inner), BF16),
        reduce=((inner, width), BF16),
        e_first_t=((features, tall), BF16),
        e_second_w=((features, features), BF16),
        e_third_w=((features, features), BF16),
        edges_raw=((slots, rows, features), BF16),
        cots_raw=((slots, rows, features), BF16),
        cot_rows=((rows, width), BF16),
        onehot=((slots, rows, LANES), BF16),
        table=((LANES + features, hidden), BF16),
        e_table=((LANES + features, features), BF16),
        kept=((3 * total, hidden), BF16),
        pooled=((rows, hidden), F32),
        summed=((rows, width), F32),
        second=((rows, width), F32),
        pre_expand=((rows, inner), F32),
        normed=((rows, width), BF16),
        edge_out=((slots, rows, features), BF16),
        edge_grad=((slots, rows, features), F32),
        ge_norm=((8, features), F32),
        ge_first=((LANES + features, features), F32),
        ge_second=((features, features), F32),
        ge_third=((features, features), F32),
        ge_own=((features, width), F32),
        ge_far=((features, width), F32),
        e_own_back=((rows, width), F32),
        edge_landing=((places, features), F32),
        edge_total=((rows, features), F32),
        ds=((rows, width), BF16),
        du=((rows, width), F32),
        dm=((rows, width), BF16),
        slot_grad=((rows, hidden), F32),
        small=((16, width), F32),
        g_second=((hidden, hidden), F32),
        g_first=((LANES + features, hidden), F32),
        g_bias=((1, hidden), F32),
        node_landing=((places, hidden), F32),
        node_total=((rows, hidden), F32),
        fed_grad=((CORES, rows, width // CORES), F32),
        normed_all=((chunk, width), BF16),
        ds_all=((chunk, width), BF16),
        g_expand=((width // CORES, inner), F32),
        g_reduce=((inner // CORES, width), F32),
    )
    packed = [(CORES, size, LANE) for size in chunks] + [(size, LANE) for size in chunks] * 3
    sems = dict(load_sem=13, keep_sem=15, line_send=20, line_recv=20, step_send=remote, step_recv=remote)
    for name, size in sems.items():
        scratch[name] = pltpu.SemaphoreType.DMA((size,))
    anywhere = pl.BlockSpec(memory_space=pl.ANY)
    return pl.pallas_call(
        functools.partial(kernel, tuple(scratch), features),
        out_shape=outs,
        in_specs=[pl.BlockSpec(memory_space=pltpu.VMEM)] * len(vectors) + [anywhere] * len(arrays),
        out_specs=(anywhere,) * len(outs),
        scratch_shapes=[pltpu.VMEM(*kind) if isinstance(kind, tuple) else kind for kind in scratch.values()]
        + [pltpu.VMEM(dims, BF16) for dims in packed],
        compiler_params=pltpu.CompilerParams(
            collective_id=1, has_side_effects=True, vmem_limit_bytes=VMEM
        ),
        name="graph_layer",
    )(*vectors, *arrays)


class Moved(NamedTuple):
    grads: Any
    expand: Any
    reduce: Any
    edges: Any
    state: Any
    fed: Any


class Grads(NamedTuple):
    third_g: Any
    e_first: Any
    e_second: Any
    e_third: Any
    second_g: Any
    first_g: Any


class Biases(NamedTuple):
    b_one: Any
    b_two: Any
    b_three: Any
    gain_one: Any
    shift_one: Any
    b_expand: Any
    b_reduce: Any
    gain_two: Any
    shift_two: Any
    eb_one: Any
    eb_two: Any
    eb_three: Any
    e_gain: Any
    e_shift: Any


def finish_kernel(width, hidden, features, inner, *refs):
    refs = list(refs)
    take = lambda kind: kind(*(refs.pop(0) for _ in kind._fields))
    moved_in, packed_in = take(Moved), take(Chunks)
    moved_out, grads_out, biases = take(Moved), take(Grads), take(Biases)
    r, g, via = take(Chunks), take(Grads), take(Moved)
    sem, move_sem = refs
    half = lax.axis_index("half")
    wide = width // LANE
    tall = (2 * width + features) // CORES
    copy = pltpu.make_async_copy
    fetches = [copy(*pair, sem.at[at]) for at, pair in enumerate(zip(moved_in, via))]
    moves = [copy(*pair, move_sem.at[at]) for at, pair in enumerate(zip(via, moved_out))]
    first = len(fetches)
    loads = Chunks(*(copy(*pair, sem.at[first + at]) for at, pair in enumerate(zip(packed_in, r))))
    first += len(loads)
    stores = Grads(*(copy(*pair, sem.at[first + at]) for at, pair in enumerate(zip(g, grads_out))))
    for load in loads:
        load.start()
    for fetch in fetches:
        fetch.start()
    loads.third.wait()
    g.third_g[...], _ = take_wide(r.third, 0, hidden // CORES, wide)
    stores.third_g.start()
    loads.edge.wait()
    e_whole, at = take_wide(r.edge, 0, features, up(tall, LANE) // LANE)
    g.e_first[...] = e_whole[:, :tall]
    rest = features - LANE
    part = features // CORES
    left_two, at = take_wide(r.edge, at, part, 1)
    left_three, at = take_wide(r.edge, at, part, 1)
    right, at = take_wide(r.edge, at, part, 1)
    g.e_second[...] = jnp.concatenate([left_two, right[:, :rest]], 1)
    g.e_third[...] = jnp.concatenate([left_three, right[:, rest:]], 1)
    for store in (stores.e_first, stores.e_second, stores.e_third):
        store.start()
    for fetch, move in zip(fetches[:2], moves[:2]):
        fetch.wait()
        move.start()
    loads.second.wait()
    g.second_g[...], _ = take_wide(r.second, 0, hidden // CORES, wide)
    stores.second_g.start()
    for fetch, move in zip(fetches[2:], moves[2:]):
        fetch.wait()
        move.start()
    loads.first_a.wait()
    g.first_g[:, : hidden // 2], _ = take_wide(r.first_a, 0, tall, wide // 2)
    loads.first_b.wait()
    g.first_g[:, hidden // 2 :], at = take_wide(r.first_b, 0, tall, wide // 2)
    stores.first_g.start()
    small, _ = take_wide(r.first_b, at, 16, wide)

    def share(target, row):
        size = target.shape[0]
        target[...] = jnp.where(half == 0, row[:, :size], row[:, size : 2 * size]).reshape(size)

    b = biases
    for target, at in (
        (b.b_one, 0), (b.b_two, 1), (b.b_three, 2), (b.gain_one, 3), (b.shift_one, 4), (b.b_reduce, 9),
        (b.gain_two, 10), (b.shift_two, 11),
    ):
        share(target, small[at : at + 1])
    share(b.b_expand, jnp.concatenate([small[5 + p : 6 + p] for p in range(inner // width)], 1))
    share(b.eb_one, small[12:13, :LANES])
    share(b.eb_two, small[12:13, LANES:])
    share(b.eb_three, small[13:14, :LANES])
    share(b.e_gain, small[13:14, LANES:])
    share(b.e_shift, small[14:15, :LANES])
    for store in moves + list(stores):
        store.wait()


def finish(moved, sums, width, hidden, features, inner):
    tall = (2 * width + features) // CORES
    part = features // CORES
    grads = Grads(
        third_g=(hidden // CORES, width),
        e_first=(features, tall),
        e_second=(part, features),
        e_third=(part, features),
        second_g=(hidden // CORES, hidden),
        first_g=(tall, hidden),
    )
    sizes = Biases(hidden, hidden, width, width, width, inner, width, width, width, *[features] * 5)
    anywhere, vmem = pl.BlockSpec(memory_space=pl.ANY), pl.BlockSpec(memory_space=pltpu.VMEM)
    outs = [shape(a.shape, a.dtype) for a in moved]
    outs += [shape(dims, F32) for dims in grads]
    outs += [shape((size // CORES,), F32) for size in sizes]
    got = pl.pallas_call(
        functools.partial(finish_kernel, width, hidden, features, inner),
        out_shape=outs,
        in_specs=[anywhere] * (len(moved) + len(sums)),
        out_specs=[anywhere] * (len(moved) + len(grads)) + [vmem] * len(sizes),
        scratch_shapes=[pltpu.VMEM(a.shape, BF16) for a in sums]
        + [pltpu.VMEM(dims, F32) for dims in grads]
        + [pltpu.VMEM(a.shape, a.dtype) for a in moved]
        + [pltpu.SemaphoreType.DMA((len(moved) + len(sums) + len(grads),)), pltpu.SemaphoreType.DMA((len(moved),))],
        compiler_params=pltpu.CompilerParams(vmem_limit_bytes=VMEM),
        name="finish",
    )(*moved, *sums)
    first = len(moved) + len(grads)
    return Moved(*got[: len(moved)]), Grads(*got[len(moved) : first]), Biases(*got[first:])


def body(
    nodes, edges, neighbours, counts,
    message_first, message_first_bias, message_second, message_second_bias, message_third, message_third_bias,
    node_norm_gain, node_norm_shift, expand_weight, expand_bias, reduce_weight, reduce_bias,
    output_norm_gain, output_norm_shift,
    edge_first, edge_first_bias, edge_second, edge_second_bias, edge_third, edge_third_bias,
    edge_norm_gain, edge_norm_shift, cot_nodes, cot_edges,
):
    width, features = nodes.shape[1], edges.shape[2]
    hidden, inner = message_second.shape[0], expand_weight.shape[1]

    by_slots = lambda values: jnp.transpose(values, (1, 0, 2))
    vectors = Vectors(
        message_first_bias, message_second_bias, message_third_bias, node_norm_gain, node_norm_shift, reduce_bias,
        output_norm_gain, output_norm_shift, expand_bias, edge_first_bias, edge_second_bias, edge_third_bias,
        edge_norm_gain, edge_norm_shift, counts,
    )
    arrays = Arrays(
        nodes, by_slots(edges), neighbours.T, message_first, message_second, message_third, expand_weight,
        reduce_weight, edge_first.T, edge_second, edge_third, cot_nodes, by_slots(cot_edges),
    )
    state, out, fed_grad, edge_grad, g_expand, g_reduce, _, _, *sums = run(vectors, arrays)
    moved = Moved(edge_grad, g_expand, g_reduce, out, state, fed_grad)
    m, g, b = finish(moved, sums, width, hidden, features, inner)
    return (
        m.state, by_slots(m.edges), m.fed, by_slots(m.grads),
        g.first_g, b.b_one, g.second_g, b.b_two, g.third_g, b.b_three, b.gain_one, b.shift_one,
        m.expand, b.b_expand, m.reduce, b.b_reduce, b.gain_two, b.shift_two,
        g.e_first.T, b.eb_one, g.e_second, b.eb_two, g.e_third, b.eb_three, b.e_gain, b.e_shift,
    )


def solution(mesh):
    rows, slots = P("res", None), P("res", None, None)
    copied = P()
    down, vec = P("half", None), P("half")
    return jax.shard_map(
        body,
        mesh=mesh,
        in_specs=(rows, slots, rows, P("res")) + (copied,) * 22 + (rows, slots),
        out_specs=(
            P("res", "half"),
            P("res", "half", None),
            P("res", "half"),
            P("res", "half", None),
            down, vec, down, vec, down, vec, vec, vec, down, vec, down, vec, vec, vec,
            down, vec, down, vec, down, vec, vec, vec,
        ),
        check_vma=False,
    )
```

```python
import functools
import types
from typing import Any, NamedTuple

import jax
import jax.numpy as jnp
from jax import lax
from jax.experimental import pallas as pl
from jax.experimental.pallas import tpu as pltpu
from jax.sharding import PartitionSpec as P

EPSILON = 1e-05
REACH = 64
CORES = 2
NEAR = 0.7978845608
CUBE = 0.044715
STEP = 30
CHAIN = 5
BACK_CHAIN = 15
EDGE_CHAIN = 15
EARLY_WIDE = 6
PARTS = 2
LANES = 256
LANE = 128
WIDE = 256
VMEM = 62 * 2**20
MESH = pl.DeviceIdType.MESH
F32 = jnp.float32
BF16 = jnp.bfloat16


def dot(left, right):
    return jnp.dot(left, right, preferred_element_type=F32)


def dot_t(left, right):
    return lax.dot_general(left, right, (((1,), (1,)), ((), ())), preferred_element_type=F32)


def t_dot(left, right):
    return lax.dot_general(left, right, (((0,), (0,)), ((), ())), preferred_element_type=F32)


def two_parts(values):
    high = values.astype(BF16)
    return high, (values - high.astype(F32)).astype(BF16)


def dot_wide(values, right, transposed=False):
    rows = values.shape[0]
    both = (dot_t if transposed else dot)(jnp.concatenate(two_parts(values), 0), right)
    return both[:rows] + both[rows:]


def gelu(values):
    kind = values.dtype.type
    square = values * values
    bend = jnp.tanh(values * (kind(NEAR) + kind(NEAR * CUBE) * square))
    return values * (kind(0.5) + kind(0.5) * bend)


def gelu_slope(values):
    square = values * values
    part = 0.5 + 0.5 * jnp.tanh(values * (NEAR + (NEAR * CUBE) * square))
    return part + values * part * (1.0 - part) * (2.0 * NEAR + (6.0 * NEAR * CUBE) * square)


def gelu_and_slope(values):
    values = values.astype(BF16)
    square = values * values
    part = BF16(0.5) + BF16(0.5) * jnp.tanh(values * (BF16(NEAR) + BF16(NEAR * CUBE) * square))
    act = values * part
    slope = part + act * (1 - part) * (BF16(2.0 * NEAR) + BF16(6.0 * NEAR * CUBE) * square)
    return act, slope


def norm_parts(values):
    centered = values - jnp.mean(values, -1, keepdims=True)
    scale = lax.rsqrt(jnp.mean(centered * centered, -1, keepdims=True) + EPSILON)
    return centered * scale, scale


def norm_back(grad, unit, scale, gain):
    scaled = gain * grad
    flat = jnp.mean(scaled, -1, keepdims=True)
    slant = jnp.mean(scaled * unit, -1, keepdims=True)
    return (scaled - flat - unit * slant) * scale


def col_sum(values):
    return jnp.sum(values, 0, keepdims=True)


def iota(dims, axis):
    return lax.broadcasted_iota(jnp.int32, dims, axis)


def chip_dims(count):
    side = 1
    while 2 * (2 * side) ** 3 <= count and count % (4 * side * side) == 0:
        side *= 2
    return side, count // (side * side)


def up(size, unit):
    return -(-size // unit) * unit


class Chunks(NamedTuple):
    edge: Any
    third: Any
    first_a: Any
    first_b: Any
    second: Any


ORDERS = Chunks((0, 2, 1), (0, 1, 2), (2, 0, 1), (0, 1, 2), (0, 2, 1))


def chunk_rows(count, width, hidden, features):
    tall = (2 * width + features) // CORES
    wide = width // LANE
    edge = features * (up(tall, LANE) // LANE) + 3 * (features // CORES)
    square = (hidden // CORES) * wide
    first = tall * (wide // 2)
    sizes = (edge, square, first, first + 16 * wide, square)
    return Chunks(*(up(rows, 16 * count) for rows in sizes))


def cut(pieces, start, stop):
    at, got = 0, []
    for piece in pieces:
        low, high = max(start, at), min(stop, at + piece.shape[0])
        if low < high:
            got.append(piece[low - at : high - at])
        at += piece.shape[0]
    return jnp.concatenate(got, 0) if len(got) > 1 else got[0]


def put_wide(pack, half, at, piece):
    rows = piece.shape[0]
    for block in range(piece.shape[1] // LANE):
        pack[half, pl.ds(at, rows), :] = piece[:, block * LANE : (block + 1) * LANE].astype(BF16)
        at += rows
    return at


def put_rest(pack, at):
    rest = pack.shape[1] - at
    if rest:
        for half in range(CORES):
            pack[half, pl.ds(at, rest), :] = jnp.zeros((rest, LANE), BF16)


def take_wide(packed, at, rows, blocks):
    pieces = [packed[pl.ds(at + b * rows, rows), :] for b in range(blocks)]
    return jnp.concatenate(pieces, 1).astype(F32), at + blocks * rows


class Copies:
    def __init__(self, send, recv):
        self.send, self.recv, self.used = send, recv, 0

    def group(self, entries):
        made = []
        for source, target, device in entries:
            at = self.used
            self.used += 1
            made.append(functools.partial(self._make, source, target, device, at))
        return Group(made)

    def _make(self, source, target, device, at):
        return pltpu.make_async_remote_copy(
            src_ref=source,
            dst_ref=target,
            send_sem=self.send.at[at],
            recv_sem=self.recv.at[at],
            device_id=device,
            device_id_type=MESH,
        )


class Group:
    def __init__(self, made):
        self.made = made

    def start(self):
        for make in self.made:
            make().start()

    def wait(self):
        for make in self.made:
            make().wait()


class Place:
    def __init__(self):
        res, half, count = lax.axis_index("res"), lax.axis_index("half"), lax.axis_size("res")
        side, deep = chip_dims(count)
        x, y, z = lax.rem(res, side), lax.rem(res // side, side), res // (side * side)
        first = half == 0
        self.res, self.half, self.count = res, half, count
        self.dims = (side, side, deep)
        self.at = (jnp.where(first, x, y), jnp.where(first, y, x), z)
        self.strides = (jnp.where(first, 1, side), jnp.where(first, side, 1), side * side)
        self.partner = (res, 1 - half)

    def peers(self, level):
        size, here = self.dims[level], self.at[level]
        found = []
        for ahead in range(1, size):
            to = lax.rem(here + ahead, size)
            found.append((to, (self.res + (to - here) * self.strides[level], self.half)))
        return found

    def line(self):
        res, half, count = self.res, self.half, self.count
        return (
            (res > 0, (res - 1, half)),
            (res + half > 0, (res - 1 + half, 1 - half)),
            (res + half < count, (res + half, 1 - half)),
            (res < count - 1, (res + 1, half)),
        )

    def line_count(self):
        res, half, count = self.res, self.half, self.count
        return 4 - jnp.where(res > 0, 0, 2 - half) - jnp.where(res < count - 1, 0, 1 + half)


def greet(place):
    barrier = pltpu.get_barrier_semaphore()

    def signal(device):
        pl.semaphore_signal(barrier, inc=1, device_id=device, device_id_type=MESH)

    for exists, device in place.line():
        pl.when(exists)(functools.partial(signal, device))
    signal(place.partner)
    others = 1
    for level in range(3):
        for _, device in place.peers(level):
            signal(device)
            others += 1
    pl.semaphore_wait(barrier, others + place.line_count())


def halo_layout(rows):
    edge = REACH - rows
    return ((0, edge), (edge, rows), (REACH + rows, rows), (REACH + 2 * rows, edge))


class Halo:
    def __init__(self, place, window, rows, send, recv, first):
        self.place, self.window, self.rows = place, window, rows
        self.send, self.recv, self.first = send, recv, first

    def clear(self):
        for (exists, _), (offset, size) in zip(self.place.line(), halo_layout(self.rows)):

            @pl.when(jnp.logical_not(exists))
            def _():
                self.window[pl.ds(offset, size), :] = jnp.zeros((size, self.window.shape[1]), self.window.dtype)

    def _copy(self, at, device):
        offset, size = halo_layout(self.rows)[3 - at]
        first = REACH + (self.rows - size if at == 3 else 0)
        return pltpu.make_async_remote_copy(
            src_ref=self.window.at[pl.ds(first, size)],
            dst_ref=self.window.at[pl.ds(offset, size)],
            send_sem=self.send.at[self.first + at],
            recv_sem=self.recv.at[self.first + 3 - at],
            device_id=device,
            device_id_type=MESH,
        )

    def start(self):
        for at, (exists, device) in enumerate(self.place.line()):

            @pl.when(exists)
            def _():
                self._copy(at, device).start()

    def wait(self):
        for at, (exists, device) in enumerate(self.place.line()):
            offset, size = halo_layout(self.rows)[at]

            @pl.when(exists)
            def _():
                self._copy(at, device).wait_send()
                pltpu.make_async_remote_copy(
                    src_ref=self.window.at[pl.ds(offset, size)],
                    dst_ref=self.window.at[pl.ds(offset, size)],
                    send_sem=self.send.at[self.first + at],
                    recv_sem=self.recv.at[self.first + at],
                    device_id=device,
                    device_id_type=MESH,
                ).wait_recv()


class Returns:
    def __init__(self, place, table, landing, rows, send, recv, first):
        self.place, self.table, self.landing, self.rows = place, table, landing, rows
        self.send, self.recv, self.first = send, recv, first

    def _copy(self, at, device):
        layout = halo_layout(self.rows)
        offset, size = layout[at]
        return pltpu.make_async_remote_copy(
            src_ref=self.table.at[pl.ds(offset, size)],
            dst_ref=self.landing.at[pl.ds(layout[3 - at][0], size)],
            send_sem=self.send.at[self.first + at],
            recv_sem=self.recv.at[self.first + 3 - at],
            device_id=device,
            device_id_type=MESH,
        )

    def start(self):
        for at, (exists, device) in enumerate(self.place.line()):

            @pl.when(exists)
            def _():
                self._copy(at, device).start()

    def finish(self, total):
        total[...] = self.table[pl.ds(REACH, self.rows), :]
        for at, (exists, device) in enumerate(self.place.line()):
            offset, size = halo_layout(self.rows)[at]
            first = self.rows - size if at == 3 else 0

            @pl.when(exists)
            def _():
                self._copy(at, device).wait_send()
                pltpu.make_async_remote_copy(
                    src_ref=self.table.at[pl.ds(offset, size)],
                    dst_ref=self.landing.at[pl.ds(offset, size)],
                    send_sem=self.send.at[self.first + at],
                    recv_sem=self.recv.at[self.first + at],
                    device_id=device,
                    device_id_type=MESH,
                ).wait_recv()
                total[pl.ds(first, size), :] += self.landing[pl.ds(offset, size), :]


def gather_groups(place, copies, ref, unit, source=None, base=0):
    mine = (place.at[0] * place.dims[1] + place.at[1]) * place.dims[2] + place.at[2]
    groups, size = [], unit
    start = mine * unit
    for level in (2, 1, 0):
        here = ref.at[pl.ds(pl.multiple_of(base + start, 16), size)]
        from_ref = here if source is None or level < 2 else source
        groups.append(copies.group([(from_ref, here, device) for _, device in place.peers(level)]))
        start = start - place.at[level] * size
        size = size * place.dims[level]
    return groups


class ChipSum:
    def __init__(self, place, copies, order, pack, got, landed, gathered):
        self.place, self.pack, self.got, self.landed, self.gathered = place, pack, got, landed, gathered
        half, size = place.half, pack.shape[1]
        self.pair = copies.group([(pack.at[1 - half], got, place.partner)])
        self.steps, self.shares, self.back = [], [], []
        start, base = 0, 0
        for level in order:
            share = size // place.dims[level]
            entries, lands = [], []
            for to, device in place.peers(level):
                source = pack.at[half, pl.ds(pl.multiple_of(start + to * share, 16), share)]
                entries.append((source, landed.at[pl.ds(base, share)], device))
                lands.append(base)
                base += share
            start = pl.multiple_of(start + place.at[level] * share, 16)
            size = share
            self.steps.append(copies.group(entries))
            self.shares.append((start, share, lands))
            here = gathered.at[pl.ds(start, share)]
            back = [(here, here, device) for _, device in place.peers(level)]
            self.back.insert(0, copies.group(back))

    def send_pair(self):
        self.pair.start()

    def add_pair(self):
        self.pair.wait()
        half = self.place.half
        self.pack[half] = (self.pack[half].astype(F32) + self.got[...].astype(F32)).astype(BF16)

    def start(self, level):
        self.steps[level].start()

    def finish(self, level):
        self.steps[level].wait()
        start, share, lands = self.shares[level]
        half = self.place.half
        total = self.pack[half, pl.ds(start, share), :].astype(F32)
        for base in lands:
            total = total + self.landed[pl.ds(base, share), :].astype(F32)
        if level < len(self.steps) - 1:
            self.pack[half, pl.ds(start, share), :] = total.astype(BF16)
        else:
            self.gathered[pl.ds(start, share), :] = total.astype(BF16)

    def start_back(self, step):
        self.back[step].start()

    def finish_back(self, step):
        self.back[step].wait()


def flat(values):
    return values.reshape(values.shape[0] * values.shape[1], values.shape[2])


def feed_forward(r, pooled, own):
    width = own.shape[1]
    mean = pooled / r.counts[:, 0:1]
    summed = own + dot_wide(mean, r.third[...]) + r.b_three
    unit, _ = norm_parts(summed)
    normed = unit * r.gain_one + r.shift_one
    low = normed.astype(BF16)
    pre = dot(low, r.expand[...]) + r.b_expand
    second = normed + dot(gelu(pre).astype(BF16), r.reduce[...]) + r.b_reduce
    unit_two, _ = norm_parts(second)
    r.summed[...] = summed
    r.pre_expand[...] = pre
    r.second[...] = second
    r.normed[...] = low
    return unit_two * r.gain_two + r.shift_two


def fill_own(window, far, own, bias, table, rows, multiply):
    here = pl.ds(REACH, rows)
    table[here, :] = multiply(window[here, :], far).astype(BF16)
    table[pl.ds(window.shape[0], rows), :] = (multiply(window[here, :], own) + bias).astype(BF16)


def fill_far(window, far, table, rows, multiply):
    for here in (pl.ds(0, REACH), pl.ds(REACH + rows, REACH)):
        table[here, :] = multiply(window[here, :], far).astype(BF16)


def chain_parts(step):
    return [step * STEP + part * CHAIN for part in range(STEP // CHAIN)]


def chain_rows(r, slot):
    rows = r.counts.shape[0]
    return pl.ds(pl.multiple_of(slot * rows, CHAIN * rows), CHAIN * rows)


def step_rows(r, step):
    rows = r.counts.shape[0]
    return pl.ds(pl.multiple_of(step * (STEP * rows), STEP * rows), STEP * rows)


def build_block(r, step, half, places):
    rows = r.counts.shape[0]
    here = pl.ds(step * STEP, STEP)
    named = r.picks[here]
    dims = (STEP, rows, named.shape[2])
    spread = jnp.broadcast_to(named, dims)
    mine = iota(dims, 2) == iota(dims, 1) + half * rows
    pick = jnp.sum(jnp.where(mine, spread, 0.0), -1, keepdims=True)
    dims = (STEP, rows, LANES)
    lane = iota(dims, 2)
    hit = (lane.astype(F32) == pick) | (lane == iota(dims, 1) + places)
    r.onehot[here] = jnp.where(hit, 1.0, 0.0).astype(BF16)


def joined_rows(r, slot, slots):
    here = pl.ds(slot, slots)
    return jnp.concatenate([flat(r.onehot[here]), flat(r.edges_raw[here])], 1)


def live_rows(r, slot, width):
    count = r.counts[...]
    dims = (CHAIN,) + count.shape
    live = jnp.where(iota(dims, 0) + slot < count[None], 1.0, 0.0)
    return flat(jnp.concatenate([live] * (width // LANE), -1))


def live_column(r, slot, slots):
    count = r.counts[...]
    dims = (slots,) + count.shape
    return flat(jnp.where(iota(dims, 0) + slot < count[None], 1.0, 0.0))[:, 0:1]


def node_block(r, step, keep):
    rows = r.counts.shape[0]
    hidden = r.second_w.shape[0]
    slots = chain_parts(step)
    dims = (rows, CHAIN * rows)
    count = jnp.broadcast_to(r.counts[:, 0:1], dims)
    pre = [dot(joined_rows(r, slot, CHAIN), r.table[...]) for slot in slots]
    acts = []
    for slot, values in zip(slots, pre):
        if keep:
            here = chain_rows(r, slot)
            act, slope = gelu_and_slope(values)
            r.act[here, :] = act
            r.slope_one[here, :] = slope
        else:
            act = gelu(values.astype(BF16))
        acts.append(act)
    pre = [dot(act, r.second_w[...]) + r.b_two for act in acts]
    total = r.pooled[...]
    for slot, values in zip(slots, pre):
        if keep:
            act, slope = gelu_and_slope(values)
            r.slope_two[chain_rows(r, slot), :] = slope * live_rows(r, slot, hidden).astype(BF16)
        else:
            act = gelu(values.astype(BF16))
        used = jnp.where(r.lane_slot[0:1, :] + slot.astype(F32) < count, r.diagonal[...], 0.0)
        total = total + dot(used.astype(BF16), act.astype(BF16))
    r.pooled[...] = total


def edge_block(r, step, features):
    rows = r.counts.shape[0]
    split = lambda values: values.reshape(values.shape[0] // rows, rows, features)
    slots = [step * STEP + part * EDGE_CHAIN for part in range(STEP // EDGE_CHAIN)]
    each = lambda body, *lists: [body(*items) for items in zip(*lists)]
    joined = [joined_rows(r, slot, EDGE_CHAIN) for slot in slots]
    live = [live_column(r, slot, EDGE_CHAIN) for slot in slots]
    pre = each(lambda z: dot(z, r.e_table[...]), joined)
    o_one, slope_one = zip(*each(gelu_and_slope, pre))
    pre = each(lambda a: dot(a, r.e_second_w[...]) + r.eb_two, o_one)
    o_two, slope_two = zip(*each(gelu_and_slope, pre))
    summed = each(lambda z, a: z[:, LANES:].astype(F32) + (dot(a, r.e_third_w[...]) + r.eb_three), joined, o_two)
    unit, scale = zip(*each(norm_parts, summed))
    d_three, d_sums = [], []
    for slot, u, k, used in zip(slots, unit, scale, live):
        here = pl.ds(slot, EDGE_CHAIN)
        r.edge_out[here] = split((u * r.e_gain + r.e_shift) * used).astype(BF16)
        d_out = flat(r.cots_raw[here]).astype(F32) * used
        r.ge_norm[0:1, :] += col_sum(d_out * u)
        r.ge_norm[1:2, :] += col_sum(d_out)
        d_sum = norm_back(d_out, u, k, r.e_gain)
        r.ge_norm[2:3, :] += col_sum(d_sum)
        d_sums.append(d_sum)
        d_three.append(d_sum.astype(BF16))
    d_two = each(lambda d, k: dot_t(d, r.e_third_w[...]) * k, d_three, slope_two)
    r.ge_norm[3:4, :] += sum(col_sum(d) for d in d_two)
    d_two = each(lambda d: d.astype(BF16), d_two)
    d_one = each(lambda d, k: (dot_t(d, r.e_second_w[...]) * k).astype(BF16), d_two, slope_one)
    for slot, d_sum, d in zip(slots, d_sums, d_one):
        more = dot(d, r.e_first_t[:, pl.ds(2 * r.nodes_width, features)])
        r.edge_grad[pl.ds(slot, EDGE_CHAIN)] = split(d_sum + more)
    together = lambda values: jnp.concatenate(values, 0)
    r.ge_third[...] += t_dot(together(o_two), together(d_three))
    r.ge_second[...] += t_dot(together(o_one), together(d_two))
    r.ge_first[...] += t_dot(together(joined), together(d_one))


def node_grad(r, cot, far_total, when_ds):
    width = cot.shape[1]
    grad = cot.astype(F32) + r.e_own_back[...] + dot_wide(far_total, r.e_first_t[:, pl.ds(width, width)])
    unit, scale = norm_parts(r.second[...])
    dw = norm_back(grad, unit, scale, r.gain_two)
    gain_two, shift_two = col_sum(grad * unit), col_sum(grad)
    ds = dw.astype(BF16)
    r.ds[...] = ds
    when_ds()
    slope = gelu_slope(r.pre_expand[...])
    dq = (dot_t(ds, r.reduce[...]) * slope).astype(BF16)
    dv = dw + dot_t(dq, r.expand[...])
    unit, scale = norm_parts(r.summed[...])
    du = norm_back(dv, unit, scale, r.gain_one)
    r.du[...] = du
    counts = r.counts[:, 0:1]
    dm = (du / counts).astype(BF16)
    r.slot_grad[...] = dot_t(dm, r.third[...])
    r.dm[...] = dm
    small = r.small
    small[...] = jnp.zeros(small.shape, F32)
    small[2:3, :] = col_sum(counts * dm.astype(F32))
    small[3:4, :] = col_sum(dv * unit)
    small[4:5, :] = col_sum(dv)
    dq_sum = col_sum(dq.astype(F32))
    for part in range(dq_sum.shape[1] // width):
        small[5 + part : 6 + part, :] = dq_sum[:, part * width : (part + 1) * width]
    small[9:10, :] = col_sum(ds.astype(F32))
    small[10:11, :] = gain_two
    small[11:12, :] = shift_two


def put_features(pack, half, at, e_second, e_third):
    part = e_second.shape[0] // CORES
    two = [ref[pl.ds(half * part, part), :] for ref in (e_second, e_third)]
    for piece in two:
        at = put_wide(pack, half, at, piece[:, :LANE])
    return put_wide(pack, half, at, jnp.concatenate([piece[:, LANE:] for piece in two], 1))


def pack_edge(r, pack):
    features = r.ge_second.shape[0]
    g_edge = jnp.transpose(r.ge_first[pl.ds(LANES, features), :])
    e_first = jnp.concatenate([r.ge_own[...], r.ge_far[...], g_edge], 1)
    tall = e_first.shape[1] // CORES
    fill = jnp.zeros((features, up(tall, LANE) - tall), F32)
    for half in range(CORES):
        piece = jnp.concatenate([e_first[:, half * tall : (half + 1) * tall], fill], 1)
        at = put_wide(pack, half, 0, piece)
        at = put_features(pack, half, at, r.ge_second, r.ge_third)
    put_rest(pack, at)


def pack_third(r, pack):
    dm = r.dm[...]
    found = t_dot(jnp.concatenate(two_parts(r.pooled[...]), 0), jnp.concatenate([dm, dm], 0))
    part = found.shape[0] // CORES
    for half in range(CORES):
        at = put_wide(pack, half, 0, found[half * part : (half + 1) * part])
    put_rest(pack, at)


def pack_second(r, pack):
    part = r.g_second.shape[0] // CORES
    for half in range(CORES):
        at = put_wide(pack, half, 0, r.g_second[pl.ds(half * part, part), :])
    put_rest(pack, at)


def small_rows(r, places):
    rows = r.counts.shape[0]
    features = r.ge_norm.shape[1]
    fill = jnp.zeros((1, LANES - features), F32)
    own = pl.ds(places, rows)
    edge = [col_sum(r.ge_first[own, :])] + [r.ge_norm[at : at + 1, :] for at in (3, 2, 0, 1)]
    edge = [jnp.concatenate([row, fill], 1) for row in edge] + [jnp.zeros((1, LANES), F32)]
    lines = [col_sum(r.g_first[own, :]), r.g_bias[...], r.small[2:12, :]]
    lines += [jnp.concatenate(edge[at : at + 2], 1) for at in (0, 2, 4)]
    return jnp.concatenate(lines + [jnp.zeros((1, r.small.shape[1]), F32)], 0)


def pack_first(r, packs, g_own, g_far, features, small):
    pieces = [g_own, g_far, r.g_first[pl.ds(LANES, features), :]]
    tall = sum(piece.shape[0] for piece in pieces) // CORES
    hidden = g_own.shape[1]
    for side, pack in enumerate(packs):
        cols = slice(side * (hidden // 2), (side + 1) * (hidden // 2))
        for half in range(CORES):
            at = put_wide(pack, half, 0, cut([piece[:, cols] for piece in pieces], half * tall, (half + 1) * tall))
            if side == 1:
                at = put_wide(pack, half, at, small)
        put_rest(pack, at)


def first_grad_block(r, step, features):
    rows = r.counts.shape[0]
    hidden = r.act.shape[1]
    coming = jnp.broadcast_to(r.slot_grad[...][None], (BACK_CHAIN,) + r.slot_grad.shape)
    slots = [step * STEP + part * BACK_CHAIN for part in range(STEP // BACK_CHAIN)]
    places = [pl.ds(pl.multiple_of(slot * rows, BACK_CHAIN * rows), BACK_CHAIN * rows) for slot in slots]
    twos, ones = [], []
    for here in places:
        d_two = flat(coming) * r.slope_two[here, :].astype(F32)
        r.g_bias[...] += col_sum(d_two)
        twos.append(d_two.astype(BF16))
        r.slope_two[here, :] = twos[-1]
    backs = [dot_t(d_two, r.second_w[...]) for d_two in twos]
    for here, back in zip(places, backs):
        ones.append((back * r.slope_one[here, :].astype(F32)).astype(BF16))
        r.slope_one[here, :] = ones[-1]
    r.g_first[...] += t_dot(joined_rows(r, step * STEP, STEP), jnp.concatenate(ones, 0))


def second_grad_block(r, step, features):
    rows = r.counts.shape[0]
    here = step_rows(r, step)
    r.g_second[...] += t_dot(r.act[here, :], r.slope_two[here, :])
    more = dot_t(r.slope_one[here, :], r.table[pl.ds(LANES, features), :])
    there = pl.ds(step * STEP, STEP)
    r.edge_grad_low[there] = (r.edge_grad[there] + more.reshape(STEP, rows, features)).astype(BF16)


def put(target, rows, cols, found, fresh):
    target[rows, cols] = (found if fresh else target[rows, cols] + found).astype(target.dtype)


class WideBlock:
    def __init__(self, r, step, half):
        width, inner = r.expand.shape
        blocks = inner // WIDE
        self.r, self.step, self.mine = r, step, blocks // CORES
        self.block = lax.rem(step + half * self.mine, blocks)
        self.here = pl.ds(pl.multiple_of(self.block * WIDE, WIDE), WIDE)
        part = width // CORES
        self.cols = pl.ds(pl.multiple_of(half * part, part), part)
        self.total = r.normed_all.shape[0]
        size = self.total // PARTS
        self.rows = [pl.ds(at * size, size) for at in range(PARTS)]

    def forward(self):
        r = self.r
        bias = r.bias_wide[pl.ds(self.block, 1), :]
        pre = [dot(r.normed_all[rows, :], r.expand[:, self.here]) + bias for rows in self.rows]
        both = [gelu_and_slope(values) for values in pre]
        return [act for act, _ in both], [slope for _, slope in both]

    def place(self, slot, rows=None):
        size = self.total if rows is None else rows.size
        first = (slot // 2) * self.total + (0 if rows is None else rows.start)
        return self.r.kept.at[
            pl.ds(pl.multiple_of(first, 16), size), pl.ds(pl.multiple_of(lax.rem(slot, 2) * WIDE, WIDE), WIDE)
        ]

    def keep(self):
        acts, slopes = self.forward()
        for rows, slope in zip(self.rows, slopes):
            self.place(self.step, rows)[...] = slope

        @pl.when(self.step < self.mine)
        def _():
            for rows, act in zip(self.rows, acts):
                self.place(EARLY_WIDE + self.step, rows)[...] = act

    def backward(self, slopes, act, fresh):
        r = self.r
        back = [dot_t(r.ds_all[rows, :], r.reduce[self.here, :]) for rows in self.rows]
        dqs = [(grad * slope.astype(F32)).astype(BF16) for grad, slope in zip(back, slopes)]
        found = t_dot(r.normed_all[:, self.cols], jnp.concatenate(dqs, 0))
        put(r.g_expand, slice(None), self.here, found, fresh)

        @pl.when(self.step < self.mine)
        def _():
            out = pl.ds(pl.multiple_of(self.step * WIDE, WIDE), WIDE)
            found = t_dot(act(), r.ds_all[...])
            put(r.g_reduce, out, slice(None), found, fresh)

    def from_kept(self):
        slopes = [self.place(self.step, rows)[...] for rows in self.rows]
        self.backward(slopes, lambda: self.place(EARLY_WIDE + self.step)[...], True)

    def whole(self, fresh):
        acts, slopes = self.forward()
        self.backward(slopes, lambda: jnp.concatenate(acts, 0), fresh)


class Vectors(NamedTuple):
    b_one: Any
    b_two: Any
    b_three: Any
    gain_one: Any
    shift_one: Any
    b_reduce: Any
    gain_two: Any
    shift_two: Any
    b_expand: Any
    eb_one: Any
    eb_two: Any
    eb_three: Any
    e_gain: Any
    e_shift: Any
    counts_in: Any


class Arrays(NamedTuple):
    nodes: Any
    edges: Any
    neighbours: Any
    first_in: Any
    second_in: Any
    third_in: Any
    expand_in: Any
    reduce_in: Any
    e_first_in: Any
    e_second_in: Any
    e_third_in: Any
    cot_nodes: Any
    cot_edges: Any


class Results(NamedTuple):
    state_out: Any
    edges_out: Any
    fed_out: Any
    grads_out: Any
    expand_out: Any
    reduce_out: Any
    normed_slots: Any
    ds_slots: Any


def kernel(names, features, *refs):
    kinds, refs = (Vectors, Arrays, Results), list(refs)
    r = types.SimpleNamespace()
    for kind in kinds:
        for name in kind._fields:
            setattr(r, name, refs.pop(0))
    r.sums_out = Chunks(*(refs.pop(0) for _ in Chunks._fields))
    for name in names:
        setattr(r, name, refs.pop(0))
    r.pack, r.got, r.landed, r.gathered = (Chunks(*(refs.pop(0) for _ in Chunks._fields)) for _ in range(4))
    place = Place()
    res, half, count = place.res, place.half, place.count
    rows_dev, width = r.nodes.shape
    rows = rows_dev // CORES
    places = rows + 2 * REACH
    slots = r.edges.shape[0]
    each = slots // CORES
    steps = slots // STEP
    r.nodes_width = width
    total = r.edges_raw.shape[0] * rows
    r.edge_grad_low = r.cots_raw
    r.act, r.slope_one, r.slope_two = (r.kept.at[pl.ds(at * total, total)] for at in range(3))
    for name in Vectors._fields:
        vector = getattr(r, name)
        setattr(r, name, vector[...].astype(F32).reshape(1, vector.shape[0]))
    own = pl.ds(REACH, rows)
    mine = pl.ds(pl.multiple_of(half * rows, 16), rows)

    pairs = dict(
        nodes=(r.nodes.at[mine], r.windows.at[0, own]),
        neighbours=(r.neighbours, r.neighbours_raw),
        first=(r.first_in, r.first),
        edges=(r.edges.at[:, mine, :], r.edges_raw),
        second=(r.second_in, r.second_w),
        e_first=(r.e_first_in, r.e_first_t),
        e_second=(r.e_second_in, r.e_second_w),
        e_third=(r.e_third_in, r.e_third_w),
        third=(r.third_in, r.third),
        expand=(r.expand_in, r.expand),
        reduce=(r.reduce_in, r.reduce),
        cot_edges=(r.cot_edges.at[:, mine, :], r.cots_raw),
        cot_nodes=(r.cot_nodes.at[mine], r.cot_rows),
    )
    loads = types.SimpleNamespace()
    for at, (name, pair) in enumerate(pairs.items()):
        copy = pltpu.make_async_copy(*pair, r.load_sem.at[at])
        setattr(loads, name, copy)
        copy.start()

    halos = [
        Halo(place, r.windows.at[k], rows, r.line_send, r.line_recv, 4 * k) for k in range(3)
    ]
    edge_returns = Returns(place, r.ge_first, r.edge_landing, rows, r.line_send, r.line_recv, 12)
    node_returns = Returns(place, r.g_first, r.node_landing, rows, r.line_send, r.line_recv, 16)
    copies = Copies(r.step_send, r.step_recv)
    edge, third, first_a, first_b, second = sums = Chunks(
        *(ChipSum(place, copies, *parts) for parts in zip(ORDERS, r.pack, r.got, r.landed, r.gathered))
    )
    span = count * rows

    def row_gather(source, slot_ref):
        base = half * span
        groups = gather_groups(place, copies, slot_ref, rows, source, base)
        here = slot_ref.at[pl.ds(pl.multiple_of(base, 16), span)]
        groups.append(copies.group([(here, here, place.partner)]))
        return groups

    normed_gather = row_gather(r.normed, r.normed_slots)
    ds_gather = row_gather(r.ds, r.ds_slots)
    my_unit = (place.at[0] * place.dims[1] + place.at[1]) * place.dims[2] + place.at[2]
    my_slot = pl.ds(pl.multiple_of(half * span + my_unit * rows, 16), rows)
    normed_keep = pltpu.make_async_copy(r.normed, r.normed_slots.at[my_slot], r.keep_sem.at[0])
    ds_keep = pltpu.make_async_copy(r.ds, r.ds_slots.at[my_slot], r.keep_sem.at[1])
    there = pl.ds(pl.multiple_of(half * rows, 16), rows)
    my_slots = pl.ds(half * each, each)
    its_slots = pl.ds((1 - half) * each, each)
    edges_target = r.edges_out.at[:, there, :]
    edges_pair = copies.group([(r.edge_out.at[its_slots], edges_target, place.partner)])
    edges_keep = pltpu.make_async_copy(r.edge_out.at[my_slots], edges_target, r.keep_sem.at[2])
    grads_target = r.grads_out.at[:, there, :]
    grads_pair = copies.group([(r.edge_grad_low.at[its_slots], grads_target, place.partner)])
    grads_keep = pltpu.make_async_copy(r.edge_grad_low.at[my_slots], grads_target, r.keep_sem.at[3])
    fed_pair = copies.group([(r.fed_grad.at[1 - half], r.fed_out.at[there], place.partner)])
    fed_keep = pltpu.make_async_copy(r.fed_grad.at[half], r.fed_out.at[there], r.keep_sem.at[4])

    greet(place)
    loads.nodes.wait()
    halos[0].start()
    for halo in halos:
        halo.clear()
    dims = (rows, LANE)
    counted = jnp.broadcast_to(r.counts_in, (rows, rows_dev))
    here = iota(counted.shape, 1) == iota(counted.shape, 0) + half * rows
    r.counts[...] = jnp.broadcast_to(jnp.sum(jnp.where(here, counted, 0.0), -1, keepdims=True), dims)
    for block in range(r.expand.shape[1] // WIDE):
        r.bias_wide[block : block + 1, :] = r.b_expand[:, block * WIDE : (block + 1) * WIDE]
    dims = (rows, CHAIN * rows)
    lane = iota(dims, 1)
    r.diagonal[...] = jnp.where(lax.rem(lane, rows) == iota(dims, 0), 1.0, 0.0)
    r.lane_slot[...] = (iota(r.lane_slot.shape, 1) // rows).astype(F32)
    loads.neighbours.wait()
    base = res * rows_dev + half * rows - REACH
    named = (r.neighbours_raw[...] - base).astype(F32)
    r.picks[...] = named.reshape(slots, 1, rows_dev)

    def build(step, carry):
        build_block(r, step, half, places)
        return carry

    lax.fori_loop(0, steps, build, 0)
    for table in (r.table, r.e_table):
        rest = LANES - places - rows
        if rest:
            table[pl.ds(places + rows, rest), :] = jnp.zeros((rest, table.shape[1]), BF16)
    for load in (loads.first, loads.e_first, loads.e_second, loads.e_third):
        load.wait()
    r.table[pl.ds(LANES, features), :] = r.first[pl.ds(2 * width, features), :]
    edge_part = r.e_first_t[:, pl.ds(2 * width, features)]
    r.e_table[pl.ds(LANES, features), :] = jnp.transpose(edge_part.astype(F32)).astype(BF16)
    loads.edges.wait()
    bias = r.b_one
    far_w, own_w = r.first[pl.ds(width, width), :], r.first[pl.ds(0, width), :]
    fill_own(r.windows.at[0], far_w, own_w, bias, r.table, rows, dot)
    halos[0].wait()
    fill_far(r.windows.at[0], far_w, r.table, rows, dot)
    r.pooled[...] = jnp.zeros(r.pooled.shape, F32)
    loads.second.wait()

    def first_pass(step, carry):
        node_block(r, step, False)
        return carry

    lax.fori_loop(0, steps, first_pass, 0)
    loads.third.wait()
    loads.expand.wait()
    loads.reduce.wait()
    r.windows[1, own, :] = feed_forward(r, r.pooled[...], r.windows[0, own, :].astype(F32)).astype(BF16)

    halos[1].start()
    loads.cot_edges.wait()
    loads.cot_nodes.wait()
    fill_own(r.windows.at[1], far_w, own_w, bias, r.table, rows, dot)
    halos[1].wait()
    fill_far(r.windows.at[1], far_w, r.table, rows, dot)
    r.pooled[...] = jnp.zeros(r.pooled.shape, F32)

    def second_pass(step, carry):
        node_block(r, step, True)
        return carry

    lax.fori_loop(0, steps, second_pass, 0)
    r.windows[2, own, :] = feed_forward(r, r.pooled[...], r.windows[1, own, :].astype(F32)).astype(BF16)

    halos[2].start()
    normed_keep.start()
    normed_gather[0].start()
    for ref in (r.ge_norm, r.ge_first, r.ge_second, r.ge_third, r.g_second, r.g_first, r.g_bias):
        ref[...] = jnp.zeros(ref.shape, F32)
    e_own, e_far = r.e_first_t[:, pl.ds(0, width)], r.e_first_t[:, pl.ds(width, width)]
    fill_own(r.windows.at[2], e_far, e_own, r.eb_one, r.e_table, rows, dot_t)
    halos[2].wait()
    fill_far(r.windows.at[2], e_far, r.e_table, rows, dot_t)
    state_keep = pltpu.make_async_copy(
        r.windows.at[
            2,
            pl.ds(pl.multiple_of(REACH - half * rows, 16), rows_dev),
            pl.ds(pl.multiple_of(half * (width // CORES), width // CORES), width // CORES),
        ],
        r.state_out,
        r.keep_sem.at[5],
    )
    state_keep.start()

    def loop(count, body, events=None):
        def one(step, carry):
            body(step)
            for when, actions in (events or {}).items():

                @pl.when(step == when)
                def _():
                    for act in actions:
                        act()

            return carry

        lax.fori_loop(0, count, one, 0)

    loop(
        steps,
        lambda step: edge_block(r, step, features),
        {0: (normed_keep.wait, normed_gather[0].wait, normed_gather[1].start)},
    )
    edge_returns.start()
    edges_keep.start()
    normed_gather[1].wait()
    normed_gather[2].start()
    own_spread = r.ge_first[pl.ds(places, rows), :]
    r.ge_own[...] = t_dot(own_spread.astype(BF16), r.windows[2, own, :])
    r.ge_far[...] = t_dot(r.ge_first[pl.ds(0, places), :].astype(BF16), r.windows[2])
    pack_edge(r, r.pack.edge)
    edge.send_pair()
    edges_pair.start()
    r.e_own_back[...] = dot_wide(own_spread, e_own)

    outs = [(r.g_expand, r.expand_out), (r.g_reduce, r.reduce_out)] + list(zip(r.gathered, r.sums_out))
    stores = [pltpu.make_async_copy(*pair, r.keep_sem.at[8 + at]) for at, pair in enumerate(outs)]
    expand_store, reduce_store = stores[:2]
    sum_stores = dict(zip(sums, stores[2:]))

    def move(chunk, at):
        if at == 0:
            chunk.add_pair()
            chunk.start(0)
        elif at < 3:
            chunk.finish(at - 1)
            chunk.start(at)
        elif at == 3:
            chunk.finish(2)
            chunk.start_back(0)
        elif at < 6:
            chunk.finish_back(at - 4)
            chunk.start_back(at - 3)
        else:
            chunk.finish_back(2)
            sum_stores[chunk].start()

    def ahead(groups, at):
        groups[at].wait()
        if at + 1 < len(groups):
            groups[at + 1].start()

    def moves(*pairs):
        for chunk, at in pairs:
            (move if isinstance(chunk, ChipSum) else ahead)(chunk, at)

    def events(*pairs):
        return (functools.partial(moves, *pairs),)

    moves((edge, 0))
    edge_returns.finish(r.edge_total)

    def send_ds():
        ds_keep.start()
        ds_gather[0].start()

    node_grad(r, r.cot_rows[...], r.edge_total[...], send_ds)
    pack_third(r, r.pack.third)
    third.send_pair()
    loop(steps, lambda step: first_grad_block(r, step, features), {0: events((third, 0))})
    node_returns.start()
    moves((normed_gather, 2))
    own_spread = r.g_first[pl.ds(places, rows), :]
    g_own = t_dot(r.windows[1, own, :], own_spread.astype(BF16))
    g_far = t_dot(r.windows[1], r.g_first[pl.ds(0, places), :].astype(BF16))
    pack_first(r, (r.pack.first_a, r.pack.first_b), g_own, g_far, features, small_rows(r, places))
    first_a.send_pair()
    first_b.send_pair()
    moves((edge, 1))
    ds_keep.wait()
    moves((ds_gather, 0))
    own_back = r.du[...] + dot_wide(own_spread, own_w, True)
    loop(steps, lambda step: second_grad_block(r, step, features), {0: events((third, 1))})
    moves((normed_gather, 3), (first_a, 0))
    pack_second(r, r.pack.second)
    second.send_pair()
    grads_keep.start()
    moves((first_b, 0))
    grads_pair.start()
    node_returns.finish(r.node_total)
    fed = own_back + dot_wide(r.node_total[...], far_w, True)
    for part in range(CORES):
        r.fed_grad[part] = fed[:, part * (width // CORES) : (part + 1) * (width // CORES)]
    fed_keep.start()
    fed_pair.start()

    blocks = r.expand.shape[1] // WIDE
    chunk = r.normed_all.shape[0]
    chunks = 2 * span // chunk
    waiting = events((second, 0), (ds_gather, 1), (edge, 2), (third, 2)), events((first_b, 1))
    until_ds = (
        (second, 1), (first_a, 1), (third, 3), (ds_gather, 2), (edge, 3), (first_b, 2), (second, 2), (first_a, 2),
        (third, 4), (edge, 4), (ds_gather, 3),
    )
    beside = {
        0: events((second, 3)),
        1: events((first_a, 3), (first_b, 3)),
        2: events((third, 5)),
        3: events((second, 4)) + (reduce_store.start,),
        4: events((first_a, 4), (edge, 5)),
        5: events((first_b, 4)),
        6: events((third, 6), (first_a, 5)),
        7: events((second, 5), (edge, 6), (first_b, 5)),
    }

    def fetch(slots, target, sem, at=0):
        return pltpu.make_async_copy(slots.at[pl.ds(at * chunk, chunk)], target, r.keep_sem.at[sem])

    if chunks == 1:
        normed_fetch = fetch(r.normed_slots, r.normed_all, 6)
        normed_fetch.start()
        normed_fetch.wait()
        loop(EARLY_WIDE, lambda step: WideBlock(r, step, half).keep(), {1: waiting[0], 4: waiting[1]})
        moves(*until_ds)
        ds_fetch = fetch(r.ds_slots, r.ds_all, 7)
        ds_fetch.start()
        ds_fetch.wait()
        loop(EARLY_WIDE, lambda step: WideBlock(r, step, half).from_kept(), beside)
        last = {at - EARLY_WIDE: actions for at, actions in beside.items() if at >= EARLY_WIDE}
        loop(blocks - EARLY_WIDE, lambda step: WideBlock(r, step + EARLY_WIDE, half).whole(True), last)
    else:
        for actions in waiting:
            for act in actions:
                act()
        moves(*until_ds)
        for at in range(chunks):
            fetches = [fetch(r.normed_slots, r.normed_all, 6, at), fetch(r.ds_slots, r.ds_all, 7, at)]
            for copy in fetches:
                copy.start()
            for copy in fetches:
                copy.wait()
            loop(blocks, lambda step: WideBlock(r, step, half).whole(at == 0))
        for actions in beside.values():
            for act in actions:
                act()
    expand_store.start()
    for group in (edges_pair, grads_pair, fed_pair):
        group.wait()
    for copy in (edges_keep, grads_keep, fed_keep, state_keep):
        copy.wait()
    moves((second, 6), (first_b, 6), (first_a, 6))
    for store in stores:
        store.wait()


def shape(dims, kind):
    return jax.ShapeDtypeStruct(dims, kind)


def run(vectors, arrays):
    count = lax.axis_size("res")
    rows_dev, width = arrays.nodes.shape
    slots, _, features = arrays.edges.shape
    hidden = arrays.second_in.shape[0]
    inner = arrays.expand_in.shape[1]
    rows = rows_dev // CORES
    places = rows + 2 * REACH
    total = rows * slots
    each = slots // CORES
    tall = arrays.first_in.shape[0]
    chunks = chunk_rows(count, width, hidden, features)
    side, deep = chip_dims(count)
    everyone = CORES * count * rows
    chunk = everyone if everyone <= 16 * rows_dev else 8 * rows_dev
    wide_kind = BF16 if chunk == everyone else F32
    outs = (
        shape((rows_dev, width // CORES), BF16),
        shape((each, rows_dev, features), BF16),
        shape((rows_dev, width // CORES), F32),
        shape((each, rows_dev, features), BF16),
        shape((width // CORES, inner), wide_kind),
        shape((inner // CORES, width), wide_kind),
        shape((everyone, width), BF16),
        shape((everyone, width), BF16),
    ) + tuple(shape((size, LANE), BF16) for size in chunks)
    peers = 2 * (side - 1) + deep - 1
    remote = len(chunks) * (2 * peers + 1) + 2 * (peers + 1) + 3
    scratch = dict(
        windows=((3, places, width), BF16),
        neighbours_raw=((slots, rows_dev), jnp.int32),
        picks=((slots, 1, rows_dev), F32),
        counts=((rows, LANE), F32),
        bias_wide=((inner // WIDE, WIDE), F32),
        diagonal=((rows, CHAIN * rows), F32),
        lane_slot=((8, CHAIN * rows), F32),
        first=((tall, hidden), BF16),
        second_w=((hidden, hidden), BF16),
        third=((hidden, width), BF16),
        expand=((width, inner), BF16),
        reduce=((inner, width), BF16),
        e_first_t=((features, tall), BF16),
        e_second_w=((features, features), BF16),
        e_third_w=((features, features), BF16),
        edges_raw=((slots, rows, features), BF16),
        cots_raw=((slots, rows, features), BF16),
        cot_rows=((rows, width), BF16),
        onehot=((slots, rows, LANES), BF16),
        table=((LANES + features, hidden), BF16),
        e_table=((LANES + features, features), BF16),
        kept=((3 * total, hidden), BF16),
        pooled=((rows, hidden), F32),
        summed=((rows, width), F32),
        second=((rows, width), F32),
        pre_expand=((rows, inner), F32),
        normed=((rows, width), BF16),
        edge_out=((slots, rows, features), BF16),
        edge_grad=((slots, rows, features), F32),
        ge_norm=((8, features), F32),
        ge_first=((LANES + features, features), F32),
        ge_second=((features, features), F32),
        ge_third=((features, features), F32),
        ge_own=((features, width), F32),
        ge_far=((features, width), F32),
        e_own_back=((rows, width), F32),
        edge_landing=((places, features), F32),
        edge_total=((rows, features), F32),
        ds=((rows, width), BF16),
        du=((rows, width), F32),
        dm=((rows, width), BF16),
        slot_grad=((rows, hidden), F32),
        small=((16, width), F32),
        g_second=((hidden, hidden), F32),
        g_first=((LANES + features, hidden), F32),
        g_bias=((1, hidden), F32),
        node_landing=((places, hidden), F32),
        node_total=((rows, hidden), F32),
        fed_grad=((CORES, rows, width // CORES), F32),
        normed_all=((chunk, width), BF16),
        ds_all=((chunk, width), BF16),
        g_expand=((width // CORES, inner), wide_kind),
        g_reduce=((inner // CORES, width), wide_kind),
    )
    packed = [(CORES, size, LANE) for size in chunks] + [(size, LANE) for size in chunks] * 3
    sems = dict(load_sem=13, keep_sem=15, line_send=20, line_recv=20, step_send=remote, step_recv=remote)
    for name, size in sems.items():
        scratch[name] = pltpu.SemaphoreType.DMA((size,))
    anywhere = pl.BlockSpec(memory_space=pl.ANY)
    return pl.pallas_call(
        functools.partial(kernel, tuple(scratch), features),
        out_shape=outs,
        in_specs=[pl.BlockSpec(memory_space=pltpu.VMEM)] * len(vectors) + [anywhere] * len(arrays),
        out_specs=(anywhere,) * len(outs),
        scratch_shapes=[pltpu.VMEM(*kind) if isinstance(kind, tuple) else kind for kind in scratch.values()]
        + [pltpu.VMEM(dims, BF16) for dims in packed],
        compiler_params=pltpu.CompilerParams(
            collective_id=1, has_side_effects=True, vmem_limit_bytes=VMEM
        ),
        name="graph_layer",
    )(*vectors, *arrays)


class Moved(NamedTuple):
    grads: Any
    expand: Any
    reduce: Any
    edges: Any
    state: Any
    fed: Any


class Grads(NamedTuple):
    third_g: Any
    e_first: Any
    e_second: Any
    e_third: Any
    second_g: Any
    first_g: Any


class Biases(NamedTuple):
    b_one: Any
    b_two: Any
    b_three: Any
    gain_one: Any
    shift_one: Any
    b_expand: Any
    b_reduce: Any
    gain_two: Any
    shift_two: Any
    eb_one: Any
    eb_two: Any
    eb_three: Any
    e_gain: Any
    e_shift: Any


def finish_kernel(width, hidden, features, inner, *refs):
    refs = list(refs)
    take = lambda kind: kind(*(refs.pop(0) for _ in kind._fields))
    moved_in, packed_in = take(Moved), take(Chunks)
    moved_out, grads_out, biases = take(Moved), take(Grads), take(Biases)
    r, g, via, ready = take(Chunks), take(Grads), take(Moved), take(Moved)
    sem, move_sem = refs
    half = lax.axis_index("half")
    wide = width // LANE
    tall = (2 * width + features) // CORES
    copy = pltpu.make_async_copy
    fetches = [copy(*pair, sem.at[at]) for at, pair in enumerate(zip(moved_in, via))]
    moves = [
        copy(a if a.dtype == c.dtype else b, c, move_sem.at[at]) for at, (a, b, c) in enumerate(zip(via, ready, moved_out))
    ]
    first = len(fetches)
    loads = Chunks(*(copy(*pair, sem.at[first + at]) for at, pair in enumerate(zip(packed_in, r))))
    first += len(loads)
    stores = Grads(*(copy(*pair, sem.at[first + at]) for at, pair in enumerate(zip(g, grads_out))))
    for load in loads:
        load.start()
    for fetch in fetches:
        fetch.start()

    def move_on(at):
        fetches[at].wait()
        if via[at].dtype != ready[at].dtype:
            ready[at][...] = via[at][...].astype(ready[at].dtype)
        moves[at].start()

    loads.third.wait()
    g.third_g[...], _ = take_wide(r.third, 0, hidden // CORES, wide)
    stores.third_g.start()
    loads.edge.wait()
    e_whole, at = take_wide(r.edge, 0, features, up(tall, LANE) // LANE)
    g.e_first[...] = e_whole[:, :tall]
    rest = features - LANE
    part = features // CORES
    left_two, at = take_wide(r.edge, at, part, 1)
    left_three, at = take_wide(r.edge, at, part, 1)
    right, at = take_wide(r.edge, at, part, 1)
    g.e_second[...] = jnp.concatenate([left_two, right[:, :rest]], 1)
    g.e_third[...] = jnp.concatenate([left_three, right[:, rest:]], 1)
    for store in (stores.e_first, stores.e_second, stores.e_third):
        store.start()
    for at in range(2):
        move_on(at)
    loads.second.wait()
    g.second_g[...], _ = take_wide(r.second, 0, hidden // CORES, wide)
    stores.second_g.start()
    for at in range(2, len(fetches)):
        move_on(at)
    loads.first_a.wait()
    g.first_g[:, : hidden // 2], _ = take_wide(r.first_a, 0, tall, wide // 2)
    loads.first_b.wait()
    g.first_g[:, hidden // 2 :], at = take_wide(r.first_b, 0, tall, wide // 2)
    stores.first_g.start()
    small, _ = take_wide(r.first_b, at, 16, wide)

    def share(target, row):
        size = target.shape[0]
        target[...] = jnp.where(half == 0, row[:, :size], row[:, size : 2 * size]).reshape(size)

    b = biases
    for target, at in (
        (b.b_one, 0), (b.b_two, 1), (b.b_three, 2), (b.gain_one, 3), (b.shift_one, 4), (b.b_reduce, 9),
        (b.gain_two, 10), (b.shift_two, 11),
    ):
        share(target, small[at : at + 1])
    share(b.b_expand, jnp.concatenate([small[5 + p : 6 + p] for p in range(inner // width)], 1))
    share(b.eb_one, small[12:13, :LANES])
    share(b.eb_two, small[12:13, LANES:])
    share(b.eb_three, small[13:14, :LANES])
    share(b.e_gain, small[13:14, LANES:])
    share(b.e_shift, small[14:15, :LANES])
    for store in moves + list(stores):
        store.wait()


def finish(moved, sums, width, hidden, features, inner):
    tall = (2 * width + features) // CORES
    part = features // CORES
    grads = Grads(
        third_g=(hidden // CORES, width),
        e_first=(features, tall),
        e_second=(part, features),
        e_third=(part, features),
        second_g=(hidden // CORES, hidden),
        first_g=(tall, hidden),
    )
    sizes = Biases(hidden, hidden, width, width, width, inner, width, width, width, *[features] * 5)
    anywhere, vmem = pl.BlockSpec(memory_space=pl.ANY), pl.BlockSpec(memory_space=pltpu.VMEM)
    kinds = Moved(F32, F32, F32, BF16, BF16, F32)
    outs = [shape(a.shape, kind) for a, kind in zip(moved, kinds)]
    outs += [shape(dims, F32) for dims in grads]
    outs += [shape((size // CORES,), F32) for size in sizes]
    got = pl.pallas_call(
        functools.partial(finish_kernel, width, hidden, features, inner),
        out_shape=outs,
        in_specs=[anywhere] * (len(moved) + len(sums)),
        out_specs=[anywhere] * (len(moved) + len(grads)) + [vmem] * len(sizes),
        scratch_shapes=[pltpu.VMEM(a.shape, BF16) for a in sums]
        + [pltpu.VMEM(dims, F32) for dims in grads]
        + [pltpu.VMEM(a.shape, a.dtype) for a in moved]
        + [pltpu.VMEM(a.shape if a.dtype != kind else (16, LANE), kind) for a, kind in zip(moved, kinds)]
        + [pltpu.SemaphoreType.DMA((len(moved) + len(sums) + len(grads),)), pltpu.SemaphoreType.DMA((len(moved),))],
        compiler_params=pltpu.CompilerParams(vmem_limit_bytes=VMEM),
        name="finish",
    )(*moved, *sums)
    first = len(moved) + len(grads)
    return Moved(*got[: len(moved)]), Grads(*got[len(moved) : first]), Biases(*got[first:])


def body(
    nodes, edges, neighbours, counts,
    message_first, message_first_bias, message_second, message_second_bias, message_third, message_third_bias,
    node_norm_gain, node_norm_shift, expand_weight, expand_bias, reduce_weight, reduce_bias,
    output_norm_gain, output_norm_shift,
    edge_first, edge_first_bias, edge_second, edge_second_bias, edge_third, edge_third_bias,
    edge_norm_gain, edge_norm_shift, cot_nodes, cot_edges,
):
    width, features = nodes.shape[1], edges.shape[2]
    hidden, inner = message_second.shape[0], expand_weight.shape[1]

    by_slots = lambda values: jnp.transpose(values, (1, 0, 2))
    vectors = Vectors(
        message_first_bias, message_second_bias, message_third_bias, node_norm_gain, node_norm_shift, reduce_bias,
        output_norm_gain, output_norm_shift, expand_bias, edge_first_bias, edge_second_bias, edge_third_bias,
        edge_norm_gain, edge_norm_shift, counts,
    )
    arrays = Arrays(
        nodes, by_slots(edges), neighbours.T, message_first, message_second, message_third, expand_weight,
        reduce_weight, edge_first.T, edge_second, edge_third, cot_nodes, by_slots(cot_edges),
    )
    state, out, fed_grad, edge_grad, g_expand, g_reduce, _, _, *sums = run(vectors, arrays)
    moved = Moved(edge_grad, g_expand, g_reduce, out, state, fed_grad)
    m, g, b = finish(moved, sums, width, hidden, features, inner)
    return (
        m.state, by_slots(m.edges), m.fed, by_slots(m.grads),
        g.first_g, b.b_one, g.second_g, b.b_two, g.third_g, b.b_three, b.gain_one, b.shift_one,
        m.expand, b.b_expand, m.reduce, b.b_reduce, b.gain_two, b.shift_two,
        g.e_first.T, b.eb_one, g.e_second, b.eb_two, g.e_third, b.eb_three, b.e_gain, b.e_shift,
    )


def solution(mesh):
    rows, slots = P("res", None), P("res", None, None)
    copied = P()
    down, vec = P("half", None), P("half")
    return jax.shard_map(
        body,
        mesh=mesh,
        in_specs=(rows, slots, rows, P("res")) + (copied,) * 22 + (rows, slots),
        out_specs=(
            P("res", "half"),
            P("res", "half", None),
            P("res", "half"),
            P("res", "half", None),
            down, vec, down, vec, down, vec, vec, vec, down, vec, down, vec, vec, vec,
            down, vec, down, vec, down, vec, vec, vec,
        ),
        check_vma=False,
    )
```

```python
import functools
import types
from typing import Any, NamedTuple

import jax
import jax.numpy as jnp
from jax import lax
from jax.experimental import pallas as pl
from jax.experimental.pallas import tpu as pltpu
from jax.sharding import PartitionSpec as P

EPSILON = 1e-05
REACH = 64
CORES = 2
NEAR = 0.7978845608
CUBE = 0.044715
STEP = 30
CHAIN = 5
BACK_CHAIN = 15
EDGE_CHAIN = 15
EARLY_WIDE = 6
PARTS = 2
LANES = 256
LANE = 128
WIDE = 256
VMEM = 62 * 2**20
MESH = pl.DeviceIdType.MESH
F32 = jnp.float32
BF16 = jnp.bfloat16


def dot(left, right):
    return jnp.dot(left, right, preferred_element_type=F32)


def dot_t(left, right):
    return lax.dot_general(left, right, (((1,), (1,)), ((), ())), preferred_element_type=F32)


def t_dot(left, right):
    return lax.dot_general(left, right, (((0,), (0,)), ((), ())), preferred_element_type=F32)


def two_parts(values):
    high = values.astype(BF16)
    return high, (values - high.astype(F32)).astype(BF16)


def dot_wide(values, right, transposed=False):
    rows = values.shape[0]
    both = (dot_t if transposed else dot)(jnp.concatenate(two_parts(values), 0), right)
    return both[:rows] + both[rows:]


def gelu(values):
    kind = values.dtype.type
    square = values * values
    bend = jnp.tanh(values * (kind(NEAR) + kind(NEAR * CUBE) * square))
    return values * (kind(0.5) + kind(0.5) * bend)


def gelu_slope(values):
    square = values * values
    part = 0.5 + 0.5 * jnp.tanh(values * (NEAR + (NEAR * CUBE) * square))
    return part + values * part * (1.0 - part) * (2.0 * NEAR + (6.0 * NEAR * CUBE) * square)


def gelu_and_slope(values):
    values = values.astype(BF16)
    square = values * values
    part = BF16(0.5) + BF16(0.5) * jnp.tanh(values * (BF16(NEAR) + BF16(NEAR * CUBE) * square))
    act = values * part
    slope = part + act * (1 - part) * (BF16(2.0 * NEAR) + BF16(6.0 * NEAR * CUBE) * square)
    return act, slope


def norm_parts(values):
    centered = values - jnp.mean(values, -1, keepdims=True)
    scale = lax.rsqrt(jnp.mean(centered * centered, -1, keepdims=True) + EPSILON)
    return centered * scale, scale


def norm_back(grad, unit, scale, gain):
    scaled = gain * grad
    flat = jnp.mean(scaled, -1, keepdims=True)
    slant = jnp.mean(scaled * unit, -1, keepdims=True)
    return (scaled - flat - unit * slant) * scale


def col_sum(values):
    return jnp.sum(values, 0, keepdims=True)


def iota(dims, axis):
    return lax.broadcasted_iota(jnp.int32, dims, axis)


def chip_dims(count):
    side = 1
    while 2 * (2 * side) ** 3 <= count and count % (4 * side * side) == 0:
        side *= 2
    return side, count // (side * side)


def up(size, unit):
    return -(-size // unit) * unit


class Chunks(NamedTuple):
    edge: Any
    third: Any
    first_a: Any
    first_b: Any
    second: Any


ORDERS = Chunks((0, 2, 1), (0, 1, 2), (2, 0, 1), (0, 1, 2), (0, 2, 1))


def chunk_rows(count, width, hidden, features):
    tall = (2 * width + features) // CORES
    wide = width // LANE
    edge = features * (up(tall, LANE) // LANE) + 3 * (features // CORES)
    square = (hidden // CORES) * wide
    first = tall * (wide // 2)
    sizes = (edge, square, first, first + 16 * wide, square)
    return Chunks(*(up(rows, 16 * count) for rows in sizes))


def cut(pieces, start, stop):
    at, got = 0, []
    for piece in pieces:
        low, high = max(start, at), min(stop, at + piece.shape[0])
        if low < high:
            got.append(piece[low - at : high - at])
        at += piece.shape[0]
    return jnp.concatenate(got, 0) if len(got) > 1 else got[0]


def put_wide(pack, half, at, piece):
    rows = piece.shape[0]
    for block in range(piece.shape[1] // LANE):
        pack[half, pl.ds(at, rows), :] = piece[:, block * LANE : (block + 1) * LANE].astype(BF16)
        at += rows
    return at


def put_rest(pack, at):
    rest = pack.shape[1] - at
    if rest:
        for half in range(CORES):
            pack[half, pl.ds(at, rest), :] = jnp.zeros((rest, LANE), BF16)


def take_wide(packed, at, rows, blocks):
    pieces = [packed[pl.ds(at + b * rows, rows), :] for b in range(blocks)]
    return jnp.concatenate(pieces, 1).astype(F32), at + blocks * rows


class Copies:
    def __init__(self, send, recv):
        self.send, self.recv, self.used = send, recv, 0

    def group(self, entries):
        made = []
        for source, target, device in entries:
            at = self.used
            self.used += 1
            made.append(functools.partial(self._make, source, target, device, at))
        return Group(made)

    def _make(self, source, target, device, at):
        return pltpu.make_async_remote_copy(
            src_ref=source,
            dst_ref=target,
            send_sem=self.send.at[at],
            recv_sem=self.recv.at[at],
            device_id=device,
            device_id_type=MESH,
        )


class Group:
    def __init__(self, made):
        self.made = made

    def start(self):
        for make in self.made:
            make().start()

    def wait(self):
        for make in self.made:
            make().wait()


class Place:
    def __init__(self):
        res, half, count = lax.axis_index("res"), lax.axis_index("half"), lax.axis_size("res")
        side, deep = chip_dims(count)
        x, y, z = lax.rem(res, side), lax.rem(res // side, side), res // (side * side)
        first = half == 0
        self.res, self.half, self.count = res, half, count
        self.dims = (side, side, deep)
        self.at = (jnp.where(first, x, y), jnp.where(first, y, x), z)
        self.strides = (jnp.where(first, 1, side), jnp.where(first, side, 1), side * side)
        self.partner = (res, 1 - half)

    def peers(self, level):
        size, here = self.dims[level], self.at[level]
        found = []
        for ahead in range(1, size):
            to = lax.rem(here + ahead, size)
            found.append((to, (self.res + (to - here) * self.strides[level], self.half)))
        return found

    def line(self):
        res, half, count = self.res, self.half, self.count
        return (
            (res > 0, (res - 1, half)),
            (res + half > 0, (res - 1 + half, 1 - half)),
            (res + half < count, (res + half, 1 - half)),
            (res < count - 1, (res + 1, half)),
        )

    def line_count(self):
        res, half, count = self.res, self.half, self.count
        return 4 - jnp.where(res > 0, 0, 2 - half) - jnp.where(res < count - 1, 0, 1 + half)


def greet(place):
    barrier = pltpu.get_barrier_semaphore()

    def signal(device):
        pl.semaphore_signal(barrier, inc=1, device_id=device, device_id_type=MESH)

    for exists, device in place.line():
        pl.when(exists)(functools.partial(signal, device))
    signal(place.partner)
    others = 1
    for level in range(3):
        for _, device in place.peers(level):
            signal(device)
            others += 1
    pl.semaphore_wait(barrier, others + place.line_count())


def halo_layout(rows):
    edge = REACH - rows
    return ((0, edge), (edge, rows), (REACH + rows, rows), (REACH + 2 * rows, edge))


class Halo:
    def __init__(self, place, window, rows, send, recv, first):
        self.place, self.window, self.rows = place, window, rows
        self.send, self.recv, self.first = send, recv, first

    def clear(self):
        for (exists, _), (offset, size) in zip(self.place.line(), halo_layout(self.rows)):

            @pl.when(jnp.logical_not(exists))
            def _():
                self.window[pl.ds(offset, size), :] = jnp.zeros((size, self.window.shape[1]), self.window.dtype)

    def _copy(self, at, device):
        offset, size = halo_layout(self.rows)[3 - at]
        first = REACH + (self.rows - size if at == 3 else 0)
        return pltpu.make_async_remote_copy(
            src_ref=self.window.at[pl.ds(first, size)],
            dst_ref=self.window.at[pl.ds(offset, size)],
            send_sem=self.send.at[self.first + at],
            recv_sem=self.recv.at[self.first + 3 - at],
            device_id=device,
            device_id_type=MESH,
        )

    def start(self):
        for at, (exists, device) in enumerate(self.place.line()):

            @pl.when(exists)
            def _():
                self._copy(at, device).start()

    def wait(self):
        for at, (exists, device) in enumerate(self.place.line()):
            offset, size = halo_layout(self.rows)[at]

            @pl.when(exists)
            def _():
                self._copy(at, device).wait_send()
                pltpu.make_async_remote_copy(
                    src_ref=self.window.at[pl.ds(offset, size)],
                    dst_ref=self.window.at[pl.ds(offset, size)],
                    send_sem=self.send.at[self.first + at],
                    recv_sem=self.recv.at[self.first + at],
                    device_id=device,
                    device_id_type=MESH,
                ).wait_recv()


class Returns:
    def __init__(self, place, table, outgoing, landing, rows, send, recv, first):
        self.place, self.table, self.landing, self.rows = place, table, landing, rows
        self.outgoing = outgoing
        self.send, self.recv, self.first = send, recv, first

    def _copy(self, at, device):
        layout = halo_layout(self.rows)
        offset, size = layout[at]
        return pltpu.make_async_remote_copy(
            src_ref=self.outgoing.at[pl.ds(offset, size)],
            dst_ref=self.landing.at[pl.ds(layout[3 - at][0], size)],
            send_sem=self.send.at[self.first + at],
            recv_sem=self.recv.at[self.first + 3 - at],
            device_id=device,
            device_id_type=MESH,
        )

    def start(self):
        self.outgoing[...] = self.table[pl.ds(0, self.outgoing.shape[0]), :].astype(BF16)
        for at, (exists, device) in enumerate(self.place.line()):

            @pl.when(exists)
            def _():
                self._copy(at, device).start()

    def finish(self, total):
        total[...] = self.table[pl.ds(REACH, self.rows), :]
        for at, (exists, device) in enumerate(self.place.line()):
            offset, size = halo_layout(self.rows)[at]
            first = self.rows - size if at == 3 else 0

            @pl.when(exists)
            def _():
                self._copy(at, device).wait_send()
                pltpu.make_async_remote_copy(
                    src_ref=self.outgoing.at[pl.ds(offset, size)],
                    dst_ref=self.landing.at[pl.ds(offset, size)],
                    send_sem=self.send.at[self.first + at],
                    recv_sem=self.recv.at[self.first + at],
                    device_id=device,
                    device_id_type=MESH,
                ).wait_recv()
                total[pl.ds(first, size), :] += self.landing[pl.ds(offset, size), :].astype(F32)


def gather_groups(place, copies, ref, unit, source=None, base=0):
    mine = (place.at[0] * place.dims[1] + place.at[1]) * place.dims[2] + place.at[2]
    groups, size = [], unit
    start = mine * unit
    for level in (2, 1, 0):
        here = ref.at[pl.ds(pl.multiple_of(base + start, 16), size)]
        from_ref = here if source is None or level < 2 else source
        groups.append(copies.group([(from_ref, here, device) for _, device in place.peers(level)]))
        start = start - place.at[level] * size
        size = size * place.dims[level]
    return groups


class ChipSum:
    def __init__(self, place, copies, order, pack, got, landed, gathered, out, keep_sem):
        self.place, self.pack, self.got, self.landed, self.gathered = place, pack, got, landed, gathered
        half, size = place.half, pack.shape[1]
        self.pair = copies.group([(pack.at[1 - half], got, place.partner)])
        self.steps, self.shares, self.back = [], [], []
        start, base = 0, 0
        for level in order:
            share = size // place.dims[level]
            entries, lands = [], []
            for to, device in place.peers(level):
                source = pack.at[half, pl.ds(pl.multiple_of(start + to * share, 16), share)]
                entries.append((source, landed.at[pl.ds(base, share)], device))
                lands.append(base)
                base += share
            start = pl.multiple_of(start + place.at[level] * share, 16)
            size = share
            self.steps.append(copies.group(entries))
            self.shares.append((start, share, lands))
            here = gathered.at[pl.ds(start, share)]
            there = here if self.back else out.at[pl.ds(start, share)]
            back = [(here, there, device) for _, device in place.peers(level)]
            self.back.insert(0, copies.group(back))
            if there is not here:
                self.keep = pltpu.make_async_copy(here, there, keep_sem)

    def send_pair(self):
        self.pair.start()

    def add_pair(self):
        self.pair.wait()
        half = self.place.half
        self.pack[half] = (self.pack[half].astype(F32) + self.got[...].astype(F32)).astype(BF16)

    def start(self, level):
        self.steps[level].start()

    def finish(self, level):
        self.steps[level].wait()
        start, share, lands = self.shares[level]
        half = self.place.half
        total = self.pack[half, pl.ds(start, share), :].astype(F32)
        for base in lands:
            total = total + self.landed[pl.ds(base, share), :].astype(F32)
        if level < len(self.steps) - 1:
            self.pack[half, pl.ds(start, share), :] = total.astype(BF16)
        else:
            self.gathered[pl.ds(start, share), :] = total.astype(BF16)

    def start_back(self, step):
        self.back[step].start()
        if step == len(self.back) - 1:
            self.keep.start()

    def finish_back(self, step):
        self.back[step].wait()
        if step == len(self.back) - 1:
            self.keep.wait()


def flat(values):
    return values.reshape(values.shape[0] * values.shape[1], values.shape[2])


def feed_forward(r, pooled, own):
    width = own.shape[1]
    mean = pooled / r.counts[:, 0:1]
    summed = own + dot_wide(mean, r.third[...]) + r.b_three
    unit, _ = norm_parts(summed)
    normed = unit * r.gain_one + r.shift_one
    low = normed.astype(BF16)
    pre = dot(low, r.expand[...]) + r.b_expand
    second = normed + dot(gelu(pre).astype(BF16), r.reduce[...]) + r.b_reduce
    unit_two, _ = norm_parts(second)
    r.summed[...] = summed
    r.pre_expand[...] = pre
    r.second[...] = second
    r.normed[...] = low
    return unit_two * r.gain_two + r.shift_two


def fill_own(window, far, own, bias, table, rows, multiply):
    here = pl.ds(REACH, rows)
    table[here, :] = multiply(window[here, :], far).astype(BF16)
    table[pl.ds(window.shape[0], rows), :] = (multiply(window[here, :], own) + bias).astype(BF16)


def fill_far(window, far, table, rows, multiply):
    for here in (pl.ds(0, REACH), pl.ds(REACH + rows, REACH)):
        table[here, :] = multiply(window[here, :], far).astype(BF16)


def chain_parts(step):
    return [step * STEP + part * CHAIN for part in range(STEP // CHAIN)]


def chain_rows(r, slot):
    rows = r.counts.shape[0]
    return pl.ds(pl.multiple_of(slot * rows, CHAIN * rows), CHAIN * rows)


def step_rows(r, step):
    rows = r.counts.shape[0]
    return pl.ds(pl.multiple_of(step * (STEP * rows), STEP * rows), STEP * rows)


def build_block(r, step, half, places):
    rows = r.counts.shape[0]
    here = pl.ds(step * STEP, STEP)
    named = r.picks[here]
    dims = (STEP, rows, named.shape[2])
    spread = jnp.broadcast_to(named, dims)
    mine = iota(dims, 2) == iota(dims, 1) + half * rows
    pick = jnp.sum(jnp.where(mine, spread, 0.0), -1, keepdims=True)
    dims = (STEP, rows, LANES)
    lane = iota(dims, 2)
    hit = (lane.astype(F32) == pick) | (lane == iota(dims, 1) + places)
    r.onehot[here] = jnp.where(hit, 1.0, 0.0).astype(BF16)


def joined_rows(r, slot, slots):
    here = pl.ds(slot, slots)
    return jnp.concatenate([flat(r.onehot[here]), flat(r.edges_raw[here])], 1)


def live_rows(r, slot, width):
    count = r.counts[...]
    dims = (CHAIN,) + count.shape
    live = jnp.where(iota(dims, 0) + slot < count[None], 1.0, 0.0)
    return flat(jnp.concatenate([live] * (width // LANE), -1))


def live_column(r, slot, slots):
    count = r.counts[...]
    dims = (slots,) + count.shape
    return flat(jnp.where(iota(dims, 0) + slot < count[None], 1.0, 0.0))[:, 0:1]


def node_block(r, step, keep):
    rows = r.counts.shape[0]
    hidden = r.second_w.shape[0]
    slots = chain_parts(step)
    dims = (rows, CHAIN * rows)
    count = jnp.broadcast_to(r.counts[:, 0:1], dims)
    pre = [dot(joined_rows(r, slot, CHAIN), r.table[...]) for slot in slots]
    acts = []
    for slot, values in zip(slots, pre):
        if keep:
            here = chain_rows(r, slot)
            act, slope = gelu_and_slope(values)
            r.act[here, :] = act
            r.slope_one[here, :] = slope
        else:
            act = gelu(values.astype(BF16))
        acts.append(act)
    pre = [dot(act, r.second_w[...]) + r.b_two for act in acts]
    total = r.pooled[...]
    for slot, values in zip(slots, pre):
        if keep:
            act, slope = gelu_and_slope(values)
            r.slope_two[chain_rows(r, slot), :] = slope * live_rows(r, slot, hidden).astype(BF16)
        else:
            act = gelu(values.astype(BF16))
        used = jnp.where(r.lane_slot[0:1, :] + slot.astype(F32) < count, r.diagonal[...], 0.0)
        total = total + dot(used.astype(BF16), act.astype(BF16))
    r.pooled[...] = total


def edge_block(r, step, features):
    rows = r.counts.shape[0]
    split = lambda values: values.reshape(values.shape[0] // rows, rows, features)
    slots = [step * STEP + part * EDGE_CHAIN for part in range(STEP // EDGE_CHAIN)]
    each = lambda body, *lists: [body(*items) for items in zip(*lists)]
    joined = [joined_rows(r, slot, EDGE_CHAIN) for slot in slots]
    live = [live_column(r, slot, EDGE_CHAIN) for slot in slots]
    pre = each(lambda z: dot(z, r.e_table[...]), joined)
    o_one, slope_one = zip(*each(gelu_and_slope, pre))
    pre = each(lambda a: dot(a, r.e_second_w[...]) + r.eb_two, o_one)
    o_two, slope_two = zip(*each(gelu_and_slope, pre))
    summed = each(lambda z, a: z[:, LANES:].astype(F32) + (dot(a, r.e_third_w[...]) + r.eb_three), joined, o_two)
    unit, scale = zip(*each(norm_parts, summed))
    d_three, d_sums = [], []
    for slot, u, k, used in zip(slots, unit, scale, live):
        here = pl.ds(slot, EDGE_CHAIN)
        r.edge_out[here] = split((u * r.e_gain + r.e_shift) * used).astype(BF16)
        d_out = flat(r.cots_raw[here]).astype(F32) * used
        r.ge_norm[0:1, :] += col_sum(d_out * u)
        r.ge_norm[1:2, :] += col_sum(d_out)
        d_sum = norm_back(d_out, u, k, r.e_gain)
        r.ge_norm[2:3, :] += col_sum(d_sum)
        d_sums.append(d_sum)
        d_three.append(d_sum.astype(BF16))
    d_two = each(lambda d, k: dot_t(d, r.e_third_w[...]) * k, d_three, slope_two)
    r.ge_norm[3:4, :] += sum(col_sum(d) for d in d_two)
    d_two = each(lambda d: d.astype(BF16), d_two)
    d_one = each(lambda d, k: (dot_t(d, r.e_second_w[...]) * k).astype(BF16), d_two, slope_one)
    for slot, d_sum, d in zip(slots, d_sums, d_one):
        more = dot(d, r.e_first_t[:, pl.ds(2 * r.nodes_width, features)])
        r.edge_grad[pl.ds(slot, EDGE_CHAIN)] = split(d_sum + more)
    together = lambda values: jnp.concatenate(values, 0)
    r.ge_third[...] += t_dot(together(o_two), together(d_three))
    r.ge_second[...] += t_dot(together(o_one), together(d_two))
    r.ge_first[...] += t_dot(together(joined), together(d_one))


def node_grad(r, cot, far_total, when_ds):
    width = cot.shape[1]
    grad = cot.astype(F32) + r.e_own_back[...] + dot_wide(far_total, r.e_first_t[:, pl.ds(width, width)])
    unit, scale = norm_parts(r.second[...])
    dw = norm_back(grad, unit, scale, r.gain_two)
    gain_two, shift_two = col_sum(grad * unit), col_sum(grad)
    ds = dw.astype(BF16)
    r.ds[...] = ds
    when_ds()
    slope = gelu_slope(r.pre_expand[...])
    dq = (dot_t(ds, r.reduce[...]) * slope).astype(BF16)
    dv = dw + dot_t(dq, r.expand[...])
    unit, scale = norm_parts(r.summed[...])
    du = norm_back(dv, unit, scale, r.gain_one)
    r.du[...] = du
    counts = r.counts[:, 0:1]
    dm = (du / counts).astype(BF16)
    r.slot_grad[...] = dot_t(dm, r.third[...])
    r.dm[...] = dm
    small = r.small
    small[...] = jnp.zeros(small.shape, F32)
    small[2:3, :] = col_sum(counts * dm.astype(F32))
    small[3:4, :] = col_sum(dv * unit)
    small[4:5, :] = col_sum(dv)
    dq_sum = col_sum(dq.astype(F32))
    for part in range(dq_sum.shape[1] // width):
        small[5 + part : 6 + part, :] = dq_sum[:, part * width : (part + 1) * width]
    small[9:10, :] = col_sum(ds.astype(F32))
    small[10:11, :] = gain_two
    small[11:12, :] = shift_two


def put_features(pack, half, at, e_second, e_third):
    part = e_second.shape[0] // CORES
    two = [ref[pl.ds(half * part, part), :] for ref in (e_second, e_third)]
    for piece in two:
        at = put_wide(pack, half, at, piece[:, :LANE])
    return put_wide(pack, half, at, jnp.concatenate([piece[:, LANE:] for piece in two], 1))


def pack_edge(r, pack):
    features = r.ge_second.shape[0]
    g_edge = jnp.transpose(r.ge_first[pl.ds(LANES, features), :])
    e_first = jnp.concatenate([r.ge_own[...], r.ge_far[...], g_edge], 1)
    tall = e_first.shape[1] // CORES
    fill = jnp.zeros((features, up(tall, LANE) - tall), F32)
    for half in range(CORES):
        piece = jnp.concatenate([e_first[:, half * tall : (half + 1) * tall], fill], 1)
        at = put_wide(pack, half, 0, piece)
        at = put_features(pack, half, at, r.ge_second, r.ge_third)
    put_rest(pack, at)


def pack_third(r, pack):
    dm = r.dm[...]
    found = t_dot(jnp.concatenate(two_parts(r.pooled[...]), 0), jnp.concatenate([dm, dm], 0))
    part = found.shape[0] // CORES
    for half in range(CORES):
        at = put_wide(pack, half, 0, found[half * part : (half + 1) * part])
    put_rest(pack, at)


def pack_second(r, pack):
    part = r.g_second.shape[0] // CORES
    for half in range(CORES):
        at = put_wide(pack, half, 0, r.g_second[pl.ds(half * part, part), :])
    put_rest(pack, at)


def small_rows(r, places):
    rows = r.counts.shape[0]
    features = r.ge_norm.shape[1]
    fill = jnp.zeros((1, LANES - features), F32)
    own = pl.ds(places, rows)
    edge = [col_sum(r.ge_first[own, :])] + [r.ge_norm[at : at + 1, :] for at in (3, 2, 0, 1)]
    edge = [jnp.concatenate([row, fill], 1) for row in edge] + [jnp.zeros((1, LANES), F32)]
    lines = [col_sum(r.g_first[own, :]), r.g_bias[...], r.small[2:12, :]]
    lines += [jnp.concatenate(edge[at : at + 2], 1) for at in (0, 2, 4)]
    return jnp.concatenate(lines + [jnp.zeros((1, r.small.shape[1]), F32)], 0)


def pack_first(r, side, pack, window, spread, own_spread, own, features, places):
    hidden = own_spread.shape[1]
    cols = slice(side * (hidden // 2), (side + 1) * (hidden // 2))
    pieces = [
        t_dot(window[own, :], own_spread[:, cols].astype(BF16)),
        t_dot(window[...], spread[:, cols].astype(BF16)),
        r.g_first[pl.ds(LANES, features), cols],
    ]
    tall = sum(piece.shape[0] for piece in pieces) // CORES
    small = small_rows(r, places) if side == 1 else None
    for half in range(CORES):
        at = put_wide(pack, half, 0, cut(pieces, half * tall, (half + 1) * tall))
        if side == 1:
            at = put_wide(pack, half, at, small)
    put_rest(pack, at)


def first_grad_block(r, step, features):
    rows = r.counts.shape[0]
    hidden = r.act.shape[1]
    coming = jnp.broadcast_to(r.slot_grad[...][None], (BACK_CHAIN,) + r.slot_grad.shape)
    slots = [step * STEP + part * BACK_CHAIN for part in range(STEP // BACK_CHAIN)]
    places = [pl.ds(pl.multiple_of(slot * rows, BACK_CHAIN * rows), BACK_CHAIN * rows) for slot in slots]
    twos, ones = [], []
    for here in places:
        d_two = flat(coming) * r.slope_two[here, :].astype(F32)
        r.g_bias[...] += col_sum(d_two)
        twos.append(d_two.astype(BF16))
        r.slope_two[here, :] = twos[-1]
    backs = [dot_t(d_two, r.second_w[...]) for d_two in twos]
    for here, back in zip(places, backs):
        ones.append((back * r.slope_one[here, :].astype(F32)).astype(BF16))
        r.slope_one[here, :] = ones[-1]
    r.g_first[...] += t_dot(joined_rows(r, step * STEP, STEP), jnp.concatenate(ones, 0))


def second_grad_block(r, step, features):
    rows = r.counts.shape[0]
    here = step_rows(r, step)
    r.g_second[...] += t_dot(r.act[here, :], r.slope_two[here, :])
    more = dot_t(r.slope_one[here, :], r.table[pl.ds(LANES, features), :])
    there = pl.ds(step * STEP, STEP)
    r.edge_grad_low[there] = (r.edge_grad[there] + more.reshape(STEP, rows, features)).astype(BF16)


def put(target, rows, cols, found, fresh):
    target[rows, cols] = (found if fresh else target[rows, cols] + found).astype(target.dtype)


class WideBlock:
    def __init__(self, r, step, half):
        width, inner = r.expand.shape
        blocks = inner // WIDE
        self.r, self.step, self.mine = r, step, blocks // CORES
        self.block = lax.rem(step + half * self.mine, blocks)
        self.here = pl.ds(pl.multiple_of(self.block * WIDE, WIDE), WIDE)
        part = width // CORES
        self.cols = pl.ds(pl.multiple_of(half * part, part), part)
        self.total = r.normed_all.shape[0]
        size = self.total // PARTS
        self.rows = [pl.ds(at * size, size) for at in range(PARTS)]

    def forward(self):
        r = self.r
        bias = r.bias_wide[pl.ds(self.block, 1), :]
        pre = [dot(r.normed_all[rows, :], r.expand[:, self.here]) + bias for rows in self.rows]
        both = [gelu_and_slope(values) for values in pre]
        return [act for act, _ in both], [slope for _, slope in both]

    def place(self, slot, rows=None):
        size = self.total if rows is None else rows.size
        first = (slot // 2) * self.total + (0 if rows is None else rows.start)
        return self.r.kept.at[
            pl.ds(pl.multiple_of(first, 16), size), pl.ds(pl.multiple_of(lax.rem(slot, 2) * WIDE, WIDE), WIDE)
        ]

    def keep(self):
        acts, slopes = self.forward()
        for rows, slope in zip(self.rows, slopes):
            self.place(self.step, rows)[...] = slope

        @pl.when(self.step < self.mine)
        def _():
            for rows, act in zip(self.rows, acts):
                self.place(EARLY_WIDE + self.step, rows)[...] = act

    def backward(self, slopes, act, fresh):
        r = self.r
        back = [dot_t(r.ds_all[rows, :], r.reduce[self.here, :]) for rows in self.rows]
        dqs = [(grad * slope.astype(F32)).astype(BF16) for grad, slope in zip(back, slopes)]
        found = t_dot(r.normed_all[:, self.cols], jnp.concatenate(dqs, 0))
        put(r.g_expand, slice(None), self.here, found, fresh)

        @pl.when(self.step < self.mine)
        def _():
            out = pl.ds(pl.multiple_of(self.step * WIDE, WIDE), WIDE)
            found = t_dot(act(), r.ds_all[...])
            put(r.g_reduce, out, slice(None), found, fresh)

    def from_kept(self):
        slopes = [self.place(self.step, rows)[...] for rows in self.rows]
        self.backward(slopes, lambda: self.place(EARLY_WIDE + self.step)[...], True)

    def whole(self, fresh):
        acts, slopes = self.forward()
        self.backward(slopes, lambda: jnp.concatenate(acts, 0), fresh)


class Vectors(NamedTuple):
    b_one: Any
    b_two: Any
    b_three: Any
    gain_one: Any
    shift_one: Any
    b_reduce: Any
    gain_two: Any
    shift_two: Any
    b_expand: Any
    eb_one: Any
    eb_two: Any
    eb_three: Any
    e_gain: Any
    e_shift: Any
    counts_in: Any


class Arrays(NamedTuple):
    nodes: Any
    edges: Any
    neighbours: Any
    first_in: Any
    second_in: Any
    third_in: Any
    expand_in: Any
    reduce_in: Any
    e_first_in: Any
    e_second_in: Any
    e_third_in: Any
    cot_nodes: Any
    cot_edges: Any


class Results(NamedTuple):
    state_out: Any
    edges_out: Any
    fed_out: Any
    grads_out: Any
    expand_out: Any
    reduce_out: Any
    normed_slots: Any
    ds_slots: Any


def kernel(names, features, *refs):
    kinds, refs = (Vectors, Arrays, Results), list(refs)
    r = types.SimpleNamespace()
    for kind in kinds:
        for name in kind._fields:
            setattr(r, name, refs.pop(0))
    r.sums_out = Chunks(*(refs.pop(0) for _ in Chunks._fields))
    for name in names:
        setattr(r, name, refs.pop(0))
    r.pack, r.got, r.landed, r.gathered = (Chunks(*(refs.pop(0) for _ in Chunks._fields)) for _ in range(4))
    place = Place()
    res, half, count = place.res, place.half, place.count
    rows_dev, width = r.nodes.shape
    rows = rows_dev // CORES
    places = rows + 2 * REACH
    slots = r.edges.shape[0]
    each = slots // CORES
    steps = slots // STEP
    r.nodes_width = width
    total = r.edges_raw.shape[0] * rows
    r.edge_grad_low = r.cots_raw
    r.act, r.slope_one, r.slope_two = (r.kept.at[pl.ds(at * total, total)] for at in range(3))
    for name in Vectors._fields:
        vector = getattr(r, name)
        setattr(r, name, vector[...].astype(F32).reshape(1, vector.shape[0]))
    own = pl.ds(REACH, rows)
    mine = pl.ds(pl.multiple_of(half * rows, 16), rows)

    pairs = dict(
        nodes=(r.nodes.at[mine], r.windows.at[0, own]),
        neighbours=(r.neighbours, r.neighbours_raw),
        first=(r.first_in, r.first),
        edges=(r.edges.at[:, mine, :], r.edges_raw),
        second=(r.second_in, r.second_w),
        e_first=(r.e_first_in, r.e_first_t),
        e_second=(r.e_second_in, r.e_second_w),
        e_third=(r.e_third_in, r.e_third_w),
        third=(r.third_in, r.third),
        expand=(r.expand_in, r.expand),
        reduce=(r.reduce_in, r.reduce),
        cot_edges=(r.cot_edges.at[:, mine, :], r.cots_raw),
        cot_nodes=(r.cot_nodes.at[mine], r.cot_rows),
    )
    loads = types.SimpleNamespace()
    for at, (name, pair) in enumerate(pairs.items()):
        copy = pltpu.make_async_copy(*pair, r.load_sem.at[at])
        setattr(loads, name, copy)
        copy.start()

    halos = [
        Halo(place, r.windows.at[k], rows, r.line_send, r.line_recv, 4 * k) for k in range(3)
    ]
    edge_returns = Returns(place, r.ge_first, r.edge_outgoing, r.edge_landing, rows, r.line_send, r.line_recv, 12)
    node_returns = Returns(place, r.g_first, r.node_outgoing, r.node_landing, rows, r.line_send, r.line_recv, 16)
    copies = Copies(r.step_send, r.step_recv)
    edge, third, first_a, first_b, second = sums = Chunks(
        *(
            ChipSum(place, copies, *parts, r.keep_sem.at[10 + at])
            for at, parts in enumerate(zip(ORDERS, r.pack, r.got, r.landed, r.gathered, r.sums_out))
        )
    )
    span = count * rows

    def row_gather(source, slot_ref):
        base = half * span
        groups = gather_groups(place, copies, slot_ref, rows, source, base)
        here = slot_ref.at[pl.ds(pl.multiple_of(base, 16), span)]
        groups.append(copies.group([(here, here, place.partner)]))
        return groups

    normed_gather = row_gather(r.normed, r.normed_slots)
    ds_gather = row_gather(r.ds, r.ds_slots)
    my_unit = (place.at[0] * place.dims[1] + place.at[1]) * place.dims[2] + place.at[2]
    my_slot = pl.ds(pl.multiple_of(half * span + my_unit * rows, 16), rows)
    normed_keep = pltpu.make_async_copy(r.normed, r.normed_slots.at[my_slot], r.keep_sem.at[0])
    ds_keep = pltpu.make_async_copy(r.ds, r.ds_slots.at[my_slot], r.keep_sem.at[1])
    there = pl.ds(pl.multiple_of(half * rows, 16), rows)
    my_slots = pl.ds(half * each, each)
    its_slots = pl.ds((1 - half) * each, each)
    edges_target = r.edges_out.at[:, there, :]
    edges_pair = copies.group([(r.edge_out.at[its_slots], edges_target, place.partner)])
    edges_keep = pltpu.make_async_copy(r.edge_out.at[my_slots], edges_target, r.keep_sem.at[2])
    grads_target = r.grads_out.at[:, there, :]
    grads_pair = copies.group([(r.edge_grad_low.at[its_slots], grads_target, place.partner)])
    grads_keep = pltpu.make_async_copy(r.edge_grad_low.at[my_slots], grads_target, r.keep_sem.at[3])
    fed_pair = copies.group([(r.fed_grad.at[1 - half], r.fed_out.at[there], place.partner)])
    fed_keep = pltpu.make_async_copy(r.fed_grad.at[half], r.fed_out.at[there], r.keep_sem.at[4])

    greet(place)
    loads.nodes.wait()
    halos[0].start()
    for halo in halos:
        halo.clear()
    dims = (rows, LANE)
    counted = jnp.broadcast_to(r.counts_in, (rows, rows_dev))
    here = iota(counted.shape, 1) == iota(counted.shape, 0) + half * rows
    r.counts[...] = jnp.broadcast_to(jnp.sum(jnp.where(here, counted, 0.0), -1, keepdims=True), dims)
    for block in range(r.expand.shape[1] // WIDE):
        r.bias_wide[block : block + 1, :] = r.b_expand[:, block * WIDE : (block + 1) * WIDE]
    dims = (rows, CHAIN * rows)
    lane = iota(dims, 1)
    r.diagonal[...] = jnp.where(lax.rem(lane, rows) == iota(dims, 0), 1.0, 0.0)
    r.lane_slot[...] = (iota(r.lane_slot.shape, 1) // rows).astype(F32)
    loads.neighbours.wait()
    base = res * rows_dev + half * rows - REACH
    named = (r.neighbours_raw[...] - base).astype(F32)
    r.picks[...] = named.reshape(slots, 1, rows_dev)

    def build(step, carry):
        build_block(r, step, half, places)
        return carry

    lax.fori_loop(0, steps, build, 0)
    for table in (r.table, r.e_table):
        rest = LANES - places - rows
        if rest:
            table[pl.ds(places + rows, rest), :] = jnp.zeros((rest, table.shape[1]), BF16)
    for load in (loads.first, loads.e_first, loads.e_second, loads.e_third):
        load.wait()
    r.table[pl.ds(LANES, features), :] = r.first[pl.ds(2 * width, features), :]
    edge_part = r.e_first_t[:, pl.ds(2 * width, features)]
    r.e_table[pl.ds(LANES, features), :] = jnp.transpose(edge_part.astype(F32)).astype(BF16)
    loads.edges.wait()
    bias = r.b_one
    far_w, own_w = r.first[pl.ds(width, width), :], r.first[pl.ds(0, width), :]
    fill_own(r.windows.at[0], far_w, own_w, bias, r.table, rows, dot)
    halos[0].wait()
    fill_far(r.windows.at[0], far_w, r.table, rows, dot)
    r.pooled[...] = jnp.zeros(r.pooled.shape, F32)
    loads.second.wait()

    def first_pass(step, carry):
        node_block(r, step, False)
        return carry

    lax.fori_loop(0, steps, first_pass, 0)
    loads.third.wait()
    loads.expand.wait()
    loads.reduce.wait()
    r.windows[1, own, :] = feed_forward(r, r.pooled[...], r.windows[0, own, :].astype(F32)).astype(BF16)

    halos[1].start()
    loads.cot_edges.wait()
    loads.cot_nodes.wait()
    fill_own(r.windows.at[1], far_w, own_w, bias, r.table, rows, dot)
    halos[1].wait()
    fill_far(r.windows.at[1], far_w, r.table, rows, dot)
    r.pooled[...] = jnp.zeros(r.pooled.shape, F32)

    def second_pass(step, carry):
        node_block(r, step, True)
        return carry

    lax.fori_loop(0, steps, second_pass, 0)
    r.windows[2, own, :] = feed_forward(r, r.pooled[...], r.windows[1, own, :].astype(F32)).astype(BF16)

    halos[2].start()
    normed_keep.start()
    normed_gather[0].start()
    for ref in (r.ge_norm, r.ge_first, r.ge_second, r.ge_third, r.g_second, r.g_first, r.g_bias):
        ref[...] = jnp.zeros(ref.shape, F32)
    e_own, e_far = r.e_first_t[:, pl.ds(0, width)], r.e_first_t[:, pl.ds(width, width)]
    fill_own(r.windows.at[2], e_far, e_own, r.eb_one, r.e_table, rows, dot_t)
    halos[2].wait()
    fill_far(r.windows.at[2], e_far, r.e_table, rows, dot_t)
    state_keep = pltpu.make_async_copy(
        r.windows.at[
            2,
            pl.ds(pl.multiple_of(REACH - half * rows, 16), rows_dev),
            pl.ds(pl.multiple_of(half * (width // CORES), width // CORES), width // CORES),
        ],
        r.state_out,
        r.keep_sem.at[5],
    )
    state_keep.start()

    def loop(count, body, events=None):
        def one(step, carry):
            body(step)
            for when, actions in (events or {}).items():

                @pl.when(step == when)
                def _():
                    for act in actions:
                        act()

            return carry

        lax.fori_loop(0, count, one, 0)

    loop(
        steps,
        lambda step: edge_block(r, step, features),
        {0: (normed_keep.wait, normed_gather[0].wait, normed_gather[1].start)},
    )
    edge_returns.start()
    edges_keep.start()
    normed_gather[1].wait()
    normed_gather[2].start()
    own_spread = r.ge_first[pl.ds(places, rows), :]
    r.ge_own[...] = t_dot(own_spread.astype(BF16), r.windows[2, own, :])
    r.ge_far[...] = t_dot(r.ge_first[pl.ds(0, places), :].astype(BF16), r.windows[2])
    pack_edge(r, r.pack.edge)
    edge.send_pair()
    edges_pair.start()
    r.e_own_back[...] = dot_wide(own_spread, e_own)

    expand_store = pltpu.make_async_copy(r.g_expand, r.expand_out, r.keep_sem.at[8])
    reduce_store = pltpu.make_async_copy(r.g_reduce, r.reduce_out, r.keep_sem.at[9])

    def move(chunk, at):
        if at == 0:
            chunk.add_pair()
            chunk.start(0)
        elif at < 3:
            chunk.finish(at - 1)
            chunk.start(at)
        elif at == 3:
            chunk.finish(2)
            chunk.start_back(0)
        elif at < 6:
            chunk.finish_back(at - 4)
            chunk.start_back(at - 3)
        else:
            chunk.finish_back(2)

    def ahead(groups, at):
        groups[at].wait()
        if at + 1 < len(groups):
            groups[at + 1].start()

    def moves(*pairs):
        for chunk, at in pairs:
            (move if isinstance(chunk, ChipSum) else ahead)(chunk, at)

    def events(*pairs):
        return (functools.partial(moves, *pairs),)

    moves((edge, 0))
    edge_returns.finish(r.edge_total)

    def send_ds():
        ds_keep.start()
        ds_gather[0].start()

    node_grad(r, r.cot_rows[...], r.edge_total[...], send_ds)
    pack_third(r, r.pack.third)
    third.send_pair()
    loop(steps, lambda step: first_grad_block(r, step, features), {0: events((third, 0))})
    node_returns.start()
    moves((normed_gather, 2))
    own_spread = r.g_first[pl.ds(places, rows), :]
    spread = r.g_first[pl.ds(0, places), :]
    for side, chunk_sum in enumerate((first_a, first_b)):
        pack_first(r, side, chunk_sum.pack, r.windows.at[1], spread, own_spread, own, features, places)
        chunk_sum.send_pair()
    moves((edge, 1))
    ds_keep.wait()
    moves((ds_gather, 0))
    own_back = r.du[...] + dot_wide(own_spread, own_w, True)
    loop(steps, lambda step: second_grad_block(r, step, features), {0: events((third, 1))})
    moves((normed_gather, 3), (first_a, 0))
    pack_second(r, r.pack.second)
    second.send_pair()
    grads_keep.start()
    moves((first_b, 0))
    grads_pair.start()
    node_returns.finish(r.node_total)
    fed = own_back + dot_wide(r.node_total[...], far_w, True)
    for part in range(CORES):
        r.fed_grad[part] = fed[:, part * (width // CORES) : (part + 1) * (width // CORES)]
    fed_keep.start()
    fed_pair.start()

    blocks = r.expand.shape[1] // WIDE
    chunk = r.normed_all.shape[0]
    chunks = 2 * span // chunk
    waiting = events((second, 0), (ds_gather, 1), (edge, 2), (third, 2)), events((first_b, 1))
    until_ds = (
        (second, 1), (first_a, 1), (third, 3), (ds_gather, 2), (edge, 3), (first_b, 2), (second, 2), (first_a, 2),
        (third, 4), (edge, 4), (ds_gather, 3),
    )
    beside = {
        0: events((second, 3)),
        1: events((first_a, 3), (first_b, 3)),
        2: events((third, 5)),
        3: events((second, 4)) + (reduce_store.start,),
        4: events((first_a, 4), (edge, 5)),
        5: events((first_b, 4)),
        6: events((third, 6), (first_a, 5)),
        7: events((second, 5), (edge, 6), (first_b, 5)),
    }

    def fetch(slots, target, sem, at=0):
        return pltpu.make_async_copy(slots.at[pl.ds(at * chunk, chunk)], target, r.keep_sem.at[sem])

    if chunks == 1:
        normed_fetch = fetch(r.normed_slots, r.normed_all, 6)
        normed_fetch.start()
        normed_fetch.wait()
        loop(EARLY_WIDE, lambda step: WideBlock(r, step, half).keep(), {1: waiting[0], 4: waiting[1]})
        moves(*until_ds)
        ds_fetch = fetch(r.ds_slots, r.ds_all, 7)
        ds_fetch.start()
        ds_fetch.wait()
        loop(EARLY_WIDE, lambda step: WideBlock(r, step, half).from_kept(), beside)
        last = {at - EARLY_WIDE: actions for at, actions in beside.items() if at >= EARLY_WIDE}
        loop(blocks - EARLY_WIDE, lambda step: WideBlock(r, step + EARLY_WIDE, half).whole(True), last)
    else:
        for actions in waiting:
            for act in actions:
                act()
        moves(*until_ds)
        for at in range(chunks):
            fetches = [fetch(r.normed_slots, r.normed_all, 6, at), fetch(r.ds_slots, r.ds_all, 7, at)]
            for copy in fetches:
                copy.start()
            for copy in fetches:
                copy.wait()
            loop(blocks, lambda step: WideBlock(r, step, half).whole(at == 0))
        for actions in beside.values():
            for act in actions:
                act()
    expand_store.start()
    for group in (edges_pair, grads_pair, fed_pair):
        group.wait()
    for copy in (edges_keep, grads_keep, fed_keep, state_keep):
        copy.wait()
    moves((second, 6), (first_b, 6), (first_a, 6))
    expand_store.wait()
    reduce_store.wait()


def shape(dims, kind):
    return jax.ShapeDtypeStruct(dims, kind)


def run(vectors, arrays):
    count = lax.axis_size("res")
    rows_dev, width = arrays.nodes.shape
    slots, _, features = arrays.edges.shape
    hidden = arrays.second_in.shape[0]
    inner = arrays.expand_in.shape[1]
    rows = rows_dev // CORES
    places = rows + 2 * REACH
    total = rows * slots
    each = slots // CORES
    tall = arrays.first_in.shape[0]
    chunks = chunk_rows(count, width, hidden, features)
    side, deep = chip_dims(count)
    everyone = CORES * count * rows
    chunk = everyone if everyone <= 16 * rows_dev else 8 * rows_dev
    wide_kind = BF16 if chunk == everyone else F32
    outs = (
        shape((rows_dev, width // CORES), BF16),
        shape((each, rows_dev, features), BF16),
        shape((rows_dev, width // CORES), F32),
        shape((each, rows_dev, features), BF16),
        shape((width // CORES, inner), wide_kind),
        shape((inner // CORES, width), wide_kind),
        shape((everyone, width), BF16),
        shape((everyone, width), BF16),
    ) + tuple(shape((size, LANE), BF16) for size in chunks)
    peers = 2 * (side - 1) + deep - 1
    remote = len(chunks) * (2 * peers + 1) + 2 * (peers + 1) + 3
    scratch = dict(
        windows=((3, places, width), BF16),
        neighbours_raw=((slots, rows_dev), jnp.int32),
        picks=((slots, 1, rows_dev), F32),
        counts=((rows, LANE), F32),
        bias_wide=((inner // WIDE, WIDE), F32),
        diagonal=((rows, CHAIN * rows), F32),
        lane_slot=((8, CHAIN * rows), F32),
        first=((tall, hidden), BF16),
        second_w=((hidden, hidden), BF16),
        third=((hidden, width), BF16),
        expand=((width, inner), BF16),
        reduce=((inner, width), BF16),
        e_first_t=((features, tall), BF16),
        e_second_w=((features, features), BF16),
        e_third_w=((features, features), BF16),
        edges_raw=((slots, rows, features), BF16),
        cots_raw=((slots, rows, features), BF16),
        cot_rows=((rows, width), BF16),
        onehot=((slots, rows, LANES), BF16),
        table=((LANES + features, hidden), BF16),
        e_table=((LANES + features, features), BF16),
        kept=((3 * total, hidden), BF16),
        pooled=((rows, hidden), F32),
        summed=((rows, width), F32),
        second=((rows, width), F32),
        pre_expand=((rows, inner), F32),
        normed=((rows, width), BF16),
        edge_out=((slots, rows, features), BF16),
        edge_grad=((slots, rows, features), F32),
        ge_norm=((8, features), F32),
        ge_first=((LANES + features, features), F32),
        ge_second=((features, features), F32),
        ge_third=((features, features), F32),
        ge_own=((features, width), F32),
        ge_far=((features, width), F32),
        e_own_back=((rows, width), F32),
        edge_outgoing=((places, features), BF16),
        edge_landing=((places, features), BF16),
        edge_total=((rows, features), F32),
        ds=((rows, width), BF16),
        du=((rows, width), F32),
        dm=((rows, width), BF16),
        slot_grad=((rows, hidden), F32),
        small=((16, width), F32),
        g_second=((hidden, hidden), F32),
        g_first=((LANES + features, hidden), F32),
        g_bias=((1, hidden), F32),
        node_outgoing=((places, hidden), BF16),
        node_landing=((places, hidden), BF16),
        node_total=((rows, hidden), F32),
        fed_grad=((CORES, rows, width // CORES), F32),
        normed_all=((chunk, width), BF16),
        ds_all=((chunk, width), BF16),
        g_expand=((width // CORES, inner), wide_kind),
        g_reduce=((inner // CORES, width), wide_kind),
    )
    packed = [(CORES, size, LANE) for size in chunks] + [(size, LANE) for size in chunks] * 3
    sems = dict(load_sem=13, keep_sem=15, line_send=20, line_recv=20, step_send=remote, step_recv=remote)
    for name, size in sems.items():
        scratch[name] = pltpu.SemaphoreType.DMA((size,))
    anywhere = pl.BlockSpec(memory_space=pl.ANY)
    return pl.pallas_call(
        functools.partial(kernel, tuple(scratch), features),
        out_shape=outs,
        in_specs=[pl.BlockSpec(memory_space=pltpu.VMEM)] * len(vectors) + [anywhere] * len(arrays),
        out_specs=(anywhere,) * len(outs),
        scratch_shapes=[pltpu.VMEM(*kind) if isinstance(kind, tuple) else kind for kind in scratch.values()]
        + [pltpu.VMEM(dims, BF16) for dims in packed],
        compiler_params=pltpu.CompilerParams(
            collective_id=1, has_side_effects=True, vmem_limit_bytes=VMEM
        ),
        name="graph_layer",
    )(*vectors, *arrays)


class Moved(NamedTuple):
    grads: Any
    expand: Any
    reduce: Any
    edges: Any
    state: Any
    fed: Any


class Grads(NamedTuple):
    third_g: Any
    e_first: Any
    e_second: Any
    e_third: Any
    second_g: Any
    first_g: Any


class Biases(NamedTuple):
    b_one: Any
    b_two: Any
    b_three: Any
    gain_one: Any
    shift_one: Any
    b_expand: Any
    b_reduce: Any
    gain_two: Any
    shift_two: Any
    eb_one: Any
    eb_two: Any
    eb_three: Any
    e_gain: Any
    e_shift: Any


def finish_kernel(width, hidden, features, inner, *refs):
    refs = list(refs)
    take = lambda kind: kind(*(refs.pop(0) for _ in kind._fields))
    moved_in, packed_in = take(Moved), take(Chunks)
    moved_out, grads_out, biases = take(Moved), take(Grads), take(Biases)
    r, g, via, ready = take(Chunks), take(Grads), take(Moved), take(Moved)
    sem, move_sem = refs
    half = lax.axis_index("half")
    wide = width // LANE
    tall = (2 * width + features) // CORES
    copy = pltpu.make_async_copy
    fetches = [copy(*pair, sem.at[at]) for at, pair in enumerate(zip(moved_in, via))]
    moves = [
        copy(a if a.dtype == c.dtype else b, c, move_sem.at[at]) for at, (a, b, c) in enumerate(zip(via, ready, moved_out))
    ]
    first = len(fetches)
    loads = Chunks(*(copy(*pair, sem.at[first + at]) for at, pair in enumerate(zip(packed_in, r))))
    first += len(loads)
    stores = Grads(*(copy(*pair, sem.at[first + at]) for at, pair in enumerate(zip(g, grads_out))))
    for load in loads:
        load.start()
    for fetch in fetches:
        fetch.start()

    def move_on(at):
        fetches[at].wait()
        if via[at].dtype != ready[at].dtype:
            ready[at][...] = via[at][...].astype(ready[at].dtype)
        moves[at].start()

    loads.third.wait()
    g.third_g[...], _ = take_wide(r.third, 0, hidden // CORES, wide)
    stores.third_g.start()
    loads.edge.wait()
    e_whole, at = take_wide(r.edge, 0, features, up(tall, LANE) // LANE)
    g.e_first[...] = e_whole[:, :tall]
    rest = features - LANE
    part = features // CORES
    left_two, at = take_wide(r.edge, at, part, 1)
    left_three, at = take_wide(r.edge, at, part, 1)
    right, at = take_wide(r.edge, at, part, 1)
    g.e_second[...] = jnp.concatenate([left_two, right[:, :rest]], 1)
    g.e_third[...] = jnp.concatenate([left_three, right[:, rest:]], 1)
    for store in (stores.e_first, stores.e_second, stores.e_third):
        store.start()
    for at in range(2):
        move_on(at)
    loads.second.wait()
    g.second_g[...], _ = take_wide(r.second, 0, hidden // CORES, wide)
    stores.second_g.start()
    for at in range(2, len(fetches)):
        move_on(at)
    loads.first_a.wait()
    g.first_g[:, : hidden // 2], _ = take_wide(r.first_a, 0, tall, wide // 2)
    loads.first_b.wait()
    g.first_g[:, hidden // 2 :], at = take_wide(r.first_b, 0, tall, wide // 2)
    stores.first_g.start()
    small, _ = take_wide(r.first_b, at, 16, wide)

    def share(target, row):
        size = target.shape[0]
        target[...] = jnp.where(half == 0, row[:, :size], row[:, size : 2 * size]).reshape(size)

    b = biases
    for target, at in (
        (b.b_one, 0), (b.b_two, 1), (b.b_three, 2), (b.gain_one, 3), (b.shift_one, 4), (b.b_reduce, 9),
        (b.gain_two, 10), (b.shift_two, 11),
    ):
        share(target, small[at : at + 1])
    share(b.b_expand, jnp.concatenate([small[5 + p : 6 + p] for p in range(inner // width)], 1))
    share(b.eb_one, small[12:13, :LANES])
    share(b.eb_two, small[12:13, LANES:])
    share(b.eb_three, small[13:14, :LANES])
    share(b.e_gain, small[13:14, LANES:])
    share(b.e_shift, small[14:15, :LANES])
    for store in moves + list(stores):
        store.wait()


def finish(moved, sums, width, hidden, features, inner):
    tall = (2 * width + features) // CORES
    part = features // CORES
    grads = Grads(
        third_g=(hidden // CORES, width),
        e_first=(features, tall),
        e_second=(part, features),
        e_third=(part, features),
        second_g=(hidden // CORES, hidden),
        first_g=(tall, hidden),
    )
    sizes = Biases(hidden, hidden, width, width, width, inner, width, width, width, *[features] * 5)
    anywhere, vmem = pl.BlockSpec(memory_space=pl.ANY), pl.BlockSpec(memory_space=pltpu.VMEM)
    kinds = Moved(F32, F32, F32, BF16, BF16, F32)
    outs = [shape(a.shape, kind) for a, kind in zip(moved, kinds)]
    outs += [shape(dims, F32) for dims in grads]
    outs += [shape((size // CORES,), F32) for size in sizes]
    got = pl.pallas_call(
        functools.partial(finish_kernel, width, hidden, features, inner),
        out_shape=outs,
        in_specs=[anywhere] * (len(moved) + len(sums)),
        out_specs=[anywhere] * (len(moved) + len(grads)) + [vmem] * len(sizes),
        scratch_shapes=[pltpu.VMEM(a.shape, BF16) for a in sums]
        + [pltpu.VMEM(dims, F32) for dims in grads]
        + [pltpu.VMEM(a.shape, a.dtype) for a in moved]
        + [pltpu.VMEM(a.shape if a.dtype != kind else (16, LANE), kind) for a, kind in zip(moved, kinds)]
        + [pltpu.SemaphoreType.DMA((len(moved) + len(sums) + len(grads),)), pltpu.SemaphoreType.DMA((len(moved),))],
        compiler_params=pltpu.CompilerParams(vmem_limit_bytes=VMEM),
        name="finish",
    )(*moved, *sums)
    first = len(moved) + len(grads)
    return Moved(*got[: len(moved)]), Grads(*got[len(moved) : first]), Biases(*got[first:])


def body(
    nodes, edges, neighbours, counts,
    message_first, message_first_bias, message_second, message_second_bias, message_third, message_third_bias,
    node_norm_gain, node_norm_shift, expand_weight, expand_bias, reduce_weight, reduce_bias,
    output_norm_gain, output_norm_shift,
    edge_first, edge_first_bias, edge_second, edge_second_bias, edge_third, edge_third_bias,
    edge_norm_gain, edge_norm_shift, cot_nodes, cot_edges,
):
    width, features = nodes.shape[1], edges.shape[2]
    hidden, inner = message_second.shape[0], expand_weight.shape[1]

    by_slots = lambda values: jnp.transpose(values, (1, 0, 2))
    vectors = Vectors(
        message_first_bias, message_second_bias, message_third_bias, node_norm_gain, node_norm_shift, reduce_bias,
        output_norm_gain, output_norm_shift, expand_bias, edge_first_bias, edge_second_bias, edge_third_bias,
        edge_norm_gain, edge_norm_shift, counts,
    )
    arrays = Arrays(
        nodes, by_slots(edges), neighbours.T, message_first, message_second, message_third, expand_weight,
        reduce_weight, edge_first.T, edge_second, edge_third, cot_nodes, by_slots(cot_edges),
    )
    state, out, fed_grad, edge_grad, g_expand, g_reduce, _, _, *sums = run(vectors, arrays)
    moved = Moved(edge_grad, g_expand, g_reduce, out, state, fed_grad)
    m, g, b = finish(moved, sums, width, hidden, features, inner)
    return (
        m.state, by_slots(m.edges), m.fed, by_slots(m.grads),
        g.first_g, b.b_one, g.second_g, b.b_two, g.third_g, b.b_three, b.gain_one, b.shift_one,
        m.expand, b.b_expand, m.reduce, b.b_reduce, b.gain_two, b.shift_two,
        g.e_first.T, b.eb_one, g.e_second, b.eb_two, g.e_third, b.eb_three, b.e_gain, b.e_shift,
    )


def solution(mesh):
    rows, slots = P("res", None), P("res", None, None)
    copied = P()
    down, vec = P("half", None), P("half")
    return jax.shard_map(
        body,
        mesh=mesh,
        in_specs=(rows, slots, rows, P("res")) + (copied,) * 22 + (rows, slots),
        out_specs=(
            P("res", "half"),
            P("res", "half", None),
            P("res", "half"),
            P("res", "half", None),
            down, vec, down, vec, down, vec, vec, vec, down, vec, down, vec, vec, vec,
            down, vec, down, vec, down, vec, vec, vec,
        ),
        check_vma=False,
    )
```

```python
import functools
import types
from typing import Any, NamedTuple

import jax
import jax.numpy as jnp
from jax import lax
from jax.experimental import pallas as pl
from jax.experimental.pallas import tpu as pltpu
from jax.sharding import PartitionSpec as P

EPSILON = 1e-05
REACH = 64
CORES = 2
NEAR = 0.7978845608
CUBE = 0.044715
STEP = 30
CHAIN = 5
BACK_CHAIN = 30
EDGE_CHAIN = 15
EARLY_WIDE = 6
PARTS = 2
LANES = 256
LANE = 128
WIDE = 256
VMEM = 62 * 2**20
MESH = pl.DeviceIdType.MESH
F32 = jnp.float32
BF16 = jnp.bfloat16


def dot(left, right):
    return jnp.dot(left, right, preferred_element_type=F32)


def dot_t(left, right):
    return lax.dot_general(left, right, (((1,), (1,)), ((), ())), preferred_element_type=F32)


def t_dot(left, right):
    return lax.dot_general(left, right, (((0,), (0,)), ((), ())), preferred_element_type=F32)


def two_parts(values):
    high = values.astype(BF16)
    return high, (values - high.astype(F32)).astype(BF16)


def dot_wide(values, right, transposed=False):
    rows = values.shape[0]
    both = (dot_t if transposed else dot)(jnp.concatenate(two_parts(values), 0), right)
    return both[:rows] + both[rows:]


def gelu(values):
    kind = values.dtype.type
    square = values * values
    bend = jnp.tanh(values * (kind(NEAR) + kind(NEAR * CUBE) * square))
    return values * (kind(0.5) + kind(0.5) * bend)


def gelu_slope(values):
    square = values * values
    part = 0.5 + 0.5 * jnp.tanh(values * (NEAR + (NEAR * CUBE) * square))
    return part + values * part * (1.0 - part) * (2.0 * NEAR + (6.0 * NEAR * CUBE) * square)


def gelu_and_slope(values):
    values = values.astype(BF16)
    square = values * values
    part = BF16(0.5) + BF16(0.5) * jnp.tanh(values * (BF16(NEAR) + BF16(NEAR * CUBE) * square))
    act = values * part
    slope = part + act * (1 - part) * (BF16(2.0 * NEAR) + BF16(6.0 * NEAR * CUBE) * square)
    return act, slope


def norm_parts(values):
    centered = values - jnp.mean(values, -1, keepdims=True)
    scale = lax.rsqrt(jnp.mean(centered * centered, -1, keepdims=True) + EPSILON)
    return centered * scale, scale


def norm_back(grad, unit, scale, gain):
    scaled = gain * grad
    flat = jnp.mean(scaled, -1, keepdims=True)
    slant = jnp.mean(scaled * unit, -1, keepdims=True)
    return (scaled - flat - unit * slant) * scale


def col_sum(values):
    return jnp.sum(values, 0, keepdims=True)


def iota(dims, axis):
    return lax.broadcasted_iota(jnp.int32, dims, axis)


def chip_dims(count):
    side = 1
    while 2 * (2 * side) ** 3 <= count and count % (4 * side * side) == 0:
        side *= 2
    return side, count // (side * side)


def up(size, unit):
    return -(-size // unit) * unit


class Chunks(NamedTuple):
    edge: Any
    third: Any
    first_a: Any
    first_b: Any
    second: Any


ORDERS = Chunks((0, 2, 1), (0, 1, 2), (2, 0, 1), (0, 1, 2), (0, 1, 2))


def chunk_rows(count, width, hidden, features):
    tall = (2 * width + features) // CORES
    wide = width // LANE
    edge = features * (up(tall, LANE) // LANE) + 3 * (features // CORES)
    square = (hidden // CORES) * wide
    first = tall * (wide // 2)
    sizes = (edge, square, first, first + 16 * wide, square)
    return Chunks(*(up(rows, 16 * count) for rows in sizes))


def cut(pieces, start, stop):
    at, got = 0, []
    for piece in pieces:
        low, high = max(start, at), min(stop, at + piece.shape[0])
        if low < high:
            got.append(piece[low - at : high - at])
        at += piece.shape[0]
    return jnp.concatenate(got, 0) if len(got) > 1 else got[0]


def put_wide(pack, half, at, piece):
    rows = piece.shape[0]
    for block in range(piece.shape[1] // LANE):
        pack[half, pl.ds(at, rows), :] = piece[:, block * LANE : (block + 1) * LANE].astype(BF16)
        at += rows
    return at


def put_rest(pack, at):
    rest = pack.shape[1] - at
    if rest:
        for half in range(CORES):
            pack[half, pl.ds(at, rest), :] = jnp.zeros((rest, LANE), BF16)


def take_wide(packed, at, rows, blocks):
    pieces = [packed[pl.ds(at + b * rows, rows), :] for b in range(blocks)]
    return jnp.concatenate(pieces, 1).astype(F32), at + blocks * rows


class Copies:
    def __init__(self, send, recv):
        self.send, self.recv, self.used = send, recv, 0

    def group(self, entries):
        made = []
        for source, target, device in entries:
            at = self.used
            self.used += 1
            made.append(functools.partial(self._make, source, target, device, at))
        return Group(made)

    def _make(self, source, target, device, at):
        return pltpu.make_async_remote_copy(
            src_ref=source,
            dst_ref=target,
            send_sem=self.send.at[at],
            recv_sem=self.recv.at[at],
            device_id=device,
            device_id_type=MESH,
        )


class Group:
    def __init__(self, made):
        self.made = made

    def start(self):
        for make in self.made:
            make().start()

    def wait(self):
        for make in self.made:
            make().wait()


class Place:
    def __init__(self):
        res, half, count = lax.axis_index("res"), lax.axis_index("half"), lax.axis_size("res")
        side, deep = chip_dims(count)
        x, y, z = lax.rem(res, side), lax.rem(res // side, side), res // (side * side)
        first = half == 0
        self.res, self.half, self.count = res, half, count
        self.dims = (side, side, deep)
        self.at = (jnp.where(first, x, y), jnp.where(first, y, x), z)
        self.strides = (jnp.where(first, 1, side), jnp.where(first, side, 1), side * side)
        self.partner = (res, 1 - half)

    def peers(self, level):
        size, here = self.dims[level], self.at[level]
        found = []
        for ahead in range(1, size):
            to = lax.rem(here + ahead, size)
            found.append((to, (self.res + (to - here) * self.strides[level], self.half)))
        return found

    def line(self):
        res, half, count = self.res, self.half, self.count
        return (
            (res > 0, (res - 1, half)),
            (res + half > 0, (res - 1 + half, 1 - half)),
            (res + half < count, (res + half, 1 - half)),
            (res < count - 1, (res + 1, half)),
        )

    def line_count(self):
        res, half, count = self.res, self.half, self.count
        return 4 - jnp.where(res > 0, 0, 2 - half) - jnp.where(res < count - 1, 0, 1 + half)


def greet(place):
    barrier = pltpu.get_barrier_semaphore()

    def signal(device):
        pl.semaphore_signal(barrier, inc=1, device_id=device, device_id_type=MESH)

    for exists, device in place.line():
        pl.when(exists)(functools.partial(signal, device))
    signal(place.partner)
    others = 1
    for level in range(3):
        for _, device in place.peers(level):
            signal(device)
            others += 1
    pl.semaphore_wait(barrier, others + place.line_count())


def halo_layout(rows):
    edge = REACH - rows
    return ((0, edge), (edge, rows), (REACH + rows, rows), (REACH + 2 * rows, edge))


class Halo:
    def __init__(self, place, window, rows, send, recv, first):
        self.place, self.window, self.rows = place, window, rows
        self.send, self.recv, self.first = send, recv, first

    def clear(self):
        for (exists, _), (offset, size) in zip(self.place.line(), halo_layout(self.rows)):

            @pl.when(jnp.logical_not(exists))
            def _():
                self.window[pl.ds(offset, size), :] = jnp.zeros((size, self.window.shape[1]), self.window.dtype)

    def _copy(self, at, device):
        offset, size = halo_layout(self.rows)[3 - at]
        first = REACH + (self.rows - size if at == 3 else 0)
        return pltpu.make_async_remote_copy(
            src_ref=self.window.at[pl.ds(first, size)],
            dst_ref=self.window.at[pl.ds(offset, size)],
            send_sem=self.send.at[self.first + at],
            recv_sem=self.recv.at[self.first + 3 - at],
            device_id=device,
            device_id_type=MESH,
        )

    def start(self):
        for at, (exists, device) in enumerate(self.place.line()):

            @pl.when(exists)
            def _():
                self._copy(at, device).start()

    def wait(self):
        for at, (exists, device) in enumerate(self.place.line()):
            offset, size = halo_layout(self.rows)[at]

            @pl.when(exists)
            def _():
                self._copy(at, device).wait_send()
                pltpu.make_async_remote_copy(
                    src_ref=self.window.at[pl.ds(offset, size)],
                    dst_ref=self.window.at[pl.ds(offset, size)],
                    send_sem=self.send.at[self.first + at],
                    recv_sem=self.recv.at[self.first + at],
                    device_id=device,
                    device_id_type=MESH,
                ).wait_recv()


class Returns:
    def __init__(self, place, table, outgoing, landing, rows, send, recv, first):
        self.place, self.table, self.landing, self.rows = place, table, landing, rows
        self.outgoing = outgoing
        self.send, self.recv, self.first = send, recv, first

    def _copy(self, at, device):
        layout = halo_layout(self.rows)
        offset, size = layout[at]
        return pltpu.make_async_remote_copy(
            src_ref=self.outgoing.at[pl.ds(offset, size)],
            dst_ref=self.landing.at[pl.ds(layout[3 - at][0], size)],
            send_sem=self.send.at[self.first + at],
            recv_sem=self.recv.at[self.first + 3 - at],
            device_id=device,
            device_id_type=MESH,
        )

    def start(self):
        self.outgoing[...] = self.table[pl.ds(0, self.outgoing.shape[0]), :].astype(BF16)
        for at, (exists, device) in enumerate(self.place.line()):

            @pl.when(exists)
            def _():
                self._copy(at, device).start()

    def finish(self, total):
        total[...] = self.table[pl.ds(REACH, self.rows), :]
        for at, (exists, device) in enumerate(self.place.line()):
            offset, size = halo_layout(self.rows)[at]
            first = self.rows - size if at == 3 else 0

            @pl.when(exists)
            def _():
                self._copy(at, device).wait_send()
                pltpu.make_async_remote_copy(
                    src_ref=self.outgoing.at[pl.ds(offset, size)],
                    dst_ref=self.landing.at[pl.ds(offset, size)],
                    send_sem=self.send.at[self.first + at],
                    recv_sem=self.recv.at[self.first + at],
                    device_id=device,
                    device_id_type=MESH,
                ).wait_recv()
                total[pl.ds(first, size), :] += self.landing[pl.ds(offset, size), :].astype(F32)


def gather_groups(place, copies, ref, unit, source=None, base=0):
    mine = (place.at[0] * place.dims[1] + place.at[1]) * place.dims[2] + place.at[2]
    groups, size = [], unit
    start = mine * unit
    for level in (2, 1, 0):
        here = ref.at[pl.ds(pl.multiple_of(base + start, 16), size)]
        from_ref = here if source is None or level < 2 else source
        groups.append(copies.group([(from_ref, here, device) for _, device in place.peers(level)]))
        start = start - place.at[level] * size
        size = size * place.dims[level]
    return groups


class ChipSum:
    def __init__(self, place, copies, order, pack, got, landed, gathered, out, keep_sem):
        self.place, self.pack, self.got, self.landed, self.gathered = place, pack, got, landed, gathered
        half, size = place.half, pack.shape[1]
        self.pair = copies.group([(pack.at[1 - half], got, place.partner)])
        self.steps, self.shares, self.back = [], [], []
        start, base = 0, 0
        for level in order:
            share = size // place.dims[level]
            entries, lands = [], []
            for to, device in place.peers(level):
                source = pack.at[half, pl.ds(pl.multiple_of(start + to * share, 16), share)]
                entries.append((source, landed.at[pl.ds(base, share)], device))
                lands.append(base)
                base += share
            start = pl.multiple_of(start + place.at[level] * share, 16)
            size = share
            self.steps.append(copies.group(entries))
            self.shares.append((start, share, lands))
            here = gathered.at[pl.ds(start, share)]
            there = here if self.back else out.at[pl.ds(start, share)]
            back = [(here, there, device) for _, device in place.peers(level)]
            self.back.insert(0, copies.group(back))
            if there is not here:
                self.keep = pltpu.make_async_copy(here, there, keep_sem)

    def send_pair(self):
        self.pair.start()

    def add_pair(self):
        self.pair.wait()
        half = self.place.half
        self.pack[half] = (self.pack[half].astype(F32) + self.got[...].astype(F32)).astype(BF16)

    def start(self, level):
        self.steps[level].start()

    def finish(self, level):
        self.steps[level].wait()
        start, share, lands = self.shares[level]
        half = self.place.half
        total = self.pack[half, pl.ds(start, share), :].astype(F32)
        for base in lands:
            total = total + self.landed[pl.ds(base, share), :].astype(F32)
        if level < len(self.steps) - 1:
            self.pack[half, pl.ds(start, share), :] = total.astype(BF16)
        else:
            self.gathered[pl.ds(start, share), :] = total.astype(BF16)

    def start_back(self, step):
        self.back[step].start()
        if step == len(self.back) - 1:
            self.keep.start()

    def finish_back(self, step):
        self.back[step].wait()
        if step == len(self.back) - 1:
            self.keep.wait()


def flat(values):
    return values.reshape(values.shape[0] * values.shape[1], values.shape[2])


def feed_forward(r, pooled, own):
    width = own.shape[1]
    mean = pooled / r.counts[:, 0:1]
    summed = own + dot_wide(mean, r.third[...]) + r.b_three
    unit, _ = norm_parts(summed)
    normed = unit * r.gain_one + r.shift_one
    low = normed.astype(BF16)
    pre = dot(low, r.expand[...]) + r.b_expand
    second = normed + dot(gelu(pre).astype(BF16), r.reduce[...]) + r.b_reduce
    unit_two, _ = norm_parts(second)
    r.summed[...] = summed
    r.pre_expand[...] = pre
    r.second[...] = second
    r.normed[...] = low
    return unit_two * r.gain_two + r.shift_two


def fill_own(window, far, own, bias, table, rows, multiply):
    here = pl.ds(REACH, rows)
    table[here, :] = multiply(window[here, :], far).astype(BF16)
    table[pl.ds(window.shape[0], rows), :] = (multiply(window[here, :], own) + bias).astype(BF16)


def fill_far(window, far, table, rows, multiply):
    for here in (pl.ds(0, REACH), pl.ds(REACH + rows, REACH)):
        table[here, :] = multiply(window[here, :], far).astype(BF16)


def chain_parts(step):
    return [step * STEP + part * CHAIN for part in range(STEP // CHAIN)]


def chain_rows(r, slot):
    rows = r.counts.shape[0]
    return pl.ds(pl.multiple_of(slot * rows, CHAIN * rows), CHAIN * rows)


def step_rows(r, step):
    rows = r.counts.shape[0]
    return pl.ds(pl.multiple_of(step * (STEP * rows), STEP * rows), STEP * rows)


def build_block(r, step, half, places):
    rows = r.counts.shape[0]
    here = pl.ds(step * STEP, STEP)
    named = r.picks[here]
    dims = (STEP, rows, named.shape[2])
    spread = jnp.broadcast_to(named, dims)
    mine = iota(dims, 2) == iota(dims, 1) + half * rows
    pick = jnp.sum(jnp.where(mine, spread, 0.0), -1, keepdims=True)
    dims = (STEP, rows, LANES)
    lane = iota(dims, 2)
    hit = (lane.astype(F32) == pick) | (lane == iota(dims, 1) + places)
    r.onehot[here] = jnp.where(hit, 1.0, 0.0).astype(BF16)


def joined_rows(r, slot, slots):
    here = pl.ds(slot, slots)
    return jnp.concatenate([flat(r.onehot[here]), flat(r.edges_raw[here])], 1)


def live_rows(r, slot, width):
    count = r.counts[...]
    dims = (CHAIN,) + count.shape
    live = jnp.where(iota(dims, 0) + slot < count[None], 1.0, 0.0)
    return flat(jnp.concatenate([live] * (width // LANE), -1))


def live_column(r, slot, slots):
    count = r.counts[...]
    dims = (slots,) + count.shape
    return flat(jnp.where(iota(dims, 0) + slot < count[None], 1.0, 0.0))[:, 0:1]


def node_block(r, step, keep):
    rows = r.counts.shape[0]
    hidden = r.second_w.shape[0]
    slots = chain_parts(step)
    dims = (rows, CHAIN * rows)
    count = jnp.broadcast_to(r.counts[:, 0:1], dims)
    pre = [dot(joined_rows(r, slot, CHAIN), r.table[...]) for slot in slots]
    acts = []
    for slot, values in zip(slots, pre):
        if keep:
            here = chain_rows(r, slot)
            act, slope = gelu_and_slope(values)
            r.act[here, :] = act
            r.slope_one[here, :] = slope
        else:
            act = gelu(values.astype(BF16))
        acts.append(act)
    pre = [dot(act, r.second_w[...]) + r.b_two for act in acts]
    total = r.pooled[...]
    for slot, values in zip(slots, pre):
        if keep:
            act, slope = gelu_and_slope(values)
            r.slope_two[chain_rows(r, slot), :] = slope * live_rows(r, slot, hidden).astype(BF16)
        else:
            act = gelu(values.astype(BF16))
        used = jnp.where(r.lane_slot[0:1, :] + slot.astype(F32) < count, r.diagonal[...], 0.0)
        total = total + dot(used.astype(BF16), act.astype(BF16))
    r.pooled[...] = total


def edge_block(r, step, features):
    rows = r.counts.shape[0]
    split = lambda values: values.reshape(values.shape[0] // rows, rows, features)
    slots = [step * STEP + part * EDGE_CHAIN for part in range(STEP // EDGE_CHAIN)]
    each = lambda body, *lists: [body(*items) for items in zip(*lists)]
    joined = [joined_rows(r, slot, EDGE_CHAIN) for slot in slots]
    live = [live_column(r, slot, EDGE_CHAIN) for slot in slots]
    pre = each(lambda z: dot(z, r.e_table[...]), joined)
    o_one, slope_one = zip(*each(gelu_and_slope, pre))
    pre = each(lambda a: dot(a, r.e_second_w[...]) + r.eb_two, o_one)
    o_two, slope_two = zip(*each(gelu_and_slope, pre))
    summed = each(lambda z, a: z[:, LANES:].astype(F32) + (dot(a, r.e_third_w[...]) + r.eb_three), joined, o_two)
    unit, scale = zip(*each(norm_parts, summed))
    d_three, d_sums = [], []
    for slot, u, k, used in zip(slots, unit, scale, live):
        here = pl.ds(slot, EDGE_CHAIN)
        r.edge_out[here] = split((u * r.e_gain + r.e_shift) * used).astype(BF16)
        d_out = flat(r.cots_raw[here]).astype(F32) * used
        r.ge_norm[0:1, :] += col_sum(d_out * u)
        r.ge_norm[1:2, :] += col_sum(d_out)
        d_sum = norm_back(d_out, u, k, r.e_gain)
        r.ge_norm[2:3, :] += col_sum(d_sum)
        d_sums.append(d_sum)
        d_three.append(d_sum.astype(BF16))
    d_two = each(lambda d, k: dot_t(d, r.e_third_w[...]) * k, d_three, slope_two)
    r.ge_norm[3:4, :] += sum(col_sum(d) for d in d_two)
    d_two = each(lambda d: d.astype(BF16), d_two)
    d_one = each(lambda d, k: (dot_t(d, r.e_second_w[...]) * k).astype(BF16), d_two, slope_one)
    for slot, d_sum, d in zip(slots, d_sums, d_one):
        more = dot(d, r.e_first_t[:, pl.ds(2 * r.nodes_width, features)])
        r.edge_grad[pl.ds(slot, EDGE_CHAIN)] = split(d_sum + more)
    together = lambda values: jnp.concatenate(values, 0)
    r.ge_third[...] += t_dot(together(o_two), together(d_three))
    r.ge_second[...] += t_dot(together(o_one), together(d_two))
    r.ge_first[...] += t_dot(together(joined), together(d_one))


def node_grad(r, cot, far_total, when_ds):
    width = cot.shape[1]
    grad = cot.astype(F32) + r.e_own_back[...] + dot_wide(far_total, r.e_first_t[:, pl.ds(width, width)])
    unit, scale = norm_parts(r.second[...])
    dw = norm_back(grad, unit, scale, r.gain_two)
    gain_two, shift_two = col_sum(grad * unit), col_sum(grad)
    ds = dw.astype(BF16)
    r.ds[...] = ds
    when_ds()
    slope = gelu_slope(r.pre_expand[...])
    dq = (dot_t(ds, r.reduce[...]) * slope).astype(BF16)
    dv = dw + dot_t(dq, r.expand[...])
    unit, scale = norm_parts(r.summed[...])
    du = norm_back(dv, unit, scale, r.gain_one)
    r.du[...] = du
    counts = r.counts[:, 0:1]
    dm = (du / counts).astype(BF16)
    r.slot_grad[...] = dot_t(dm, r.third[...])
    r.dm[...] = dm
    small = r.small
    small[...] = jnp.zeros(small.shape, F32)
    small[2:3, :] = col_sum(counts * dm.astype(F32))
    small[3:4, :] = col_sum(dv * unit)
    small[4:5, :] = col_sum(dv)
    dq_sum = col_sum(dq.astype(F32))
    for part in range(dq_sum.shape[1] // width):
        small[5 + part : 6 + part, :] = dq_sum[:, part * width : (part + 1) * width]
    small[9:10, :] = col_sum(ds.astype(F32))
    small[10:11, :] = gain_two
    small[11:12, :] = shift_two


def put_features(pack, half, at, e_second, e_third):
    part = e_second.shape[0] // CORES
    two = [ref[pl.ds(half * part, part), :] for ref in (e_second, e_third)]
    for piece in two:
        at = put_wide(pack, half, at, piece[:, :LANE])
    return put_wide(pack, half, at, jnp.concatenate([piece[:, LANE:] for piece in two], 1))


def pack_edge(r, pack):
    features = r.ge_second.shape[0]
    g_edge = jnp.transpose(r.ge_first[pl.ds(LANES, features), :])
    e_first = jnp.concatenate([r.ge_own[...], r.ge_far[...], g_edge], 1)
    tall = e_first.shape[1] // CORES
    fill = jnp.zeros((features, up(tall, LANE) - tall), F32)
    for half in range(CORES):
        piece = jnp.concatenate([e_first[:, half * tall : (half + 1) * tall], fill], 1)
        at = put_wide(pack, half, 0, piece)
        at = put_features(pack, half, at, r.ge_second, r.ge_third)
    put_rest(pack, at)


def pack_third(r, pack):
    dm = r.dm[...]
    found = t_dot(jnp.concatenate(two_parts(r.pooled[...]), 0), jnp.concatenate([dm, dm], 0))
    part = found.shape[0] // CORES
    for half in range(CORES):
        at = put_wide(pack, half, 0, found[half * part : (half + 1) * part])
    put_rest(pack, at)


def pack_second(r, pack):
    part = r.g_second.shape[0] // CORES
    for half in range(CORES):
        at = put_wide(pack, half, 0, r.g_second[pl.ds(half * part, part), :])
    put_rest(pack, at)


def small_rows(r, places):
    rows = r.counts.shape[0]
    features = r.ge_norm.shape[1]
    fill = jnp.zeros((1, LANES - features), F32)
    own = pl.ds(places, rows)
    edge = [col_sum(r.ge_first[own, :])] + [r.ge_norm[at : at + 1, :] for at in (3, 2, 0, 1)]
    edge = [jnp.concatenate([row, fill], 1) for row in edge] + [jnp.zeros((1, LANES), F32)]
    lines = [col_sum(r.g_first[own, :]), r.g_bias[...], r.small[2:12, :]]
    lines += [jnp.concatenate(edge[at : at + 2], 1) for at in (0, 2, 4)]
    return jnp.concatenate(lines + [jnp.zeros((1, r.small.shape[1]), F32)], 0)


def pack_first(r, side, pack, window, spread, own_spread, own, features, places):
    hidden = own_spread.shape[1]
    cols = slice(side * (hidden // 2), (side + 1) * (hidden // 2))
    pieces = [
        t_dot(window[own, :], own_spread[:, cols].astype(BF16)),
        t_dot(window[...], spread[:, cols].astype(BF16)),
        r.g_first[pl.ds(LANES, features), cols],
    ]
    tall = sum(piece.shape[0] for piece in pieces) // CORES
    small = small_rows(r, places) if side == 1 else None
    for half in range(CORES):
        at = put_wide(pack, half, 0, cut(pieces, half * tall, (half + 1) * tall))
        if side == 1:
            at = put_wide(pack, half, at, small)
    put_rest(pack, at)


def first_grad_block(r, step, features):
    rows = r.counts.shape[0]
    hidden = r.act.shape[1]
    coming = jnp.broadcast_to(r.slot_grad[...][None], (BACK_CHAIN,) + r.slot_grad.shape)
    slots = [step * STEP + part * BACK_CHAIN for part in range(STEP // BACK_CHAIN)]
    places = [pl.ds(pl.multiple_of(slot * rows, BACK_CHAIN * rows), BACK_CHAIN * rows) for slot in slots]
    twos, ones = [], []
    for here in places:
        d_two = flat(coming) * r.slope_two[here, :].astype(F32)
        r.g_bias[...] += col_sum(d_two)
        twos.append(d_two.astype(BF16))
        r.slope_two[here, :] = twos[-1]
    backs = [dot_t(d_two, r.second_w[...]) for d_two in twos]
    for here, back in zip(places, backs):
        ones.append((back * r.slope_one[here, :].astype(F32)).astype(BF16))
        r.slope_one[here, :] = ones[-1]
    r.g_first[...] += t_dot(joined_rows(r, step * STEP, STEP), jnp.concatenate(ones, 0))


def second_grad_block(r, step, features):
    rows = r.counts.shape[0]
    here = step_rows(r, step)
    r.g_second[...] += t_dot(r.act[here, :], r.slope_two[here, :])
    more = dot_t(r.slope_one[here, :], r.table[pl.ds(LANES, features), :])
    there = pl.ds(step * STEP, STEP)
    r.edge_grad_low[there] = (r.edge_grad[there] + more.reshape(STEP, rows, features)).astype(BF16)


def put(target, rows, cols, found, fresh):
    target[rows, cols] = (found if fresh else target[rows, cols] + found).astype(target.dtype)


class WideBlock:
    def __init__(self, r, step, half):
        width, inner = r.expand.shape
        blocks = inner // WIDE
        self.r, self.step, self.mine = r, step, blocks // CORES
        self.block = lax.rem(step + half * self.mine, blocks)
        self.here = pl.ds(pl.multiple_of(self.block * WIDE, WIDE), WIDE)
        part = width // CORES
        self.cols = pl.ds(pl.multiple_of(half * part, part), part)
        self.total = r.normed_all.shape[0]
        size = self.total // PARTS
        self.rows = [pl.ds(at * size, size) for at in range(PARTS)]

    def forward(self):
        r = self.r
        bias = r.bias_wide[pl.ds(self.block, 1), :]
        pre = [dot(r.normed_all[rows, :], r.expand[:, self.here]) + bias for rows in self.rows]
        both = [gelu_and_slope(values) for values in pre]
        return [act for act, _ in both], [slope for _, slope in both]

    def place(self, slot, rows=None):
        size = self.total if rows is None else rows.size
        first = (slot // 2) * self.total + (0 if rows is None else rows.start)
        return self.r.kept.at[
            pl.ds(pl.multiple_of(first, 16), size), pl.ds(pl.multiple_of(lax.rem(slot, 2) * WIDE, WIDE), WIDE)
        ]

    def keep(self):
        acts, slopes = self.forward()
        for rows, slope in zip(self.rows, slopes):
            self.place(self.step, rows)[...] = slope

        @pl.when(self.step < self.mine)
        def _():
            for rows, act in zip(self.rows, acts):
                self.place(EARLY_WIDE + self.step, rows)[...] = act

    def backward(self, slopes, act, fresh):
        r = self.r
        back = [dot_t(r.ds_all[rows, :], r.reduce[self.here, :]) for rows in self.rows]
        dqs = [(grad * slope.astype(F32)).astype(BF16) for grad, slope in zip(back, slopes)]
        found = t_dot(r.normed_all[:, self.cols], jnp.concatenate(dqs, 0))
        put(r.g_expand, slice(None), self.here, found, fresh)

        @pl.when(self.step < self.mine)
        def _():
            out = pl.ds(pl.multiple_of(self.step * WIDE, WIDE), WIDE)
            found = t_dot(act(), r.ds_all[...])
            put(r.g_reduce, out, slice(None), found, fresh)

    def from_kept(self):
        slopes = [self.place(self.step, rows)[...] for rows in self.rows]
        self.backward(slopes, lambda: self.place(EARLY_WIDE + self.step)[...], True)

    def whole(self, fresh):
        acts, slopes = self.forward()
        self.backward(slopes, lambda: jnp.concatenate(acts, 0), fresh)


class Vectors(NamedTuple):
    b_one: Any
    b_two: Any
    b_three: Any
    gain_one: Any
    shift_one: Any
    b_reduce: Any
    gain_two: Any
    shift_two: Any
    b_expand: Any
    eb_one: Any
    eb_two: Any
    eb_three: Any
    e_gain: Any
    e_shift: Any
    counts_in: Any


class Arrays(NamedTuple):
    nodes: Any
    edges: Any
    neighbours: Any
    first_in: Any
    second_in: Any
    third_in: Any
    expand_in: Any
    reduce_in: Any
    e_first_in: Any
    e_second_in: Any
    e_third_in: Any
    cot_nodes: Any
    cot_edges: Any


class Results(NamedTuple):
    state_out: Any
    edges_out: Any
    fed_out: Any
    grads_out: Any
    expand_out: Any
    reduce_out: Any
    normed_slots: Any
    ds_slots: Any


def kernel(names, features, *refs):
    kinds, refs = (Vectors, Arrays, Results), list(refs)
    r = types.SimpleNamespace()
    for kind in kinds:
        for name in kind._fields:
            setattr(r, name, refs.pop(0))
    r.sums_out = Chunks(*(refs.pop(0) for _ in Chunks._fields))
    for name in names:
        setattr(r, name, refs.pop(0))
    r.pack, r.got, r.landed, r.gathered = (Chunks(*(refs.pop(0) for _ in Chunks._fields)) for _ in range(4))
    place = Place()
    res, half, count = place.res, place.half, place.count
    rows_dev, width = r.nodes.shape
    rows = rows_dev // CORES
    places = rows + 2 * REACH
    slots = r.edges.shape[0]
    each = slots // CORES
    steps = slots // STEP
    r.nodes_width = width
    total = r.edges_raw.shape[0] * rows
    r.edge_grad_low = r.cots_raw
    r.act, r.slope_one, r.slope_two = (r.kept.at[pl.ds(at * total, total)] for at in range(3))
    for name in Vectors._fields:
        vector = getattr(r, name)
        setattr(r, name, vector[...].astype(F32).reshape(1, vector.shape[0]))
    own = pl.ds(REACH, rows)
    mine = pl.ds(pl.multiple_of(half * rows, 16), rows)

    pairs = dict(
        nodes=(r.nodes.at[mine], r.windows.at[0, own]),
        neighbours=(r.neighbours, r.neighbours_raw),
        first=(r.first_in, r.first),
        edges=(r.edges.at[:, mine, :], r.edges_raw),
        second=(r.second_in, r.second_w),
        e_first=(r.e_first_in, r.e_first_t),
        e_second=(r.e_second_in, r.e_second_w),
        e_third=(r.e_third_in, r.e_third_w),
        third=(r.third_in, r.third),
        expand=(r.expand_in, r.expand),
        reduce=(r.reduce_in, r.reduce),
        cot_edges=(r.cot_edges.at[:, mine, :], r.cots_raw),
        cot_nodes=(r.cot_nodes.at[mine], r.cot_rows),
    )
    loads = types.SimpleNamespace()
    for at, (name, pair) in enumerate(pairs.items()):
        copy = pltpu.make_async_copy(*pair, r.load_sem.at[at])
        setattr(loads, name, copy)
        copy.start()

    halos = [
        Halo(place, r.windows.at[k], rows, r.line_send, r.line_recv, 4 * k) for k in range(3)
    ]
    edge_returns = Returns(place, r.ge_first, r.edge_outgoing, r.edge_landing, rows, r.line_send, r.line_recv, 12)
    node_returns = Returns(place, r.g_first, r.node_outgoing, r.node_landing, rows, r.line_send, r.line_recv, 16)
    copies = Copies(r.step_send, r.step_recv)
    edge, third, first_a, first_b, second = sums = Chunks(
        *(
            ChipSum(place, copies, *parts, r.keep_sem.at[10 + at])
            for at, parts in enumerate(zip(ORDERS, r.pack, r.got, r.landed, r.gathered, r.sums_out))
        )
    )
    span = count * rows

    def row_gather(source, slot_ref):
        base = half * span
        groups = gather_groups(place, copies, slot_ref, rows, source, base)
        here = slot_ref.at[pl.ds(pl.multiple_of(base, 16), span)]
        groups.append(copies.group([(here, here, place.partner)]))
        return groups

    normed_gather = row_gather(r.normed, r.normed_slots)
    ds_gather = row_gather(r.ds, r.ds_slots)
    my_unit = (place.at[0] * place.dims[1] + place.at[1]) * place.dims[2] + place.at[2]
    my_slot = pl.ds(pl.multiple_of(half * span + my_unit * rows, 16), rows)
    normed_keep = pltpu.make_async_copy(r.normed, r.normed_slots.at[my_slot], r.keep_sem.at[0])
    ds_keep = pltpu.make_async_copy(r.ds, r.ds_slots.at[my_slot], r.keep_sem.at[1])
    there = pl.ds(pl.multiple_of(half * rows, 16), rows)
    my_slots = pl.ds(half * each, each)
    its_slots = pl.ds((1 - half) * each, each)
    edges_target = r.edges_out.at[:, there, :]
    edges_pair = copies.group([(r.edge_out.at[its_slots], edges_target, place.partner)])
    edges_keep = pltpu.make_async_copy(r.edge_out.at[my_slots], edges_target, r.keep_sem.at[2])
    grads_target = r.grads_out.at[:, there, :]
    grads_pair = copies.group([(r.edge_grad_low.at[its_slots], grads_target, place.partner)])
    grads_keep = pltpu.make_async_copy(r.edge_grad_low.at[my_slots], grads_target, r.keep_sem.at[3])
    fed_pair = copies.group([(r.fed_grad.at[1 - half], r.fed_out.at[there], place.partner)])
    fed_keep = pltpu.make_async_copy(r.fed_grad.at[half], r.fed_out.at[there], r.keep_sem.at[4])

    greet(place)
    loads.nodes.wait()
    halos[0].start()
    for halo in halos:
        halo.clear()
    dims = (rows, LANE)
    counted = jnp.broadcast_to(r.counts_in, (rows, rows_dev))
    here = iota(counted.shape, 1) == iota(counted.shape, 0) + half * rows
    r.counts[...] = jnp.broadcast_to(jnp.sum(jnp.where(here, counted, 0.0), -1, keepdims=True), dims)
    for block in range(r.expand.shape[1] // WIDE):
        r.bias_wide[block : block + 1, :] = r.b_expand[:, block * WIDE : (block + 1) * WIDE]
    dims = (rows, CHAIN * rows)
    lane = iota(dims, 1)
    r.diagonal[...] = jnp.where(lax.rem(lane, rows) == iota(dims, 0), 1.0, 0.0)
    r.lane_slot[...] = (iota(r.lane_slot.shape, 1) // rows).astype(F32)
    loads.neighbours.wait()
    base = res * rows_dev + half * rows - REACH
    named = (r.neighbours_raw[...] - base).astype(F32)
    r.picks[...] = named.reshape(slots, 1, rows_dev)

    def build(step, carry):
        build_block(r, step, half, places)
        return carry

    lax.fori_loop(0, steps, build, 0)
    for table in (r.table, r.e_table):
        rest = LANES - places - rows
        if rest:
            table[pl.ds(places + rows, rest), :] = jnp.zeros((rest, table.shape[1]), BF16)
    for load in (loads.first, loads.e_first, loads.e_second, loads.e_third):
        load.wait()
    r.table[pl.ds(LANES, features), :] = r.first[pl.ds(2 * width, features), :]
    edge_part = r.e_first_t[:, pl.ds(2 * width, features)]
    r.e_table[pl.ds(LANES, features), :] = jnp.transpose(edge_part.astype(F32)).astype(BF16)
    loads.edges.wait()
    bias = r.b_one
    far_w, own_w = r.first[pl.ds(width, width), :], r.first[pl.ds(0, width), :]
    fill_own(r.windows.at[0], far_w, own_w, bias, r.table, rows, dot)
    halos[0].wait()
    fill_far(r.windows.at[0], far_w, r.table, rows, dot)
    r.pooled[...] = jnp.zeros(r.pooled.shape, F32)
    loads.second.wait()

    def first_pass(step, carry):
        node_block(r, step, False)
        return carry

    lax.fori_loop(0, steps, first_pass, 0)
    loads.third.wait()
    loads.expand.wait()
    loads.reduce.wait()
    r.windows[1, own, :] = feed_forward(r, r.pooled[...], r.windows[0, own, :].astype(F32)).astype(BF16)

    halos[1].start()
    loads.cot_edges.wait()
    loads.cot_nodes.wait()
    fill_own(r.windows.at[1], far_w, own_w, bias, r.table, rows, dot)
    halos[1].wait()
    fill_far(r.windows.at[1], far_w, r.table, rows, dot)
    r.pooled[...] = jnp.zeros(r.pooled.shape, F32)

    def second_pass(step, carry):
        node_block(r, step, True)
        return carry

    lax.fori_loop(0, steps, second_pass, 0)
    r.windows[2, own, :] = feed_forward(r, r.pooled[...], r.windows[1, own, :].astype(F32)).astype(BF16)

    halos[2].start()
    normed_keep.start()
    normed_gather[0].start()
    for ref in (r.ge_norm, r.ge_first, r.ge_second, r.ge_third, r.g_second, r.g_first, r.g_bias):
        ref[...] = jnp.zeros(ref.shape, F32)
    e_own, e_far = r.e_first_t[:, pl.ds(0, width)], r.e_first_t[:, pl.ds(width, width)]
    fill_own(r.windows.at[2], e_far, e_own, r.eb_one, r.e_table, rows, dot_t)
    halos[2].wait()
    fill_far(r.windows.at[2], e_far, r.e_table, rows, dot_t)
    state_keep = pltpu.make_async_copy(
        r.windows.at[
            2,
            pl.ds(pl.multiple_of(REACH - half * rows, 16), rows_dev),
            pl.ds(pl.multiple_of(half * (width // CORES), width // CORES), width // CORES),
        ],
        r.state_out,
        r.keep_sem.at[5],
    )
    state_keep.start()

    def loop(count, body, events=None):
        def one(step, carry):
            body(step)
            for when, actions in (events or {}).items():

                @pl.when(step == when)
                def _():
                    for act in actions:
                        act()

            return carry

        lax.fori_loop(0, count, one, 0)

    loop(
        steps,
        lambda step: edge_block(r, step, features),
        {0: (normed_keep.wait, normed_gather[0].wait, normed_gather[1].start)},
    )
    edge_returns.start()
    edges_keep.start()
    normed_gather[1].wait()
    normed_gather[2].start()
    own_spread = r.ge_first[pl.ds(places, rows), :]
    r.ge_own[...] = t_dot(own_spread.astype(BF16), r.windows[2, own, :])
    r.ge_far[...] = t_dot(r.ge_first[pl.ds(0, places), :].astype(BF16), r.windows[2])
    pack_edge(r, r.pack.edge)
    edge.send_pair()
    edges_pair.start()
    r.e_own_back[...] = dot_wide(own_spread, e_own)

    expand_store = pltpu.make_async_copy(r.g_expand, r.expand_out, r.keep_sem.at[8])
    reduce_store = pltpu.make_async_copy(r.g_reduce, r.reduce_out, r.keep_sem.at[9])

    def move(chunk, at):
        if at == 0:
            chunk.add_pair()
            chunk.start(0)
        elif at < 3:
            chunk.finish(at - 1)
            chunk.start(at)
        elif at == 3:
            chunk.finish(2)
            chunk.start_back(0)
        elif at < 6:
            chunk.finish_back(at - 4)
            chunk.start_back(at - 3)
        else:
            chunk.finish_back(2)

    def ahead(groups, at):
        groups[at].wait()
        if at + 1 < len(groups):
            groups[at + 1].start()

    def moves(*pairs):
        for chunk, at in pairs:
            (move if isinstance(chunk, ChipSum) else ahead)(chunk, at)

    def events(*pairs):
        return (functools.partial(moves, *pairs),)

    moves((edge, 0))
    edge_returns.finish(r.edge_total)

    def send_ds():
        ds_keep.start()
        ds_gather[0].start()

    node_grad(r, r.cot_rows[...], r.edge_total[...], send_ds)
    pack_third(r, r.pack.third)
    third.send_pair()
    loop(steps, lambda step: first_grad_block(r, step, features), {0: events((third, 0))})
    node_returns.start()
    moves((normed_gather, 2))
    own_spread = r.g_first[pl.ds(places, rows), :]
    spread = r.g_first[pl.ds(0, places), :]
    for side, chunk_sum in enumerate((first_a, first_b)):
        pack_first(r, side, chunk_sum.pack, r.windows.at[1], spread, own_spread, own, features, places)
        chunk_sum.send_pair()
    moves((edge, 1))
    ds_keep.wait()
    moves((ds_gather, 0))
    own_back = r.du[...] + dot_wide(own_spread, own_w, True)
    loop(steps, lambda step: second_grad_block(r, step, features), {0: events((third, 1))})
    moves((normed_gather, 3), (first_a, 0))
    pack_second(r, r.pack.second)
    second.send_pair()
    grads_keep.start()
    moves((first_b, 0))
    grads_pair.start()
    node_returns.finish(r.node_total)
    fed = own_back + dot_wide(r.node_total[...], far_w, True)
    for part in range(CORES):
        r.fed_grad[part] = fed[:, part * (width // CORES) : (part + 1) * (width // CORES)]
    fed_keep.start()
    fed_pair.start()

    blocks = r.expand.shape[1] // WIDE
    chunk = r.normed_all.shape[0]
    chunks = 2 * span // chunk
    waiting = events((second, 0), (ds_gather, 1), (edge, 2), (third, 2)), events((first_b, 1))
    until_ds = (
        (second, 1), (first_a, 1), (third, 3), (ds_gather, 2), (edge, 3), (first_b, 2), (second, 2), (first_a, 2),
        (third, 4), (edge, 4), (ds_gather, 3),
    )
    beside = {
        0: events((second, 3)),
        1: events((first_a, 3), (first_b, 3)),
        2: events((third, 5)),
        3: events((second, 4)) + (reduce_store.start,),
        4: events((first_a, 4), (edge, 5)),
        5: events((first_b, 4)),
        6: events((third, 6), (first_a, 5)),
        7: events((second, 5), (edge, 6), (first_b, 5)),
    }

    def fetch(slots, target, sem, at=0):
        return pltpu.make_async_copy(slots.at[pl.ds(at * chunk, chunk)], target, r.keep_sem.at[sem])

    if chunks == 1:
        normed_fetch = fetch(r.normed_slots, r.normed_all, 6)
        normed_fetch.start()
        normed_fetch.wait()
        loop(EARLY_WIDE, lambda step: WideBlock(r, step, half).keep(), {1: waiting[0], 4: waiting[1]})
        moves(*until_ds)
        ds_fetch = fetch(r.ds_slots, r.ds_all, 7)
        ds_fetch.start()
        ds_fetch.wait()
        loop(EARLY_WIDE, lambda step: WideBlock(r, step, half).from_kept(), beside)
        last = {at - EARLY_WIDE: actions for at, actions in beside.items() if at >= EARLY_WIDE}
        loop(blocks - EARLY_WIDE, lambda step: WideBlock(r, step + EARLY_WIDE, half).whole(True), last)
    else:
        for actions in waiting:
            for act in actions:
                act()
        moves(*until_ds)
        for at in range(chunks):
            fetches = [fetch(r.normed_slots, r.normed_all, 6, at), fetch(r.ds_slots, r.ds_all, 7, at)]
            for copy in fetches:
                copy.start()
            for copy in fetches:
                copy.wait()
            loop(blocks, lambda step: WideBlock(r, step, half).whole(at == 0))
        for actions in beside.values():
            for act in actions:
                act()
    expand_store.start()
    for group in (edges_pair, grads_pair, fed_pair):
        group.wait()
    for copy in (edges_keep, grads_keep, fed_keep, state_keep):
        copy.wait()
    moves((second, 6), (first_b, 6), (first_a, 6))
    expand_store.wait()
    reduce_store.wait()


def shape(dims, kind):
    return jax.ShapeDtypeStruct(dims, kind)


def run(vectors, arrays):
    count = lax.axis_size("res")
    rows_dev, width = arrays.nodes.shape
    slots, _, features = arrays.edges.shape
    hidden = arrays.second_in.shape[0]
    inner = arrays.expand_in.shape[1]
    rows = rows_dev // CORES
    places = rows + 2 * REACH
    total = rows * slots
    each = slots // CORES
    tall = arrays.first_in.shape[0]
    chunks = chunk_rows(count, width, hidden, features)
    side, deep = chip_dims(count)
    everyone = CORES * count * rows
    chunk = everyone if everyone <= 16 * rows_dev else 8 * rows_dev
    wide_kind = BF16 if chunk == everyone else F32
    outs = (
        shape((rows_dev, width // CORES), BF16),
        shape((each, rows_dev, features), BF16),
        shape((rows_dev, width // CORES), F32),
        shape((each, rows_dev, features), BF16),
        shape((width // CORES, inner), wide_kind),
        shape((inner // CORES, width), wide_kind),
        shape((everyone, width), BF16),
        shape((everyone, width), BF16),
    ) + tuple(shape((size, LANE), BF16) for size in chunks)
    peers = 2 * (side - 1) + deep - 1
    remote = len(chunks) * (2 * peers + 1) + 2 * (peers + 1) + 3
    scratch = dict(
        windows=((3, places, width), BF16),
        neighbours_raw=((slots, rows_dev), jnp.int32),
        picks=((slots, 1, rows_dev), F32),
        counts=((rows, LANE), F32),
        bias_wide=((inner // WIDE, WIDE), F32),
        diagonal=((rows, CHAIN * rows), F32),
        lane_slot=((8, CHAIN * rows), F32),
        first=((tall, hidden), BF16),
        second_w=((hidden, hidden), BF16),
        third=((hidden, width), BF16),
        expand=((width, inner), BF16),
        reduce=((inner, width), BF16),
        e_first_t=((features, tall), BF16),
        e_second_w=((features, features), BF16),
        e_third_w=((features, features), BF16),
        edges_raw=((slots, rows, features), BF16),
        cots_raw=((slots, rows, features), BF16),
        cot_rows=((rows, width), BF16),
        onehot=((slots, rows, LANES), BF16),
        table=((LANES + features, hidden), BF16),
        e_table=((LANES + features, features), BF16),
        kept=((3 * total, hidden), BF16),
        pooled=((rows, hidden), F32),
        summed=((rows, width), F32),
        second=((rows, width), F32),
        pre_expand=((rows, inner), F32),
        normed=((rows, width), BF16),
        edge_out=((slots, rows, features), BF16),
        edge_grad=((slots, rows, features), F32),
        ge_norm=((8, features), F32),
        ge_first=((LANES + features, features), F32),
        ge_second=((features, features), F32),
        ge_third=((features, features), F32),
        ge_own=((features, width), F32),
        ge_far=((features, width), F32),
        e_own_back=((rows, width), F32),
        edge_outgoing=((places, features), BF16),
        edge_landing=((places, features), BF16),
        edge_total=((rows, features), F32),
        ds=((rows, width), BF16),
        du=((rows, width), F32),
        dm=((rows, width), BF16),
        slot_grad=((rows, hidden), F32),
        small=((16, width), F32),
        g_second=((hidden, hidden), F32),
        g_first=((LANES + features, hidden), F32),
        g_bias=((1, hidden), F32),
        node_outgoing=((places, hidden), BF16),
        node_landing=((places, hidden), BF16),
        node_total=((rows, hidden), F32),
        fed_grad=((CORES, rows, width // CORES), F32),
        normed_all=((chunk, width), BF16),
        ds_all=((chunk, width), BF16),
        g_expand=((width // CORES, inner), wide_kind),
        g_reduce=((inner // CORES, width), wide_kind),
    )
    packed = [(CORES, size, LANE) for size in chunks] + [(size, LANE) for size in chunks] * 3
    sems = dict(load_sem=13, keep_sem=15, line_send=20, line_recv=20, step_send=remote, step_recv=remote)
    for name, size in sems.items():
        scratch[name] = pltpu.SemaphoreType.DMA((size,))
    anywhere = pl.BlockSpec(memory_space=pl.ANY)
    return pl.pallas_call(
        functools.partial(kernel, tuple(scratch), features),
        out_shape=outs,
        in_specs=[pl.BlockSpec(memory_space=pltpu.VMEM)] * len(vectors) + [anywhere] * len(arrays),
        out_specs=(anywhere,) * len(outs),
        scratch_shapes=[pltpu.VMEM(*kind) if isinstance(kind, tuple) else kind for kind in scratch.values()]
        + [pltpu.VMEM(dims, BF16) for dims in packed],
        compiler_params=pltpu.CompilerParams(
            collective_id=1, has_side_effects=True, vmem_limit_bytes=VMEM
        ),
        name="graph_layer",
    )(*vectors, *arrays)


class Moved(NamedTuple):
    grads: Any
    expand: Any
    reduce: Any
    edges: Any
    state: Any
    fed: Any


class Grads(NamedTuple):
    third_g: Any
    e_first: Any
    e_second: Any
    e_third: Any
    second_g: Any
    first_g: Any


class Biases(NamedTuple):
    b_one: Any
    b_two: Any
    b_three: Any
    gain_one: Any
    shift_one: Any
    b_expand: Any
    b_reduce: Any
    gain_two: Any
    shift_two: Any
    eb_one: Any
    eb_two: Any
    eb_three: Any
    e_gain: Any
    e_shift: Any


def finish_kernel(width, hidden, features, inner, *refs):
    refs = list(refs)
    take = lambda kind: kind(*(refs.pop(0) for _ in kind._fields))
    moved_in, packed_in = take(Moved), take(Chunks)
    moved_out, grads_out, biases = take(Moved), take(Grads), take(Biases)
    r, g, via, ready = take(Chunks), take(Grads), take(Moved), take(Moved)
    sem, move_sem = refs
    half = lax.axis_index("half")
    wide = width // LANE
    tall = (2 * width + features) // CORES
    copy = pltpu.make_async_copy
    fetches = [copy(*pair, sem.at[at]) for at, pair in enumerate(zip(moved_in, via))]
    moves = [
        copy(a if a.dtype == c.dtype else b, c, move_sem.at[at]) for at, (a, b, c) in enumerate(zip(via, ready, moved_out))
    ]
    first = len(fetches)
    loads = Chunks(*(copy(*pair, sem.at[first + at]) for at, pair in enumerate(zip(packed_in, r))))
    first += len(loads)
    stores = Grads(*(copy(*pair, sem.at[first + at]) for at, pair in enumerate(zip(g, grads_out))))
    for load in loads:
        load.start()
    for fetch in fetches:
        fetch.start()

    def move_on(at):
        fetches[at].wait()
        if via[at].dtype != ready[at].dtype:
            ready[at][...] = via[at][...].astype(ready[at].dtype)
        moves[at].start()

    loads.third.wait()
    g.third_g[...], _ = take_wide(r.third, 0, hidden // CORES, wide)
    stores.third_g.start()
    loads.edge.wait()
    e_whole, at = take_wide(r.edge, 0, features, up(tall, LANE) // LANE)
    g.e_first[...] = e_whole[:, :tall]
    rest = features - LANE
    part = features // CORES
    left_two, at = take_wide(r.edge, at, part, 1)
    left_three, at = take_wide(r.edge, at, part, 1)
    right, at = take_wide(r.edge, at, part, 1)
    g.e_second[...] = jnp.concatenate([left_two, right[:, :rest]], 1)
    g.e_third[...] = jnp.concatenate([left_three, right[:, rest:]], 1)
    for store in (stores.e_first, stores.e_second, stores.e_third):
        store.start()
    for at in range(2):
        move_on(at)
    loads.second.wait()
    g.second_g[...], _ = take_wide(r.second, 0, hidden // CORES, wide)
    stores.second_g.start()
    for at in range(2, len(fetches)):
        move_on(at)
    loads.first_a.wait()
    g.first_g[:, : hidden // 2], _ = take_wide(r.first_a, 0, tall, wide // 2)
    loads.first_b.wait()
    g.first_g[:, hidden // 2 :], at = take_wide(r.first_b, 0, tall, wide // 2)
    stores.first_g.start()
    small, _ = take_wide(r.first_b, at, 16, wide)

    def share(target, row):
        size = target.shape[0]
        target[...] = jnp.where(half == 0, row[:, :size], row[:, size : 2 * size]).reshape(size)

    b = biases
    for target, at in (
        (b.b_one, 0), (b.b_two, 1), (b.b_three, 2), (b.gain_one, 3), (b.shift_one, 4), (b.b_reduce, 9),
        (b.gain_two, 10), (b.shift_two, 11),
    ):
        share(target, small[at : at + 1])
    share(b.b_expand, jnp.concatenate([small[5 + p : 6 + p] for p in range(inner // width)], 1))
    share(b.eb_one, small[12:13, :LANES])
    share(b.eb_two, small[12:13, LANES:])
    share(b.eb_three, small[13:14, :LANES])
    share(b.e_gain, small[13:14, LANES:])
    share(b.e_shift, small[14:15, :LANES])
    for store in moves + list(stores):
        store.wait()


def finish(moved, sums, width, hidden, features, inner):
    tall = (2 * width + features) // CORES
    part = features // CORES
    grads = Grads(
        third_g=(hidden // CORES, width),
        e_first=(features, tall),
        e_second=(part, features),
        e_third=(part, features),
        second_g=(hidden // CORES, hidden),
        first_g=(tall, hidden),
    )
    sizes = Biases(hidden, hidden, width, width, width, inner, width, width, width, *[features] * 5)
    anywhere, vmem = pl.BlockSpec(memory_space=pl.ANY), pl.BlockSpec(memory_space=pltpu.VMEM)
    kinds = Moved(F32, F32, F32, BF16, BF16, F32)
    outs = [shape(a.shape, kind) for a, kind in zip(moved, kinds)]
    outs += [shape(dims, F32) for dims in grads]
    outs += [shape((size // CORES,), F32) for size in sizes]
    got = pl.pallas_call(
        functools.partial(finish_kernel, width, hidden, features, inner),
        out_shape=outs,
        in_specs=[anywhere] * (len(moved) + len(sums)),
        out_specs=[anywhere] * (len(moved) + len(grads)) + [vmem] * len(sizes),
        scratch_shapes=[pltpu.VMEM(a.shape, BF16) for a in sums]
        + [pltpu.VMEM(dims, F32) for dims in grads]
        + [pltpu.VMEM(a.shape, a.dtype) for a in moved]
        + [pltpu.VMEM(a.shape if a.dtype != kind else (16, LANE), kind) for a, kind in zip(moved, kinds)]
        + [pltpu.SemaphoreType.DMA((len(moved) + len(sums) + len(grads),)), pltpu.SemaphoreType.DMA((len(moved),))],
        compiler_params=pltpu.CompilerParams(vmem_limit_bytes=VMEM),
        name="finish",
    )(*moved, *sums)
    first = len(moved) + len(grads)
    return Moved(*got[: len(moved)]), Grads(*got[len(moved) : first]), Biases(*got[first:])


def body(
    nodes, edges, neighbours, counts,
    message_first, message_first_bias, message_second, message_second_bias, message_third, message_third_bias,
    node_norm_gain, node_norm_shift, expand_weight, expand_bias, reduce_weight, reduce_bias,
    output_norm_gain, output_norm_shift,
    edge_first, edge_first_bias, edge_second, edge_second_bias, edge_third, edge_third_bias,
    edge_norm_gain, edge_norm_shift, cot_nodes, cot_edges,
):
    width, features = nodes.shape[1], edges.shape[2]
    hidden, inner = message_second.shape[0], expand_weight.shape[1]

    by_slots = lambda values: jnp.transpose(values, (1, 0, 2))
    vectors = Vectors(
        message_first_bias, message_second_bias, message_third_bias, node_norm_gain, node_norm_shift, reduce_bias,
        output_norm_gain, output_norm_shift, expand_bias, edge_first_bias, edge_second_bias, edge_third_bias,
        edge_norm_gain, edge_norm_shift, counts,
    )
    arrays = Arrays(
        nodes, by_slots(edges), neighbours.T, message_first, message_second, message_third, expand_weight,
        reduce_weight, edge_first.T, edge_second, edge_third, cot_nodes, by_slots(cot_edges),
    )
    state, out, fed_grad, edge_grad, g_expand, g_reduce, _, _, *sums = run(vectors, arrays)
    moved = Moved(edge_grad, g_expand, g_reduce, out, state, fed_grad)
    m, g, b = finish(moved, sums, width, hidden, features, inner)
    return (
        m.state, by_slots(m.edges), m.fed, by_slots(m.grads),
        g.first_g, b.b_one, g.second_g, b.b_two, g.third_g, b.b_three, b.gain_one, b.shift_one,
        m.expand, b.b_expand, m.reduce, b.b_reduce, b.gain_two, b.shift_two,
        g.e_first.T, b.eb_one, g.e_second, b.eb_two, g.e_third, b.eb_three, b.e_gain, b.e_shift,
    )


def solution(mesh):
    rows, slots = P("res", None), P("res", None, None)
    copied = P()
    down, vec = P("half", None), P("half")
    return jax.shard_map(
        body,
        mesh=mesh,
        in_specs=(rows, slots, rows, P("res")) + (copied,) * 22 + (rows, slots),
        out_specs=(
            P("res", "half"),
            P("res", "half", None),
            P("res", "half"),
            P("res", "half", None),
            down, vec, down, vec, down, vec, vec, vec, down, vec, down, vec, vec, vec,
            down, vec, down, vec, down, vec, vec, vec,
        ),
        check_vma=False,
    )
```
